256 devices in a mesh: basin: 4 (over x), tile: 64 (over y, z, core).
Axes of the slice: x: 4, y: 4, z: 8, core: 2. Of those that a mesh axis runs over, the one named last changes fastest.
Arguments:
- depth_start: float32 [4, 4096, 512], P('basin', 'tile'), may hold values from -6 to 6
- roughness: float32 [4, 4096, 512], P('basin', 'tile'), may hold values from 0.025 to 0.25
- depth_seed: float32 [4, 4096, 512], P('basin', 'tile'), may hold values from -6 to 6
- zone_label: int32 [4, 4096, 512], P('basin', 'tile'), may hold values from 0 to 32511, as said below
- owner_slot: int32 [32512], replicated, may hold values from 0 to 32511, each once
- retention: float32 [128, 8192], P('basin', 'tile'), may hold values from 0 to 1
- forcing: float32 [128, 8192], P('basin', 'tile'), may hold values from -0.6 to 0.6
- levee_cell: int32 [128, 8192], P('basin', 'tile'), may hold values from 0 to 32767
Outputs:
- zone_gradient: float32 [32512], P(('basin', 'tile'))
- zone_curvature: float32 [32512], P(('basin', 'tile'))
- reach_adjoint: float32 [128, 8192], P('basin', 'tile')
The draws below stay inside these ranges and needn't reach their ends.
Inputs may be any that keep to these rules, and one draw needn't show every extreme that they name: `zone_label`: seven cells in eight of the rows b, (t * 64) to (t * 64 + 63) take zones of the band (b * 64 + t) * 127 onward, 127 wide, lower ones more often; the others any zone. `owner_slot`: each zone once. `levee_cell`: Row-major index of a cell within rows (j // 128) * 64 to (j // 128) * 64 + 63 of basin i // 32.
All inputs are finite; a program needn't handle non-finite values.
Results may differ from the reference program's by a relative error of at most 0.0003.
Values sent between devices are 32-bit elements; how exact they have to be, the bound alone decides.
No kernel may reach another device: no remote copies, remote signals or barrier semaphores. Data moves between devices by JAX's collectives and lax.ppermute only.
A program may use at most 64 MiB of HBM per device.

```python
import math
import jax
import jax.numpy as jnp
from jax import lax

R = 64
C = 512
L_DEV = 32
CH_DEV = 128
ZONES = 32512
STEPS = 4
BASINS = 4
TILES = 64
ROWS = 4096
CHANNEL_SEGMENTS = 128
CHAINS = 8192
ZONE_SPAN = 127


def draw_zone_label(key, part):
    key_first, key_second, key_stray, key_pick = jax.random.split(jax.random.fold_in(key, 17), 4)
    shape = (BASINS, ROWS, C)
    basin_index = lax_free_iota(shape, 0)
    row_index = lax_free_iota(shape, 1)
    block_index = basin_index * TILES + row_index // R
    offset = jnp.minimum(jax.random.randint(key_first, shape, 0, ZONE_SPAN), jax.random.randint(key_second, shape, 0, ZONE_SPAN))
    home_zone = block_index * ZONE_SPAN + offset
    stray_zone = jax.random.randint(key_stray, shape, 0, ZONES)
    picked = jax.random.randint(key_pick, shape, 0, 8) == 0
    return jnp.where(picked, stray_zone, home_zone).astype(jnp.int32)


def lax_free_iota(shape, axis_number):
    sizes = [1] * len(shape)
    sizes[axis_number] = shape[axis_number]
    return jnp.broadcast_to(jnp.arange(shape[axis_number], dtype=jnp.int32).reshape(sizes), shape)


def draw_retention(key, part):
    key_chain_rates, key_perturbation, key_surge, key_multiplier = jax.random.split(jax.random.fold_in(key, 29), 4)
    lowest = 0.3 / CHANNEL_SEGMENTS
    highest = 1.0 / 30.0
    reach_chain_rates = jnp.exp(jax.random.uniform(key_chain_rates, (1, CHAINS), jnp.float32, math.log(lowest), math.log(highest)))
    perturbation = jax.random.uniform(key_perturbation, (CHANNEL_SEGMENTS, CHAINS), jnp.float32, 0.5, 2.0)
    surge_rows = jax.random.uniform(key_surge, (CHANNEL_SEGMENTS, 1), jnp.float32) < 3.0 / CHANNEL_SEGMENTS
    multiplier = jax.random.uniform(key_multiplier, (CHANNEL_SEGMENTS, 1), jnp.float32, 0.5, 0.8)
    kept_fraction = jnp.exp(-reach_chain_rates * perturbation) * jnp.where(surge_rows, multiplier, 1.0)
    return kept_fraction.astype(jnp.float32)


def place_ends(array, rng, smallest, largest):
    longest = array.shape.index(max(array.shape))
    spots = []
    for shift in (0, 1):
        where = [jax.random.randint(jax.random.fold_in(rng, axis), (), 0, length) for axis, length in enumerate(array.shape)]
        where[longest] = (where[longest] + shift) % array.shape[longest]
        spots.append(tuple(where))
    return array.at[spots[0]].set(smallest).at[spots[1]].set(largest)


def block_scale(rng, extent, pieces, least, largest):
    level = 1.0
    for dim, blocks in pieces:
        steps = jax.random.uniform(jax.random.fold_in(jax.random.fold_in(rng, 6), dim), (blocks,), jnp.float32, least / len(pieces), largest / len(pieces))
        level = level * jnp.repeat(jnp.exp(steps), extent[dim] // blocks).reshape((-1,) + (1,) * (len(extent) - 1 - dim))
    return level


def bell_draw(rng, shape, width, most, pieces=(), held_as=jnp.bfloat16):
    entries = width * jax.random.normal(rng, shape, jnp.float32)
    if pieces:
        entries = entries * block_scale(rng, shape, pieces, -0.22, 0.18)
    return jnp.clip(entries, -most, most).astype(held_as)


def setup_inputs(seed: int = 0) -> dict:
    arg_keys = jax.random.split(jax.random.key(seed), 9)
    return {
        "depth_start": bell_draw(arg_keys[0], (BASINS, ROWS, C), 1.0, 6.0, ((0, 4), (1, 64)), jnp.float32),
        "roughness": jnp.clip(jnp.exp(math.log(0.25) - 2.3025851 * jax.random.uniform(arg_keys[1], (BASINS, ROWS, C), jnp.float32) ** block_scale(arg_keys[1], (BASINS, ROWS, C), ((0, 4), (1, 64)), -0.2, 0.2)), 0.025, 0.25),
        "depth_seed": bell_draw(arg_keys[2], (BASINS, ROWS, C), 1.0, 6.0, ((0, 4), (1, 64)), jnp.float32),
        "zone_label": draw_zone_label(jax.random.fold_in(arg_keys[8], 71), 0),
        "owner_slot": jax.random.permutation(arg_keys[4], ZONES).astype(jnp.int32),
        "retention": draw_retention(jax.random.fold_in(arg_keys[8], 71), 0),
        "forcing": bell_draw(arg_keys[6], (CHANNEL_SEGMENTS, CHAINS), 0.1, 0.6, ((0, 4), (1, 64)), jnp.float32),
        "levee_cell": place_ends(jax.random.randint(arg_keys[7], (CHANNEL_SEGMENTS, CHAINS), 0, R * C), jax.random.fold_in(arg_keys[7], 1), 0, (R * C) - 1).astype(jnp.int32),
    }


courant = 0.24
rough_ref = 0.025
levee_gain = 0.1


def neighbours(padded):
    return [padded[2:, 1:-1], padded[:-2, 1:-1], padded[1:-1, 2:], padded[1:-1, :-2]]


def face_weights(conduct_pad):
    centre = conduct_pad[1:-1, 1:-1]
    return [jnp.where((centre > 0) & (opposite > 0), 0.5 * (centre + opposite), 0.0) for opposite in neighbours(conduct_pad)]


def spread(field_pad, face_list):
    centre = field_pad[1:-1, 1:-1]
    accumulated = jnp.zeros(centre.shape, jnp.float32)
    for weight, opposite in zip(face_list, neighbours(field_pad)):
        accumulated = accumulated + weight * (opposite - centre)
    return accumulated


def product_terms(depth_pad, adjoint_pad, face_list):
    depth_centre = depth_pad[1:-1, 1:-1]
    adjoint_centre = adjoint_pad[1:-1, 1:-1]
    accumulated = jnp.zeros(depth_centre.shape, jnp.float32)
    for weight, depth_near, adjoint_near in zip(face_list, neighbours(depth_pad), neighbours(adjoint_pad)):
        accumulated = accumulated + jnp.where(weight > 0, (depth_near - depth_centre) * (adjoint_near - adjoint_centre), 0.0)
    return accumulated


def basin_pass(depth_zero, rough_cells, seed_cells):
    conductance = rough_ref / rough_cells
    face_list = face_weights(jnp.pad(conductance, 1))
    states = [depth_zero]
    for section_index in range(STEPS - 1):
        states.append(states[-1] + courant * spread(jnp.pad(states[-1], 1), face_list))
    adjoint = seed_cells
    accumulated = jnp.zeros(depth_zero.shape, jnp.float32)
    for section_index in reversed(range(STEPS)):
        adjoint_pad = jnp.pad(adjoint, 1)
        accumulated = accumulated + product_terms(jnp.pad(states[section_index], 1), adjoint_pad, face_list)
        adjoint = adjoint + courant * spread(adjoint_pad, face_list)
    return adjoint, 0.5 * courant * conductance * accumulated


def reference(depth_start, roughness, depth_seed, zone_label, owner_slot, retention, forcing, levee_cell):
    def per_basin(sums, inputs):
        depth_zero, rough_cells, seed_cells, label_cells = inputs
        adjoint, cell_gradient = basin_pass(depth_zero, rough_cells, seed_cells)
        slot_ids = owner_slot[label_cells].reshape(-1)
        flat_grad = cell_gradient.reshape(-1)
        grad_sum = sums[0] + jax.ops.segment_sum(flat_grad, slot_ids, num_segments=ZONES)
        curv_sum = sums[1] + jax.ops.segment_sum(flat_grad * flat_grad, slot_ids, num_segments=ZONES)
        return (grad_sum, curv_sum), adjoint

    start_sums = (jnp.zeros((ZONES,), jnp.float32), jnp.zeros((ZONES,), jnp.float32))
    (zone_gradient, zone_curvature), adjoints = lax.scan(per_basin, start_sums, (depth_start, roughness, depth_seed, zone_label))
    blocks = adjoints.reshape(BASINS, TILES, R * C)
    basin_index = (jnp.arange(CHANNEL_SEGMENTS, dtype=jnp.int32) // L_DEV)[:, None]
    tile_index = (jnp.arange(CHAINS, dtype=jnp.int32) // CH_DEV)[None, :]
    levee_value = blocks[basin_index, tile_index, levee_cell]
    drive_term = forcing + levee_gain * levee_value

    def upstream(downstream, reach_row):
        keep_rate, inflow = reach_row
        updated = keep_rate * downstream + inflow
        return updated, updated

    last_value, reach_adjoint = lax.scan(upstream, jnp.zeros((CHAINS,), jnp.float32), (retention, drive_term), reverse=True)
    return zone_gradient, zone_curvature, reach_adjoint
```

```python
import functools

import jax
import jax.numpy as jnp
from jax import lax
from jax.experimental import pallas as pl
from jax.experimental.pallas import tpu as pltpu
from jax.sharding import PartitionSpec as P

STEPS = 4
HALO = STEPS
SPAN = 127
LANES = 128

courant = 0.24
rough_ref = 0.025
levee_gain = 0.1

VMEM = pl.BlockSpec(memory_space=pltpu.VMEM)
ROOMY = pltpu.CompilerParams(vmem_limit_bytes=48 * 2**20)


def iota_bf16(shape, offset=0):
    ids = lax.broadcasted_iota(jnp.int32, shape, len(shape) - 2)
    if len(shape) == 3:
        ids = ids + shape[1] * lax.broadcasted_iota(jnp.int32, shape, 0)
    return (ids + offset).astype(jnp.float32).astype(jnp.bfloat16)


def spread_rows(row):
    return jnp.broadcast_to(row, (16, row.shape[1])).astype(jnp.bfloat16)


def one_hot(spread, count, weights=None):
    width = spread.shape[1]
    ids = iota_bf16((count // 16, 16, width))
    hit = spread[None] == ids
    zero = jnp.zeros((), jnp.bfloat16)
    if weights is None:
        return jnp.where(hit, jnp.ones((), jnp.bfloat16), zero).reshape(count, width)
    return [jnp.where(hit, w[None], zero).reshape(count, width) for w in weights]


def slot_kernel(owner_ref, label_ref, device_ref, lane_ref, table_ref, turned_ref):
    table_ref[...] = jnp.zeros(table_ref.shape, jnp.float32)
    table_ref[0 : owner_ref.shape[0], :] = owner_ref[...].astype(jnp.float32)
    slots = jnp.transpose(table_ref[...])
    owners = jnp.floor((slots + 0.5) * (1.0 / SPAN))
    turned_ref[0:LANES, :] = owners.astype(jnp.bfloat16)
    turned_ref[LANES : 2 * LANES, :] = (slots - owners * SPAN).astype(jnp.bfloat16)

    def one_row(row, carry):
        label = label_ref[pl.ds(row, 1), :]
        width = label.shape[1]
        group = one_hot(spread_rows((label // LANES).astype(jnp.float32)), 256)
        found = jnp.dot(turned_ref[...], group, preferred_element_type=jnp.float32)
        hit = (label % LANES) == lax.broadcasted_iota(jnp.int32, (LANES, width), 0)
        device_ref[pl.ds(row, 1), :] = jnp.sum(
            jnp.where(hit, found[:LANES], 0.0), axis=0, keepdims=True
        )
        lane_ref[pl.ds(row, 1), :] = jnp.sum(
            jnp.where(hit, found[LANES:], 0.0), axis=0, keepdims=True
        )
        return carry

    lax.fori_loop(0, label_ref.shape[0], one_row, 0, unroll=4)


def slots_of(owner_slot, label):
    shape = jax.ShapeDtypeStruct(label.shape, jnp.float32)
    return pl.pallas_call(
        slot_kernel,
        out_shape=(shape, shape),
        in_specs=[VMEM, VMEM],
        out_specs=(VMEM, VMEM),
        scratch_shapes=[
            pltpu.VMEM((256, LANES), jnp.float32),
            pltpu.VMEM((256, 256), jnp.bfloat16),
        ],
        compiler_params=ROOMY,
        cost_estimate=pl.CostEstimate(
            flops=2 * 256 * 256 * label.size, bytes_accessed=16 * label.size, transcendentals=0
        ),
        name="slot_lookup",
    )(owner_slot.reshape(-1, LANES), label)


def below(x):
    return pltpu.roll(x, x.shape[0] - 1, 0)


def above(x):
    return pltpu.roll(x, 1, 0)


def rightward(x):
    return pltpu.roll(x, x.shape[1] - 1, 1)


def leftward(x):
    return pltpu.roll(x, 1, 1)


def window_kernel(depth_ref, rough_ref_, seed_ref, low_ref, high_ref, grad_ref, adjoint_ref):
    def extended(part, ref):
        start = part * HALO
        return jnp.concatenate(
            [low_ref[start : start + HALO, :], ref[...], high_ref[start : start + HALO, :]], axis=0
        )

    depth = extended(0, depth_ref)
    rough = extended(1, rough_ref_)
    adjoint = extended(2, seed_ref)
    rows, columns = depth.shape
    conduct = jnp.where(rough > 0, rough_ref / jnp.where(rough > 0, rough, 1.0), 0.0)
    not_last = lax.broadcasted_iota(jnp.int32, (rows, columns), 1) < columns - 1
    under = below(conduct)
    beside = rightward(conduct)
    down_face = (conduct > 0) & (under > 0)
    side_face = (conduct > 0) & (beside > 0) & not_last
    down_weight = jnp.where(down_face, (0.5 * courant) * (conduct + under), 0.0)
    side_weight = jnp.where(side_face, (0.5 * courant) * (conduct + beside), 0.0)

    def steps(field):
        return below(field) - field, rightward(field) - field

    def advanced(field, down_step, side_step):
        down_flux = down_weight * down_step
        side_flux = side_weight * side_step
        return field + ((down_flux - above(down_flux)) + (side_flux - leftward(side_flux)))

    depth_steps = []
    for section in range(STEPS):
        depth_steps.append(steps(depth))
        if section < STEPS - 1:
            depth = advanced(depth, *depth_steps[-1])
    down_total = jnp.zeros((rows, columns), jnp.float32)
    side_total = jnp.zeros((rows, columns), jnp.float32)
    for section in reversed(range(STEPS)):
        down_step, side_step = steps(adjoint)
        down_total = down_total + depth_steps[section][0] * down_step
        side_total = side_total + depth_steps[section][1] * side_step
        adjoint = advanced(adjoint, down_step, side_step)
    down_total = jnp.where(down_face, down_total, 0.0)
    side_total = jnp.where(side_face, side_total, 0.0)
    total = (down_total + above(down_total)) + (side_total + leftward(side_total))
    own = slice(HALO, rows - HALO)
    grad_ref[...] = ((0.5 * courant) * conduct * total)[own]
    adjoint_ref[...] = adjoint[own]


def window(depth, rough, seed, low, high):
    shape = jax.ShapeDtypeStruct(depth.shape, jnp.float32)
    return pl.pallas_call(
        window_kernel,
        out_shape=(shape, shape),
        in_specs=[VMEM] * 5,
        out_specs=(VMEM, VMEM),
        compiler_params=ROOMY,
        name="adjoint_window",
    )(depth, rough, seed, low, high)


def halves(x):
    upper = x.astype(jnp.bfloat16).astype(jnp.float32)
    return upper, x - upper


ZONE_ROWS = 8


def zone_kernel(grad_ref, device_ref, lane_ref, out_ref):
    out_ref[...] = jnp.zeros(out_ref.shape, jnp.float32)

    def some_rows(index, carry):
        left = []
        right = []
        for offset in range(ZONE_ROWS):
            row = pl.ds(index * ZONE_ROWS + offset, 1)
            grad = grad_ref[row, :]
            left.append(one_hot(spread_rows(device_ref[row, :]), 256))
            weights = [spread_rows(part) for part in halves(grad) + halves(grad * grad)]
            right.append(
                jnp.concatenate(one_hot(spread_rows(lane_ref[row, :]), LANES, weights), axis=0)
            )
        both = lax.dot_general(
            jnp.concatenate(left, axis=1),
            jnp.concatenate(right, axis=1),
            (((1,), (1,)), ((), ())),
            preferred_element_type=jnp.float32,
        )
        out_ref[...] += jnp.concatenate(
            [
                both[:, 0:LANES] + both[:, LANES : 2 * LANES],
                both[:, 2 * LANES : 3 * LANES] + both[:, 3 * LANES :],
            ],
            axis=1,
        )
        return carry

    lax.fori_loop(0, grad_ref.shape[0] // ZONE_ROWS, some_rows, 0)


def zone_partials(grad, device, lane):
    return pl.pallas_call(
        zone_kernel,
        out_shape=jax.ShapeDtypeStruct((256, 2 * LANES), jnp.float32),
        in_specs=[VMEM] * 3,
        out_specs=VMEM,
        compiler_params=ROOMY,
        cost_estimate=pl.CostEstimate(
            flops=2 * 256 * 512 * grad.size, bytes_accessed=12 * grad.size, transcendentals=0
        ),
        name="zone_partials",
    )(grad, device, lane)


def reach_kernel(adjoint_ref, cell_ref, keep_ref, forcing_ref, rate_ref, push_ref, edge_ref):
    rows, columns = adjoint_ref.shape
    upper, lower = halves(adjoint_ref[...])
    table = jnp.concatenate([upper, lower], axis=0).astype(jnp.bfloat16)
    reaches = cell_ref.shape[0]
    width = cell_ref.shape[1]
    values = []
    for reach in range(0, reaches, 4):
        cells = jnp.concatenate([cell_ref[reach + i : reach + i + 1, :] for i in range(4)], axis=1)
        column = (cells % columns).astype(jnp.float32)
        hot = jnp.concatenate(
            [one_hot(spread_rows(column - part * 256.0), 256) for part in range(columns // 256)],
            axis=0,
        )
        picked = jnp.dot(table, hot, preferred_element_type=jnp.float32)
        picked = picked[:rows] + picked[rows:]
        row_hit = (cells // columns) == lax.broadcasted_iota(jnp.int32, (rows, 4 * width), 0)
        found = jnp.sum(jnp.where(row_hit, picked, 0.0), axis=0, keepdims=True)
        values += [found[:, i * width : (i + 1) * width] for i in range(4)]
    rate = jnp.ones((1, width), jnp.float32)
    push = jnp.zeros((1, width), jnp.float32)
    for reach in reversed(range(reaches)):
        keep = keep_ref[reach : reach + 1, :]
        push = keep * push + (forcing_ref[reach : reach + 1, :] + levee_gain * values[reach])
        rate = keep * rate
        rate_ref[reach : reach + 1, :] = rate
        push_ref[reach : reach + 1, :] = push
    edge_ref[0:1, :] = rate
    edge_ref[1:2, :] = push


def reach_maps(adjoint, cells, keep, forcing):
    shape = jax.ShapeDtypeStruct(cells.shape, jnp.float32)
    return pl.pallas_call(
        reach_kernel,
        out_shape=(shape, shape, jax.ShapeDtypeStruct((2, cells.shape[1]), jnp.float32)),
        in_specs=[VMEM] * 4,
        out_specs=(VMEM, VMEM, VMEM),
        compiler_params=ROOMY,
        name="reach_maps",
    )(adjoint, cells, keep, forcing)


def moved(value, axis, steps):
    count = lax.axis_size(axis)
    pairs = [(i, i + steps) for i in range(count) if 0 <= i + steps < count]
    return lax.ppermute(value, axis, pairs)


def per_device(
    depth_start, roughness, depth_seed, zone_label, owner_slot, retention, forcing, levee_cell
):
    depth, rough, seed, label = depth_start[0], roughness[0], depth_seed[0], zone_label[0]
    rows = depth.shape[0]
    low = moved(jnp.concatenate([x[rows - HALO :] for x in (depth, rough, seed)]), "tile", 1)
    high = moved(jnp.concatenate([x[:HALO] for x in (depth, rough, seed)]), "tile", -1)
    device, lane = slots_of(owner_slot, label)
    grad, adjoint = window(depth, rough, seed, low, high)
    partials = zone_partials(grad, device, lane)
    arrived = lax.all_to_all(partials, ("basin", "tile"), 0, 0, tiled=True)
    rate, push, edge = reach_maps(adjoint, levee_cell, retention, forcing)
    incoming = jnp.zeros((edge.shape[1],), jnp.float32)
    edges = [moved(edge, "basin", -hop) for hop in range(1, lax.axis_size("basin"))]
    for from_below in reversed(edges):
        incoming = from_below[0] * incoming + from_below[1]
    reach_adjoint = rate * incoming[None, :] + push
    sums = jnp.sum(arrived, axis=0)
    return (sums[:SPAN], sums[LANES : LANES + SPAN], reach_adjoint)


def solution(mesh):
    in_specs = (
        P("basin", "tile", None),
        P("basin", "tile", None),
        P("basin", "tile", None),
        P("basin", "tile", None),
        P(),
        P("basin", "tile"),
        P("basin", "tile"),
        P("basin", "tile"),
    )
    out_specs = (P(("basin", "tile")), P(("basin", "tile")), P("basin", "tile"))
    return jax.shard_map(
        per_device, mesh=mesh, in_specs=in_specs, out_specs=out_specs, check_vma=False
    )
```

```python
import functools

import jax
import jax.numpy as jnp
from jax import lax
from jax.experimental import pallas as pl
from jax.experimental.pallas import tpu as pltpu
from jax.sharding import PartitionSpec as P

STEPS = 4
HALO = STEPS
SPAN = 127
LANES = 128

courant = 0.24
rough_ref = 0.025
levee_gain = 0.1

VMEM = pl.BlockSpec(memory_space=pltpu.VMEM)
ROOMY = pltpu.CompilerParams(vmem_limit_bytes=48 * 2**20)


def iota_bf16(shape, offset=0):
    ids = lax.broadcasted_iota(jnp.int32, shape, len(shape) - 2)
    if len(shape) == 3:
        ids = ids + shape[1] * lax.broadcasted_iota(jnp.int32, shape, 0)
    return (ids + offset).astype(jnp.float32).astype(jnp.bfloat16)


def spread_rows(row):
    return jnp.broadcast_to(row, (16, row.shape[1])).astype(jnp.bfloat16)


def one_hot(spread, count, weights=None):
    width = spread.shape[1]
    ids = iota_bf16((count // 16, 16, width))
    hit = spread[None] == ids
    zero = jnp.zeros((), jnp.bfloat16)
    if weights is None:
        return jnp.where(hit, jnp.ones((), jnp.bfloat16), zero).reshape(count, width)
    return [jnp.where(hit, w[None], zero).reshape(count, width) for w in weights]


def stacked(x):
    return jnp.concatenate(
        [x[:, start : start + LANES] for start in range(0, x.shape[1], LANES)], axis=0
    )


def from_below(x, distance):
    return pltpu.roll(x, x.shape[0] - distance, 0)


def front_kernel(depth_ref, rough_ref_, seed_ref, low_ref, high_ref):
    for part, ref in enumerate((depth_ref, rough_ref_, seed_ref)):
        rows = slice(part * HALO, (part + 1) * HALO)
        low_ref[rows, :] = ref[ref.shape[0] - HALO :, :]
        high_ref[rows, :] = ref[0:HALO, :]


def edges_to_send(depth, rough, seed):
    shape = jax.ShapeDtypeStruct((3 * HALO, depth.shape[1]), jnp.float32)
    return pl.pallas_call(
        front_kernel,
        out_shape=(shape, shape),
        in_specs=[VMEM] * 3,
        out_specs=(VMEM, VMEM),
        compiler_params=ROOMY,
        name="edge_rows",
    )(depth, rough, seed)


ABSENT = 2**15 - 1
CHUNK = 16


def slot_kernel(
    place_ref,
    owner_ref,
    label_ref,
    moves_ref,
    device_ref,
    lane_ref,
    home_ref,
    chunks_ref,
    table_ref,
    turned_ref,
    packed_ref,
):
    first_zone = place_ref[0]
    first_device = place_ref[1].astype(jnp.float32)
    table_ref[...] = jnp.full(table_ref.shape, 256.0 * SPAN, jnp.float32)
    table_ref[0 : owner_ref.shape[0], :] = owner_ref[...].astype(jnp.float32)

    def placed(slots):
        owners = jnp.floor((slots + 0.5) * (1.0 / SPAN))
        lanes = slots - owners * SPAN
        turned = owners - first_device
        turned = jnp.where(turned < 0, turned + 256.0, turned)
        return jnp.where(owners < 256.0, turned, 256.0), lanes

    owners, lanes = placed(jnp.transpose(table_ref[...]))
    turned_ref[0:LANES, :] = owners.astype(jnp.bfloat16)
    turned_ref[LANES : 2 * LANES, :] = lanes.astype(jnp.bfloat16)

    home_row = first_zone // LANES
    shift = first_zone % LANES
    back = jnp.where(shift == 0, 0, LANES - shift)
    pair = table_ref[pl.ds(home_row, 1), :], table_ref[pl.ds(home_row + 1, 1), :]
    pair = [pltpu.roll(jnp.broadcast_to(row, (8, LANES)), back, 1) for row in pair]
    spot = lax.broadcasted_iota(jnp.int32, (8, LANES), 1)
    home = jnp.where(spot + shift < LANES, pair[0], pair[1])
    home_device, home_lane = placed(jnp.where(spot < SPAN, home, 256.0 * SPAN))
    top = lax.broadcasted_iota(jnp.int32, (8, LANES), 0) == 0
    home_ref[...] = jnp.where(top, home_device, home_lane)

    label = stacked(label_ref[...])
    count = label.shape[0]
    offset = label - first_zone
    at_home = (offset >= 0) & (offset < SPAN)
    at_home_count = jnp.where(at_home, 1.0, 0.0)
    row_ids = lax.broadcasted_iota(jnp.int32, (count, count), 0)
    column_ids = lax.broadcasted_iota(jnp.int32, (count, count), 1)
    earlier = jnp.where(column_ids < row_ids, 1.0, 0.0).astype(jnp.bfloat16)
    gaps = jnp.dot(
        earlier, at_home_count.astype(jnp.bfloat16), preferred_element_type=jnp.float32
    ).astype(jnp.int32)
    packed = jnp.where(at_home, ABSENT, gaps * (ABSENT + 1) + label)
    moves = jnp.zeros(packed.shape, jnp.int32)
    bit = 0
    while 2**bit < count:
        marker = (ABSENT + 1) * 2**bit
        near = from_below(packed, 2**bit)
        taken = (near & marker) != 0
        left = (packed & marker) != 0
        packed = jnp.where(taken, near, jnp.where(left, ABSENT, packed))
        moves = jnp.where(taken, moves + 2**bit, moves)
        bit += 1
    moves_ref[...] = moves
    packed_ref[...] = packed & ABSENT
    most = count - jnp.min(jnp.sum(at_home_count, axis=0, keepdims=True)).astype(jnp.int32)
    chunks = (most + CHUNK - 1) // CHUNK
    chunks_ref[0] = chunks

    def one_chunk(index, carry):
        for quarter in range(CHUNK // 4):
            start = index * CHUNK + quarter * 4
            group_label = jnp.concatenate(
                [packed_ref[pl.ds(start + i, 1), :] for i in range(4)], axis=1
            )
            width = group_label.shape[1]
            group = one_hot(spread_rows((group_label >> 7).astype(jnp.float32)), 256)
            found = jnp.dot(turned_ref[...], group, preferred_element_type=jnp.float32)
            hit = (group_label & 127) == lax.broadcasted_iota(jnp.int32, (LANES, width), 0)
            for half, ref in enumerate((device_ref, lane_ref)):
                part = found[half * LANES : (half + 1) * LANES]
                part = jnp.sum(jnp.where(hit, part, 0.0), axis=0, keepdims=True)
                for i in range(4):
                    ref[pl.ds(start + i, 1), :] = part[:, i * LANES : (i + 1) * LANES]
        return carry

    lax.fori_loop(0, chunks, one_chunk, 0)


SMEM = pl.BlockSpec(memory_space=pltpu.SMEM)


def slots_of(place, owner_slot, label):
    count = label.size // LANES
    stack = jax.ShapeDtypeStruct((count, LANES), jnp.float32)
    return pl.pallas_call(
        slot_kernel,
        out_shape=(
            jax.ShapeDtypeStruct((count, LANES), jnp.int32),
            stack,
            stack,
            jax.ShapeDtypeStruct((8, LANES), jnp.float32),
            jax.ShapeDtypeStruct((1,), jnp.int32),
        ),
        in_specs=[SMEM, VMEM, VMEM],
        out_specs=(VMEM, VMEM, VMEM, VMEM, SMEM),
        scratch_shapes=[
            pltpu.VMEM((256, LANES), jnp.float32),
            pltpu.VMEM((256, 256), jnp.bfloat16),
            pltpu.VMEM((count, LANES), jnp.int32),
        ],
        compiler_params=ROOMY,
        cost_estimate=pl.CostEstimate(
            flops=2 * 256 * 256 * label.size // 4, bytes_accessed=16 * label.size, transcendentals=0
        ),
        name="slot_lookup",
    )(place, owner_slot.reshape(-1, LANES), label)


def below(x):
    return pltpu.roll(x, x.shape[0] - 1, 0)


def above(x):
    return pltpu.roll(x, 1, 0)


def rightward(x):
    return pltpu.roll(x, x.shape[1] - 1, 1)


def leftward(x):
    return pltpu.roll(x, 1, 1)


def window_kernel(depth_ref, rough_ref_, seed_ref, low_ref, high_ref, grad_ref, adjoint_ref):
    def extended(part, ref):
        start = part * HALO
        return jnp.concatenate(
            [low_ref[start : start + HALO, :], ref[...], high_ref[start : start + HALO, :]], axis=0
        )

    depth = extended(0, depth_ref)
    rough = extended(1, rough_ref_)
    adjoint = extended(2, seed_ref)
    rows, columns = depth.shape
    conduct = jnp.where(rough > 0, rough_ref / jnp.where(rough > 0, rough, 1.0), 0.0)
    not_last = lax.broadcasted_iota(jnp.int32, (rows, columns), 1) < columns - 1
    under = below(conduct)
    beside = rightward(conduct)
    down_face = (conduct > 0) & (under > 0)
    side_face = (conduct > 0) & (beside > 0) & not_last
    down_weight = jnp.where(down_face, (0.5 * courant) * (conduct + under), 0.0)
    side_weight = jnp.where(side_face, (0.5 * courant) * (conduct + beside), 0.0)

    def steps(field):
        return below(field) - field, rightward(field) - field

    def advanced(field, down_step, side_step):
        down_flux = down_weight * down_step
        side_flux = side_weight * side_step
        return field + ((down_flux - above(down_flux)) + (side_flux - leftward(side_flux)))

    depth_steps = []
    for section in range(STEPS):
        depth_steps.append(steps(depth))
        if section < STEPS - 1:
            depth = advanced(depth, *depth_steps[-1])
    down_total = jnp.zeros((rows, columns), jnp.float32)
    side_total = jnp.zeros((rows, columns), jnp.float32)
    for section in reversed(range(STEPS)):
        down_step, side_step = steps(adjoint)
        down_total = down_total + depth_steps[section][0] * down_step
        side_total = side_total + depth_steps[section][1] * side_step
        adjoint = advanced(adjoint, down_step, side_step)
    down_total = jnp.where(down_face, down_total, 0.0)
    side_total = jnp.where(side_face, side_total, 0.0)
    total = (down_total + above(down_total)) + (side_total + leftward(side_total))
    own = slice(HALO, rows - HALO)
    grad_ref[...] = ((0.5 * courant) * conduct * total)[own]
    adjoint_ref[...] = adjoint[own]


def window(depth, rough, seed, low, high):
    shape = jax.ShapeDtypeStruct(depth.shape, jnp.float32)
    return pl.pallas_call(
        window_kernel,
        out_shape=(shape, shape),
        in_specs=[VMEM] * 5,
        out_specs=(VMEM, VMEM),
        compiler_params=ROOMY,
        name="adjoint_window",
    )(depth, rough, seed, low, high)


def halves(x):
    upper = x.astype(jnp.bfloat16).astype(jnp.float32)
    return upper, x - upper


HOME_ROWS = 8


def zone_sums(device_rows, lane_rows, grad_rows, square_rows):
    left = []
    right = []
    for device, lane, grad, square in zip(device_rows, lane_rows, grad_rows, square_rows):
        left.append(one_hot(spread_rows(device), 256))
        weights = [spread_rows(part) for part in halves(grad) + halves(square)]
        right.append(jnp.concatenate(one_hot(spread_rows(lane), LANES, weights), axis=0))
    both = lax.dot_general(
        jnp.concatenate(left, axis=1),
        jnp.concatenate(right, axis=1),
        (((1,), (1,)), ((), ())),
        preferred_element_type=jnp.float32,
    )
    return jnp.concatenate(
        [
            both[:, 0:LANES] + both[:, LANES : 2 * LANES],
            both[:, 2 * LANES : 3 * LANES] + both[:, 3 * LANES :],
        ],
        axis=1,
    )


def home_products(label_row, grad_row):
    width = label_row.shape[1]
    group = jnp.broadcast_to((label_row >> 3).astype(jnp.float32), (16, width))
    within = jnp.broadcast_to((label_row & 7).astype(jnp.float32), (16, width))
    ids = lax.broadcasted_iota(jnp.int32, (16, width), 0)
    zero = jnp.zeros((), jnp.bfloat16)
    group_hit = group.astype(jnp.bfloat16) == ids.astype(jnp.float32).astype(jnp.bfloat16)
    left = jnp.where(group_hit, jnp.ones((), jnp.bfloat16), zero)
    within_hit = within.astype(jnp.bfloat16) == (ids & 7).astype(jnp.float32).astype(jnp.bfloat16)
    right = []
    for value in (grad_row, grad_row * grad_row):
        pair = [jnp.broadcast_to(part, (8, width)) for part in halves(value)]
        weights = jnp.concatenate(pair, axis=0).astype(jnp.bfloat16)
        right.append(jnp.where(within_hit, weights, zero))
    return left, jnp.concatenate(right, axis=0)


def zone_kernel(
    place_ref,
    chunks_ref,
    grad_ref,
    label_ref,
    moves_ref,
    device_ref,
    lane_ref,
    home_ref,
    edge_ref,
    own_ref,
    first_ref,
    second_ref,
    third_ref,
    total_ref,
    stray_ref,
    offset_ref,
):
    offset_ref[...] = label_ref[...] - place_ref[0]
    grad = stacked(grad_ref[...])
    moves = moves_ref[...]
    bit = 0
    while 2**bit < grad.shape[0]:
        grad = jnp.where((moves & 2**bit) != 0, from_below(grad, 2**bit), grad)
        bit += 1
    stray_ref[...] = grad

    def home_rows(index, total):
        left = []
        right = []
        for step in range(HOME_ROWS):
            row = pl.ds(index * HOME_ROWS + step, 1)
            one_left, one_right = home_products(offset_ref[row, :], grad_ref[row, :])
            left.append(one_left)
            right.append(one_right)
        return total + lax.dot_general(
            jnp.concatenate(left, axis=1),
            jnp.concatenate(right, axis=1),
            (((1,), (1,)), ((), ())),
            preferred_element_type=jnp.float32,
        )

    home = lax.fori_loop(
        0,
        grad_ref.shape[0] // HOME_ROWS,
        home_rows,
        jnp.zeros((16, 32), jnp.float32),
        unroll=True,
    )
    part = lax.broadcasted_iota(jnp.int32, (32, 2 * LANES), 0)
    zone = lax.broadcasted_iota(jnp.int32, (32, 2 * LANES), 1)
    chosen = ((part & 7) == (zone & 7)) & ((part >= 16) == (zone >= LANES))
    home = jnp.dot(
        home,
        jnp.where(chosen, 1.0, 0.0),
        precision=lax.Precision.HIGHEST,
        preferred_element_type=jnp.float32,
    )
    group = lax.broadcasted_iota(jnp.int32, (16, 2 * LANES), 0)
    zone = lax.broadcasted_iota(jnp.int32, (16, 2 * LANES), 1)
    home = jnp.sum(jnp.where(((zone >> 3) & 15) == group, home, 0.0), axis=0, keepdims=True)
    total_ref[...] = zone_sums(
        [home_ref[0:1, :]], [home_ref[1:2, :]], [home[:, :LANES]], [home[:, LANES:]]
    )

    def one_chunk(index, carry):
        rows = [pl.ds(index * CHUNK + step, 1) for step in range(CHUNK)]
        grads = [stray_ref[row, :] for row in rows]
        total_ref[...] += zone_sums(
            [device_ref[row, :] for row in rows],
            [lane_ref[row, :] for row in rows],
            grads,
            [grad * grad for grad in grads],
        )
        return carry

    lax.fori_loop(0, chunks_ref[0], one_chunk, 0)
    tiles = own_ref.shape[0]
    own_ref[...] = total_ref[0:tiles, :]
    edge = jnp.broadcast_to(
        jnp.concatenate([edge_ref[0:1, :], edge_ref[1:2, :]], axis=1), (8, 2 * LANES)
    )
    for step, ref in enumerate((first_ref, second_ref, third_ref), 1):
        ref[0:tiles, :] = total_ref[step * tiles : (step + 1) * tiles, :]
        ref[tiles : tiles + 8, :] = edge


def zone_partials(place, chunks, grad, label, moves, device, lane, home, edge):
    sent = jax.ShapeDtypeStruct((72, 2 * LANES), jnp.float32)
    return pl.pallas_call(
        zone_kernel,
        out_shape=(jax.ShapeDtypeStruct((64, 2 * LANES), jnp.float32), sent, sent, sent),
        in_specs=[SMEM, SMEM] + [VMEM] * 7,
        out_specs=(VMEM,) * 4,
        scratch_shapes=[
            pltpu.VMEM((256, 2 * LANES), jnp.float32),
            pltpu.VMEM((grad.size // LANES, LANES), jnp.float32),
            pltpu.VMEM(grad.shape, jnp.int32),
        ],
        compiler_params=ROOMY,
        name="zone_partials",
    )(place, chunks, grad, label, moves, device, lane, home, edge)


def arrival_kernel(place_ref, own_ref, first_ref, second_ref, third_ref, sums_ref, incoming_ref):
    tiles = own_ref.shape[0]
    sums = own_ref[...] + first_ref[0:tiles, :]
    sums = sums + (second_ref[0:tiles, :] + third_ref[0:tiles, :])
    sums_ref[...] = sums.reshape(sums_ref.shape)
    basin = place_ref[1] // tiles
    incoming = jnp.zeros((8, LANES), jnp.float32)
    for hop, ref in ((3, first_ref), (2, second_ref), (1, third_ref)):
        edge = ref[tiles : tiles + 8, :]
        there = jnp.where(basin + hop < 4, 1.0, 0.0)
        incoming = there * (edge[:, :LANES] * incoming + edge[:, LANES:])
    incoming_ref[...] = incoming


def arrivals(place, own, *others):
    return pl.pallas_call(
        arrival_kernel,
        out_shape=(
            jax.ShapeDtypeStruct((own.shape[0], 1, own.shape[1]), jnp.float32),
            jax.ShapeDtypeStruct((8, LANES), jnp.float32),
        ),
        in_specs=[SMEM] + [VMEM] * 4,
        out_specs=(VMEM, VMEM),
        compiler_params=ROOMY,
        name="arrivals",
    )(place, own, *others)


def reach_kernel(adjoint_ref, cell_ref, keep_ref, forcing_ref, rate_ref, push_ref, edge_ref):
    rows, columns = adjoint_ref.shape
    upper, lower = halves(adjoint_ref[...])
    table = jnp.concatenate([upper, lower], axis=0).astype(jnp.bfloat16)
    reaches = cell_ref.shape[0]
    width = cell_ref.shape[1]
    values = []
    for reach in range(0, reaches, 4):
        cells = jnp.concatenate([cell_ref[reach + i : reach + i + 1, :] for i in range(4)], axis=1)
        column = (cells & (columns - 1)).astype(jnp.float32)
        hot = jnp.concatenate(
            [one_hot(spread_rows(column - part * 256.0), 256) for part in range(columns // 256)],
            axis=0,
        )
        picked = jnp.dot(table, hot, preferred_element_type=jnp.float32)
        picked = picked[:rows] + picked[rows:]
        row_hit = (cells >> 9) == lax.broadcasted_iota(jnp.int32, (rows, 4 * width), 0)
        found = jnp.sum(jnp.where(row_hit, picked, 0.0), axis=0, keepdims=True)
        values += [found[:, i * width : (i + 1) * width] for i in range(4)]
    rate = jnp.ones((1, width), jnp.float32)
    push = jnp.zeros((1, width), jnp.float32)
    for reach in reversed(range(reaches)):
        keep = keep_ref[reach : reach + 1, :]
        push = keep * push + (forcing_ref[reach : reach + 1, :] + levee_gain * values[reach])
        rate = keep * rate
        rate_ref[reach : reach + 1, :] = rate
        push_ref[reach : reach + 1, :] = push
    edge_ref[0:1, :] = rate
    edge_ref[1:2, :] = push


def reach_maps(adjoint, cells, keep, forcing):
    shape = jax.ShapeDtypeStruct(cells.shape, jnp.float32)
    return pl.pallas_call(
        reach_kernel,
        out_shape=(shape, shape, jax.ShapeDtypeStruct((2, cells.shape[1]), jnp.float32)),
        in_specs=[VMEM] * 4,
        out_specs=(VMEM, VMEM, VMEM),
        compiler_params=ROOMY,
        name="reach_maps",
    )(adjoint, cells, keep, forcing)


def moved(value, axis, steps):
    count = lax.axis_size(axis)
    pairs = [(i, i + steps) for i in range(count) if 0 <= i + steps < count]
    return lax.ppermute(value, axis, pairs)


def turned(value, axis, steps):
    count = lax.axis_size(axis)
    return lax.ppermute(value, axis, [(i, (i + steps) % count) for i in range(count)])


def per_device(
    depth_start, roughness, depth_seed, zone_label, owner_slot, retention, forcing, levee_cell
):
    depth, rough, seed, label = depth_start[0], roughness[0], depth_seed[0], zone_label[0]
    tiles = lax.axis_size("tile")
    first_device = lax.axis_index("basin") * tiles
    place = jnp.stack([(first_device + lax.axis_index("tile")) * SPAN, first_device])
    place = place.astype(jnp.int32)
    to_next, to_last = edges_to_send(depth, rough, seed)
    low = moved(to_next, "tile", 1)
    high = moved(to_last, "tile", -1)
    moves, device, lane, home, chunks = slots_of(place, owner_slot, label)
    grad, adjoint = window(depth, rough, seed, low, high)
    rate, push, edge = reach_maps(adjoint, levee_cell, retention, forcing)
    own, *others = zone_partials(place, chunks, grad, label, moves, device, lane, home, edge)
    others = [turned(part, "basin", step) for step, part in enumerate(others, 1)]
    sums, incoming = arrivals(place, own, *others)
    arrived = lax.all_to_all(sums, "tile", 0, 0, tiled=True)
    reach_adjoint = rate * incoming[:1] + push
    sums = jnp.sum(arrived, axis=(0, 1))
    return (sums[:SPAN], sums[LANES : LANES + SPAN], reach_adjoint)


def solution(mesh):
    in_specs = (
        P("basin", "tile", None),
        P("basin", "tile", None),
        P("basin", "tile", None),
        P("basin", "tile", None),
        P(),
        P("basin", "tile"),
        P("basin", "tile"),
        P("basin", "tile"),
    )
    out_specs = (P(("basin", "tile")), P(("basin", "tile")), P("basin", "tile"))
    return jax.shard_map(
        per_device, mesh=mesh, in_specs=in_specs, out_specs=out_specs, check_vma=False
    )
```

```python
import functools

import jax
import jax.numpy as jnp
from jax import lax
from jax.experimental import pallas as pl
from jax.experimental.pallas import tpu as pltpu
from jax.sharding import PartitionSpec as P

STEPS = 4
HALO = STEPS
SPAN = 127
LANES = 128

courant = 0.24
rough_ref = 0.025
levee_gain = 0.1

VMEM = pl.BlockSpec(memory_space=pltpu.VMEM)
ROOMY = pltpu.CompilerParams(vmem_limit_bytes=48 * 2**20)


def iota_bf16(shape, offset=0):
    ids = lax.broadcasted_iota(jnp.int32, shape, len(shape) - 2)
    if len(shape) == 3:
        ids = ids + shape[1] * lax.broadcasted_iota(jnp.int32, shape, 0)
    return (ids + offset).astype(jnp.float32).astype(jnp.bfloat16)


def spread_rows(row):
    return jnp.broadcast_to(row, (16, row.shape[1])).astype(jnp.bfloat16)


def one_hot(spread, count, weights=None):
    width = spread.shape[1]
    ids = iota_bf16((count // 16, 16, width))
    hit = spread[None] == ids
    zero = jnp.zeros((), jnp.bfloat16)
    if weights is None:
        return jnp.where(hit, jnp.ones((), jnp.bfloat16), zero).reshape(count, width)
    return [jnp.where(hit, w[None], zero).reshape(count, width) for w in weights]


def stacked(x):
    return jnp.concatenate(
        [x[:, start : start + LANES] for start in range(0, x.shape[1], LANES)], axis=0
    )


def from_below(x, distance):
    return pltpu.roll(x, x.shape[0] - distance, 0)


HBM = pl.BlockSpec(memory_space=pltpu.HBM)


FETCH = pltpu.CompilerParams(vmem_limit_bytes=55800000)


def front_kernel(*refs):
    count = (len(refs) - 3) // 2
    sources, kept = refs[:count], refs[count : 2 * count]
    chip_ref, away_ref, arrived = refs[2 * count :]
    copies = [
        pltpu.make_async_copy(source, place, arrived.at[index])
        for index, (source, place) in enumerate(zip(sources, kept))
    ]
    for copy in copies:
        copy.start()
    first_core = lax.axis_index("core") == 0
    for part in range(3):
        copies[part].wait()
        ref = kept[part]
        rows = slice(part * HALO, (part + 1) * HALO)
        top = ref[0:HALO, :]
        bottom = ref[ref.shape[0] - HALO :, :]
        chip_ref[rows, :] = jnp.where(first_core, bottom, top)
        away_ref[rows, :] = jnp.where(first_core, top, bottom)
    for copy in copies[3:]:
        copy.wait()


def fetched(*arrays):
    edge = jax.ShapeDtypeStruct((3 * HALO, arrays[0].shape[1]), jnp.float32)
    kept = tuple(jax.ShapeDtypeStruct(x.shape, x.dtype) for x in arrays)
    return pl.pallas_call(
        front_kernel,
        out_shape=kept + (edge, edge),
        in_specs=[HBM] * len(arrays),
        out_specs=(VMEM,) * (len(arrays) + 2),
        scratch_shapes=[pltpu.SemaphoreType.DMA((len(arrays),))],
        compiler_params=FETCH,
        name="fetch_and_edges",
    )(*arrays)


ABSENT = 2**15 - 1


def own_first_zone():
    chip = lax.axis_index("basin") * lax.axis_size("chip") + lax.axis_index("chip")
    return (chip * lax.axis_size("core") + lax.axis_index("core")) * SPAN


CHUNK = 16


def slot_kernel(
    owner_ref,
    label_ref,
    moves_ref,
    device_ref,
    lane_ref,
    home_ref,
    chunks_ref,
    table_ref,
    turned_ref,
    packed_ref,
):
    first_zone = own_first_zone()
    core = lax.axis_index("core").astype(jnp.float32)
    table_ref[...] = jnp.full(table_ref.shape, 256.0 * SPAN, jnp.float32)
    table_ref[0 : owner_ref.shape[0], :] = owner_ref[...].astype(jnp.float32)

    def placed(slots):
        owners = jnp.floor((slots + 0.5) * (1.0 / SPAN))
        lanes = slots - owners * SPAN
        chips = jnp.floor(owners * 0.5)
        swapped = jnp.abs((owners - 2.0 * chips) - core)
        return jnp.where(owners < 256.0, chips + 128.0 * swapped, 256.0), lanes

    owners, lanes = placed(jnp.transpose(table_ref[...]))
    turned_ref[0:LANES, :] = owners.astype(jnp.bfloat16)
    turned_ref[LANES : 2 * LANES, :] = lanes.astype(jnp.bfloat16)

    home_row = first_zone // LANES
    shift = first_zone % LANES
    back = jnp.where(shift == 0, 0, LANES - shift)
    pair = table_ref[pl.ds(home_row, 1), :], table_ref[pl.ds(home_row + 1, 1), :]
    pair = [pltpu.roll(jnp.broadcast_to(row, (8, LANES)), back, 1) for row in pair]
    spot = lax.broadcasted_iota(jnp.int32, (8, LANES), 1)
    home = jnp.where(spot + shift < LANES, pair[0], pair[1])
    home_device, home_lane = placed(jnp.where(spot < SPAN, home, 256.0 * SPAN))
    top = lax.broadcasted_iota(jnp.int32, (8, LANES), 0) == 0
    home_ref[...] = jnp.where(top, home_device, home_lane)

    label = stacked(label_ref[...])
    count = label.shape[0]
    offset = label - first_zone
    at_home = (offset >= 0) & (offset < SPAN)
    at_home_count = jnp.where(at_home, 1.0, 0.0)
    row_ids = lax.broadcasted_iota(jnp.int32, (count, count), 0)
    column_ids = lax.broadcasted_iota(jnp.int32, (count, count), 1)
    earlier = jnp.where(column_ids < row_ids, 1.0, 0.0).astype(jnp.bfloat16)
    gaps = jnp.dot(
        earlier, at_home_count.astype(jnp.bfloat16), preferred_element_type=jnp.float32
    ).astype(jnp.int32)
    packed = jnp.where(at_home, ABSENT, gaps * (ABSENT + 1) + label)
    moves = jnp.zeros(packed.shape, jnp.int32)
    bit = 0
    while 2**bit < count:
        marker = (ABSENT + 1) * 2**bit
        near = from_below(packed, 2**bit)
        taken = (near & marker) != 0
        left = (packed & marker) != 0
        packed = jnp.where(taken, near, jnp.where(left, ABSENT, packed))
        moves = jnp.where(taken, moves + 2**bit, moves)
        bit += 1
    moves_ref[...] = moves
    packed_ref[...] = packed & ABSENT
    most = count - jnp.min(jnp.sum(at_home_count, axis=0, keepdims=True)).astype(jnp.int32)
    chunks = (most + CHUNK - 1) // CHUNK
    chunks_ref[0] = chunks

    def one_chunk(index, carry):
        for quarter in range(CHUNK // 4):
            start = index * CHUNK + quarter * 4
            group_label = jnp.concatenate(
                [packed_ref[pl.ds(start + i, 1), :] for i in range(4)], axis=1
            )
            width = group_label.shape[1]
            group = one_hot(spread_rows((group_label >> 7).astype(jnp.float32)), 256)
            found = jnp.dot(turned_ref[...], group, preferred_element_type=jnp.float32)
            hit = (group_label & 127) == lax.broadcasted_iota(jnp.int32, (LANES, width), 0)
            for half, ref in enumerate((device_ref, lane_ref)):
                part = found[half * LANES : (half + 1) * LANES]
                part = jnp.sum(jnp.where(hit, part, 0.0), axis=0, keepdims=True)
                for i in range(4):
                    ref[pl.ds(start + i, 1), :] = part[:, i * LANES : (i + 1) * LANES]
        return carry

    lax.fori_loop(0, chunks, one_chunk, 0)


SMEM = pl.BlockSpec(memory_space=pltpu.SMEM)


def slots_of(owner_slot, label):
    count = label.size // LANES
    stack = jax.ShapeDtypeStruct((count, LANES), jnp.float32)
    return pl.pallas_call(
        slot_kernel,
        out_shape=(
            jax.ShapeDtypeStruct((count, LANES), jnp.int32),
            stack,
            stack,
            jax.ShapeDtypeStruct((8, LANES), jnp.float32),
            jax.ShapeDtypeStruct((1,), jnp.int32),
        ),
        in_specs=[VMEM, VMEM],
        out_specs=(VMEM, VMEM, VMEM, VMEM, SMEM),
        scratch_shapes=[
            pltpu.VMEM((256, LANES), jnp.float32),
            pltpu.VMEM((256, 256), jnp.bfloat16),
            pltpu.VMEM((count, LANES), jnp.int32),
        ],
        compiler_params=ROOMY,
        cost_estimate=pl.CostEstimate(
            flops=2 * 256 * 256 * label.size // 4, bytes_accessed=16 * label.size, transcendentals=0
        ),
        name="slot_lookup",
    )(owner_slot, label)


def below(x):
    return pltpu.roll(x, x.shape[0] - 1, 0)


def above(x):
    return pltpu.roll(x, 1, 0)


def rightward(x):
    return pltpu.roll(x, x.shape[1] - 1, 1)


def leftward(x):
    return pltpu.roll(x, 1, 1)


def window_kernel(depth_ref, rough_ref_, seed_ref, chip_ref, away_ref, grad_ref, adjoint_ref):
    first_core = lax.axis_index("core") == 0

    def extended(part, ref):
        rows = slice(part * HALO, (part + 1) * HALO)
        chip, away = chip_ref[rows, :], away_ref[rows, :]
        low = jnp.where(first_core, away, chip)
        high = jnp.where(first_core, chip, away)
        return jnp.concatenate([low, ref[...], high], axis=0)

    depth = extended(0, depth_ref)
    rough = extended(1, rough_ref_)
    adjoint = extended(2, seed_ref)
    rows, columns = depth.shape
    conduct = jnp.where(rough > 0, rough_ref / jnp.where(rough > 0, rough, 1.0), 0.0)
    not_last = lax.broadcasted_iota(jnp.int32, (rows, columns), 1) < columns - 1
    under = below(conduct)
    beside = rightward(conduct)
    down_face = (conduct > 0) & (under > 0)
    side_face = (conduct > 0) & (beside > 0) & not_last
    down_weight = jnp.where(down_face, (0.5 * courant) * (conduct + under), 0.0)
    side_weight = jnp.where(side_face, (0.5 * courant) * (conduct + beside), 0.0)

    def steps(field):
        return below(field) - field, rightward(field) - field

    def advanced(field, down_step, side_step):
        down_flux = down_weight * down_step
        side_flux = side_weight * side_step
        return field + ((down_flux - above(down_flux)) + (side_flux - leftward(side_flux)))

    depth_steps = []
    for section in range(STEPS):
        depth_steps.append(steps(depth))
        if section < STEPS - 1:
            depth = advanced(depth, *depth_steps[-1])
    down_total = jnp.zeros((rows, columns), jnp.float32)
    side_total = jnp.zeros((rows, columns), jnp.float32)
    for section in reversed(range(STEPS)):
        down_step, side_step = steps(adjoint)
        down_total = down_total + depth_steps[section][0] * down_step
        side_total = side_total + depth_steps[section][1] * side_step
        adjoint = advanced(adjoint, down_step, side_step)
    down_total = jnp.where(down_face, down_total, 0.0)
    side_total = jnp.where(side_face, side_total, 0.0)
    total = (down_total + above(down_total)) + (side_total + leftward(side_total))
    own = slice(HALO, rows - HALO)
    grad_ref[...] = ((0.5 * courant) * conduct * total)[own]
    adjoint_ref[...] = adjoint[own]


def window(depth, rough, seed, chip, away):
    shape = jax.ShapeDtypeStruct(depth.shape, jnp.float32)
    return pl.pallas_call(
        window_kernel,
        out_shape=(shape, shape),
        in_specs=[VMEM] * 5,
        out_specs=(VMEM, VMEM),
        compiler_params=ROOMY,
        name="adjoint_window",
    )(depth, rough, seed, chip, away)


def halves(x):
    upper = x.astype(jnp.bfloat16).astype(jnp.float32)
    return upper, x - upper


HOME_ROWS = 8


def zone_sums(device_rows, lane_rows, grad_rows, square_rows):
    left = []
    right = []
    for device, lane, grad, square in zip(device_rows, lane_rows, grad_rows, square_rows):
        left.append(one_hot(spread_rows(device), 256))
        weights = [spread_rows(part) for part in halves(grad) + halves(square)]
        right.append(jnp.concatenate(one_hot(spread_rows(lane), LANES, weights), axis=0))
    both = lax.dot_general(
        jnp.concatenate(left, axis=1),
        jnp.concatenate(right, axis=1),
        (((1,), (1,)), ((), ())),
        preferred_element_type=jnp.float32,
    )
    return jnp.concatenate(
        [
            both[:, 0:LANES] + both[:, LANES : 2 * LANES],
            both[:, 2 * LANES : 3 * LANES] + both[:, 3 * LANES :],
        ],
        axis=1,
    )


def home_products(label_row, grad_row):
    width = label_row.shape[1]
    group = jnp.broadcast_to((label_row >> 3).astype(jnp.float32), (16, width))
    within = jnp.broadcast_to((label_row & 7).astype(jnp.float32), (16, width))
    ids = lax.broadcasted_iota(jnp.int32, (16, width), 0)
    zero = jnp.zeros((), jnp.bfloat16)
    group_hit = group.astype(jnp.bfloat16) == ids.astype(jnp.float32).astype(jnp.bfloat16)
    left = jnp.where(group_hit, jnp.ones((), jnp.bfloat16), zero)
    within_hit = within.astype(jnp.bfloat16) == (ids & 7).astype(jnp.float32).astype(jnp.bfloat16)
    right = []
    for value in (grad_row, grad_row * grad_row):
        pair = [jnp.broadcast_to(part, (8, width)) for part in halves(value)]
        weights = jnp.concatenate(pair, axis=0).astype(jnp.bfloat16)
        right.append(jnp.where(within_hit, weights, zero))
    return left, jnp.concatenate(right, axis=0)


def zone_kernel(
    chunks_ref,
    grad_ref,
    label_ref,
    moves_ref,
    device_ref,
    lane_ref,
    home_ref,
    own_ref,
    other_ref,
    total_ref,
    stray_ref,
    offset_ref,
):
    offset_ref[...] = label_ref[...] - own_first_zone()
    grad = stacked(grad_ref[...])
    moves = moves_ref[...]
    bit = 0
    while 2**bit < grad.shape[0]:
        grad = jnp.where((moves & 2**bit) != 0, from_below(grad, 2**bit), grad)
        bit += 1
    stray_ref[...] = grad

    def home_rows(index, total):
        left = []
        right = []
        for step in range(HOME_ROWS):
            row = pl.ds(index * HOME_ROWS + step, 1)
            one_left, one_right = home_products(offset_ref[row, :], grad_ref[row, :])
            left.append(one_left)
            right.append(one_right)
        return total + lax.dot_general(
            jnp.concatenate(left, axis=1),
            jnp.concatenate(right, axis=1),
            (((1,), (1,)), ((), ())),
            preferred_element_type=jnp.float32,
        )

    home = lax.fori_loop(
        0,
        grad_ref.shape[0] // HOME_ROWS,
        home_rows,
        jnp.zeros((16, 32), jnp.float32),
        unroll=True,
    )
    part = lax.broadcasted_iota(jnp.int32, (32, 2 * LANES), 0)
    zone = lax.broadcasted_iota(jnp.int32, (32, 2 * LANES), 1)
    chosen = ((part & 7) == (zone & 7)) & ((part >= 16) == (zone >= LANES))
    home = jnp.dot(
        home,
        jnp.where(chosen, 1.0, 0.0),
        precision=lax.Precision.HIGHEST,
        preferred_element_type=jnp.float32,
    )
    group = lax.broadcasted_iota(jnp.int32, (16, 2 * LANES), 0)
    zone = lax.broadcasted_iota(jnp.int32, (16, 2 * LANES), 1)
    home = jnp.sum(jnp.where(((zone >> 3) & 15) == group, home, 0.0), axis=0, keepdims=True)
    total_ref[...] = zone_sums(
        [home_ref[0:1, :]], [home_ref[1:2, :]], [home[:, :LANES]], [home[:, LANES:]]
    )

    def one_chunk(index, carry):
        rows = [pl.ds(index * CHUNK + step, 1) for step in range(CHUNK)]
        grads = [stray_ref[row, :] for row in rows]
        total_ref[...] += zone_sums(
            [device_ref[row, :] for row in rows],
            [lane_ref[row, :] for row in rows],
            grads,
            [grad * grad for grad in grads],
        )
        return carry

    lax.fori_loop(0, chunks_ref[0], one_chunk, 0)
    own_ref[...] = total_ref[0:LANES, :]
    other_ref[...] = total_ref[LANES:, :]


def zone_partials(chunks, grad, label, moves, device, lane, home):
    half = jax.ShapeDtypeStruct((LANES, 2 * LANES), jnp.float32)
    return pl.pallas_call(
        zone_kernel,
        out_shape=(half, half),
        in_specs=[SMEM] + [VMEM] * 6,
        out_specs=(VMEM,) * 2,
        scratch_shapes=[
            pltpu.VMEM((256, 2 * LANES), jnp.float32),
            pltpu.VMEM((grad.size // LANES, LANES), jnp.float32),
            pltpu.VMEM(grad.shape, jnp.int32),
        ],
        compiler_params=ROOMY,
        name="zone_partials",
    )(chunks, grad, label, moves, device, lane, home)


def parcel_kernel(own_ref, other_ref, edge_ref, out_ref):
    chips = own_ref.shape[0]
    sums = own_ref[...] + other_ref[...]
    out_ref[pl.ds(0, chips, stride=4), :] = sums[:, :LANES]
    out_ref[pl.ds(1, chips, stride=4), :] = sums[:, LANES:]
    for part in range(2):
        edge = jnp.broadcast_to(edge_ref[part : part + 1, :], (chips, LANES))
        out_ref[pl.ds(2 + part, chips, stride=4), :] = edge


def parcels(own, other, edge):
    return pl.pallas_call(
        parcel_kernel,
        out_shape=jax.ShapeDtypeStruct((4 * own.shape[0], LANES), jnp.float32),
        in_specs=[VMEM] * 3,
        out_specs=VMEM,
        compiler_params=ROOMY,
        name="parcels",
    )(own, other, edge)


def result_kernel(arrived_ref, rate_ref, push_ref, grad_ref, curve_ref, reach_ref):
    rows = arrived_ref.shape[0]
    sums = arrived_ref[0:8, :]
    for start in range(8, rows, 8):
        sums = sums + arrived_ref[start : start + 8, :]
    grad_ref[...] = (sums[0:1, :] + sums[4:5, :])[:, :SPAN]
    curve_ref[...] = (sums[1:2, :] + sums[5:6, :])[:, :SPAN]
    basin, chip = lax.axis_index("basin"), lax.axis_index("chip")
    basins, chips = lax.axis_size("basin"), lax.axis_size("chip")
    incoming = jnp.zeros((1, LANES), jnp.float32)
    for hop in reversed(range(1, basins)):
        there = jnp.where(basin + hop < basins, 1.0, 0.0)
        row = 4 * (jnp.minimum(basin + hop, basins - 1) * chips + chip)
        rate = arrived_ref[pl.ds(row + 2, 1), :]
        push = arrived_ref[pl.ds(row + 3, 1), :]
        incoming = there * (rate * incoming + push)
    reach_ref[...] = rate_ref[...] * incoming + push_ref[...]


def results(arrived, rate, push):
    zone = jax.ShapeDtypeStruct((1, SPAN), jnp.float32)
    return pl.pallas_call(
        result_kernel,
        out_shape=(zone, zone, jax.ShapeDtypeStruct(rate.shape, jnp.float32)),
        in_specs=[VMEM] * 3,
        out_specs=(VMEM,) * 3,
        compiler_params=ROOMY,
        name="results",
    )(arrived, rate, push)


def reach_kernel(adjoint_ref, cell_ref, keep_ref, forcing_ref, rate_ref, push_ref, edge_ref):
    rows, columns = adjoint_ref.shape
    upper, lower = halves(adjoint_ref[...])
    table = jnp.concatenate([upper, lower], axis=0).astype(jnp.bfloat16)
    reaches = cell_ref.shape[0]
    width = cell_ref.shape[1]
    values = []
    for reach in range(0, reaches, 4):
        cells = jnp.concatenate([cell_ref[reach + i : reach + i + 1, :] for i in range(4)], axis=1)
        column = (cells & (columns - 1)).astype(jnp.float32)
        hot = jnp.concatenate(
            [one_hot(spread_rows(column - part * 256.0), 256) for part in range(columns // 256)],
            axis=0,
        )
        picked = jnp.dot(table, hot, preferred_element_type=jnp.float32)
        picked = picked[:rows] + picked[rows:]
        row_hit = (cells >> 9) == lax.broadcasted_iota(jnp.int32, (rows, 4 * width), 0)
        found = jnp.sum(jnp.where(row_hit, picked, 0.0), axis=0, keepdims=True)
        values += [found[:, i * width : (i + 1) * width] for i in range(4)]
    rate = jnp.ones((1, width), jnp.float32)
    push = jnp.zeros((1, width), jnp.float32)
    for reach in reversed(range(reaches)):
        keep = keep_ref[reach : reach + 1, :]
        push = keep * push + (forcing_ref[reach : reach + 1, :] + levee_gain * values[reach])
        rate = keep * rate
        rate_ref[reach : reach + 1, :] = rate
        push_ref[reach : reach + 1, :] = push
    edge_ref[0:1, :] = rate
    edge_ref[1:2, :] = push


def reach_maps(adjoint, cells, keep, forcing):
    shape = jax.ShapeDtypeStruct(cells.shape, jnp.float32)
    return pl.pallas_call(
        reach_kernel,
        out_shape=(shape, shape, jax.ShapeDtypeStruct((2, cells.shape[1]), jnp.float32)),
        in_specs=[VMEM] * 4,
        out_specs=(VMEM, VMEM, VMEM),
        compiler_params=ROOMY,
        name="reach_maps",
    )(adjoint, cells, keep, forcing)


def swapped(value):
    return lax.ppermute(value, "core", [(0, 1), (1, 0)])


def exchanged_away(value):
    chips, cores = lax.axis_size("chip"), lax.axis_size("core")
    edges = [(i, i + 1) for i in range(1, chips * cores - 1, 2)]
    return lax.ppermute(value, ("chip", "core"), edges + [(j, i) for i, j in edges])


def per_device(
    depth_start, roughness, depth_seed, zone_label, owner_slot, retention, forcing, levee_cell
):
    depth, rough, seed, label, owner_slot, to_chip, to_away = fetched(
        depth_start[0],
        roughness[0],
        depth_seed[0],
        zone_label[0],
        owner_slot.reshape(-1, LANES),
    )
    from_away = exchanged_away(to_away)
    from_chip = swapped(to_chip)
    moves, device, lane, home, chunks = slots_of(owner_slot, label)
    grad, adjoint = window(depth, rough, seed, from_chip, from_away)
    own, other = zone_partials(chunks, grad, label, moves, device, lane, home)
    other = swapped(other)
    rate, push, edge = reach_maps(adjoint, levee_cell, retention, forcing)
    sent = parcels(own, other, edge).reshape(-1, 4, LANES)
    arrived = lax.all_to_all(sent, ("basin", "chip"), 0, 0, tiled=True)
    grad, curve, reach_adjoint = results(arrived.reshape(-1, LANES), rate, push)
    return (grad.reshape(-1), curve.reshape(-1), reach_adjoint)


def solution(mesh):
    basins, tiles = mesh.devices.shape
    fine = jax.sharding.Mesh(
        mesh.devices.reshape(basins, tiles // 2, 2), ("basin", "chip", "core")
    )
    tile = ("chip", "core")
    cells = P("basin", tile, None)
    reaches = P("basin", tile)
    zones = P(("basin", "chip", "core"))
    return jax.shard_map(
        per_device,
        mesh=fine,
        in_specs=(cells, cells, cells, cells, P(), reaches, reaches, reaches),
        out_specs=(zones, zones, reaches),
        check_vma=False,
    )
```

```python
import functools

import jax
import jax.numpy as jnp
from jax import lax
from jax.experimental import pallas as pl
from jax.experimental.pallas import tpu as pltpu
from jax.sharding import PartitionSpec as P

STEPS = 4
HALO = STEPS
SPAN = 127
LANES = 128

courant = 0.24
rough_ref = 0.025
levee_gain = 0.1

VMEM = pl.BlockSpec(memory_space=pltpu.VMEM)
ROOMY = pltpu.CompilerParams(vmem_limit_bytes=48 * 2**20)


def iota_bf16(shape, offset=0):
    ids = lax.broadcasted_iota(jnp.int32, shape, len(shape) - 2)
    if len(shape) == 3:
        ids = ids + shape[1] * lax.broadcasted_iota(jnp.int32, shape, 0)
    return (ids + offset).astype(jnp.float32).astype(jnp.bfloat16)


def spread_rows(row):
    return jnp.broadcast_to(row, (16, row.shape[1])).astype(jnp.bfloat16)


def one_hot(spread, count, weights=None):
    width = spread.shape[1]
    ids = iota_bf16((count // 16, 16, width))
    hit = spread[None] == ids
    zero = jnp.zeros((), jnp.bfloat16)
    if weights is None:
        return jnp.where(hit, jnp.ones((), jnp.bfloat16), zero).reshape(count, width)
    return [jnp.where(hit, w[None], zero).reshape(count, width) for w in weights]


def stacked(x):
    return jnp.concatenate(
        [x[:, start : start + LANES] for start in range(0, x.shape[1], LANES)], axis=0
    )


def from_below(x, distance):
    return pltpu.roll(x, x.shape[0] - distance, 0)


HBM = pl.BlockSpec(memory_space=pltpu.HBM)


FETCH = pltpu.CompilerParams(vmem_limit_bytes=55800000)


def front_kernel(*refs):
    count = (len(refs) - 3) // 2
    sources, kept = refs[:count], refs[count : 2 * count]
    chip_ref, away_ref, arrived = refs[2 * count :]
    copies = [
        pltpu.make_async_copy(source, place, arrived.at[index])
        for index, (source, place) in enumerate(zip(sources, kept))
    ]
    for copy in copies:
        copy.start()
    first_core = lax.axis_index("core") == 0
    for part in range(3):
        copies[part].wait()
        ref = kept[part]
        rows = slice(part * HALO, (part + 1) * HALO)
        top = ref[0:HALO, :]
        bottom = ref[ref.shape[0] - HALO :, :]
        chip_ref[rows, :] = jnp.where(first_core, bottom, top)
        away_ref[rows, :] = jnp.where(first_core, top, bottom)
    for copy in copies[3:]:
        copy.wait()


def fetched(*arrays):
    edge = jax.ShapeDtypeStruct((3 * HALO, arrays[0].shape[1]), jnp.float32)
    kept = tuple(jax.ShapeDtypeStruct(x.shape, x.dtype) for x in arrays)
    return pl.pallas_call(
        front_kernel,
        out_shape=kept + (edge, edge),
        in_specs=[HBM] * len(arrays),
        out_specs=(VMEM,) * (len(arrays) + 2),
        scratch_shapes=[pltpu.SemaphoreType.DMA((len(arrays),))],
        compiler_params=FETCH,
        name="fetch_and_edges",
    )(*arrays)


ABSENT = 2**15 - 1


def own_first_zone():
    chip = lax.axis_index("basin") * lax.axis_size("chip") + lax.axis_index("chip")
    return (chip * lax.axis_size("core") + lax.axis_index("core")) * SPAN


BASE_ROWS = 48
CHUNK = 8


def slot_kernel(
    owner_ref,
    label_ref,
    moves_ref,
    device_ref,
    lane_ref,
    home_ref,
    table_ref,
    turned_ref,
    packed_ref,
):
    first_zone = own_first_zone()
    core = lax.axis_index("core").astype(jnp.float32)
    table_ref[...] = jnp.full(table_ref.shape, 256.0 * SPAN, jnp.float32)
    table_ref[0 : owner_ref.shape[0], :] = owner_ref[...].astype(jnp.float32)

    def placed(slots):
        owners = jnp.floor((slots + 0.5) * (1.0 / SPAN))
        lanes = slots - owners * SPAN
        chips = jnp.floor(owners * 0.5)
        swapped = jnp.abs((owners - 2.0 * chips) - core)
        return jnp.where(owners < 256.0, chips + 128.0 * swapped, 256.0), lanes

    owners, lanes = placed(jnp.transpose(table_ref[...]))
    turned_ref[:, 0:256] = (owners * LANES).astype(jnp.bfloat16)
    turned_ref[:, 256:512] = lanes.astype(jnp.bfloat16)

    home_row = first_zone // LANES
    shift = first_zone % LANES
    back = jnp.where(shift == 0, 0, LANES - shift)
    pair = table_ref[pl.ds(home_row, 1), :], table_ref[pl.ds(home_row + 1, 1), :]
    pair = [pltpu.roll(jnp.broadcast_to(row, (8, LANES)), back, 1) for row in pair]
    spot = lax.broadcasted_iota(jnp.int32, (8, LANES), 1)
    home = jnp.where(spot + shift < LANES, pair[0], pair[1])
    home_device, home_lane = placed(jnp.where(spot < SPAN, home, 256.0 * SPAN))
    home_ref[0:1, :] = home_device[0:1]
    home_ref[1:2, :] = home_lane[0:1]

    label = stacked(label_ref[...])
    count = label.shape[0]
    offset = label - first_zone
    at_home = (offset >= 0) & (offset < SPAN)
    at_home_count = jnp.where(at_home, 1.0, 0.0)
    row_ids = lax.broadcasted_iota(jnp.int32, (count, count), 0)
    column_ids = lax.broadcasted_iota(jnp.int32, (count, count), 1)
    earlier = jnp.where(column_ids < row_ids, 1.0, 0.0).astype(jnp.bfloat16)
    gaps = jnp.dot(
        earlier, at_home_count.astype(jnp.bfloat16), preferred_element_type=jnp.float32
    ).astype(jnp.int32)
    packed = jnp.where(at_home, ABSENT, gaps * (ABSENT + 1) + label)
    moves = jnp.zeros(packed.shape, jnp.int32)
    bit = 0
    while 2**bit < count:
        marker = (ABSENT + 1) * 2**bit
        near = from_below(packed, 2**bit)
        taken = (near & marker) != 0
        left = (packed & marker) != 0
        packed = jnp.where(taken, near, jnp.where(left, ABSENT, packed))
        moves = jnp.where(taken, moves + 2**bit, moves)
        bit += 1
    moves_ref[...] = moves
    packed_ref[...] = packed & ABSENT
    most = count - jnp.min(jnp.sum(at_home_count, axis=0, keepdims=True)).astype(jnp.int32)
    chunks = jnp.maximum((most - BASE_ROWS + CHUNK - 1) // CHUNK, 0)
    home_ref[2:3, :] = jnp.full((1, LANES), chunks.astype(jnp.float32))

    def look_up(first, rows):
        for start in range(0, rows, 4):
            places = [pl.ds(first + start + i, 1) for i in range(4)]
            group_label = jnp.concatenate([packed_ref[place, :] for place in places], axis=1)
            width = group_label.shape[1]
            group = one_hot(spread_rows((group_label >> 7).astype(jnp.float32)), 256)
            found = jnp.dot(
                turned_ref[...],
                jnp.concatenate([group, group], axis=0),
                preferred_element_type=jnp.float32,
            )
            hit = (group_label & 127) == lax.broadcasted_iota(jnp.int32, (LANES, width), 0)
            slot = jnp.sum(jnp.where(hit, found, 0.0), axis=0, keepdims=True)
            owner = jnp.floor(slot * (1.0 / LANES))
            lane = slot - owner * LANES
            for i, place in enumerate(places):
                device_ref[place, :] = owner[:, i * LANES : (i + 1) * LANES]
                lane_ref[place, :] = lane[:, i * LANES : (i + 1) * LANES]

    def one_chunk(index, carry):
        look_up(BASE_ROWS + index * CHUNK, CHUNK)
        return carry

    look_up(0, BASE_ROWS)
    lax.fori_loop(0, chunks, one_chunk, 0)


def slots_of(owner_slot, label):
    count = label.size // LANES
    stack = jax.ShapeDtypeStruct((count, LANES), jnp.float32)
    return pl.pallas_call(
        slot_kernel,
        out_shape=(
            jax.ShapeDtypeStruct((count, LANES), jnp.int32),
            stack,
            stack,
            jax.ShapeDtypeStruct((8, LANES), jnp.float32),
        ),
        in_specs=[VMEM, VMEM],
        out_specs=(VMEM,) * 4,
        scratch_shapes=[
            pltpu.VMEM((256, LANES), jnp.float32),
            pltpu.VMEM((LANES, 512), jnp.bfloat16),
            pltpu.VMEM((count, LANES), jnp.int32),
        ],
        compiler_params=ROOMY,
        cost_estimate=pl.CostEstimate(
            flops=2 * 256 * 256 * label.size // 4, bytes_accessed=16 * label.size, transcendentals=0
        ),
        name="slot_lookup",
    )(owner_slot, label)


def below(x):
    return pltpu.roll(x, x.shape[0] - 1, 0)


def above(x):
    return pltpu.roll(x, 1, 0)


def rightward(x):
    return pltpu.roll(x, x.shape[1] - 1, 1)


def leftward(x):
    return pltpu.roll(x, 1, 1)


def window_kernel(depth_ref, rough_ref_, seed_ref, chip_ref, away_ref, grad_ref, adjoint_ref):
    first_core = lax.axis_index("core") == 0

    def extended(part, ref):
        rows = slice(part * HALO, (part + 1) * HALO)
        chip, away = chip_ref[rows, :], away_ref[rows, :]
        low = jnp.where(first_core, away, chip)
        high = jnp.where(first_core, chip, away)
        return jnp.concatenate([low, ref[...], high], axis=0)

    depth = extended(0, depth_ref)
    rough = extended(1, rough_ref_)
    adjoint = extended(2, seed_ref)
    rows, columns = depth.shape
    conduct = jnp.where(rough > 0, rough_ref / jnp.where(rough > 0, rough, 1.0), 0.0)
    not_last = lax.broadcasted_iota(jnp.int32, (rows, columns), 1) < columns - 1
    under = below(conduct)
    beside = rightward(conduct)
    down_face = (conduct > 0) & (under > 0)
    side_face = (conduct > 0) & (beside > 0) & not_last
    down_weight = jnp.where(down_face, (0.5 * courant) * (conduct + under), 0.0)
    side_weight = jnp.where(side_face, (0.5 * courant) * (conduct + beside), 0.0)

    def steps(field):
        return below(field) - field, rightward(field) - field

    def advanced(field, down_step, side_step):
        down_flux = down_weight * down_step
        side_flux = side_weight * side_step
        return field + ((down_flux - above(down_flux)) + (side_flux - leftward(side_flux)))

    depth_steps = []
    for section in range(STEPS):
        depth_steps.append(steps(depth))
        if section < STEPS - 1:
            depth = advanced(depth, *depth_steps[-1])
    down_total = jnp.zeros((rows, columns), jnp.float32)
    side_total = jnp.zeros((rows, columns), jnp.float32)
    for section in reversed(range(STEPS)):
        down_step, side_step = steps(adjoint)
        down_total = down_total + depth_steps[section][0] * down_step
        side_total = side_total + depth_steps[section][1] * side_step
        adjoint = advanced(adjoint, down_step, side_step)
    down_total = jnp.where(down_face, down_total, 0.0)
    side_total = jnp.where(side_face, side_total, 0.0)
    total = (down_total + above(down_total)) + (side_total + leftward(side_total))
    own = slice(HALO, rows - HALO)
    grad_ref[...] = ((0.5 * courant) * conduct * total)[own]
    adjoint_ref[...] = adjoint[own]


def window(depth, rough, seed, chip, away):
    shape = jax.ShapeDtypeStruct(depth.shape, jnp.float32)
    return pl.pallas_call(
        window_kernel,
        out_shape=(shape, shape),
        in_specs=[VMEM] * 5,
        out_specs=(VMEM, VMEM),
        compiler_params=ROOMY,
        name="adjoint_window",
    )(depth, rough, seed, chip, away)


def halves(x):
    upper = x.astype(jnp.bfloat16).astype(jnp.float32)
    return upper, x - upper


HOME_ROWS = 8


def zone_sums(rows):
    left = []
    right = []
    for device, lane, *values in rows:
        left.append(one_hot(spread_rows(device), 256))
        weights = [spread_rows(part) for part in values]
        right.append(jnp.concatenate(one_hot(spread_rows(lane), LANES, weights), axis=0))
    both = lax.dot_general(
        jnp.concatenate(left, axis=1),
        jnp.concatenate(right, axis=1),
        (((1,), (1,)), ((), ())),
        preferred_element_type=jnp.float32,
    )
    return jnp.concatenate(
        [
            both[:, 0:LANES] + both[:, LANES : 2 * LANES],
            both[:, 2 * LANES : 3 * LANES] + both[:, 3 * LANES :],
        ],
        axis=1,
    )


def pair_rows(upper, lower):
    width = upper.shape[1]
    pair = [jnp.broadcast_to(part, (8, width)) for part in (upper, lower)]
    return jnp.concatenate(pair, axis=0).astype(jnp.bfloat16)


def zone_kernel(
    grad_ref,
    label_ref,
    moves_ref,
    device_ref,
    lane_ref,
    home_ref,
    own_ref,
    other_ref,
    total_ref,
    stray_ref,
    cell_ref,
):
    offset = label_ref[...] - own_first_zone()
    grad = grad_ref[...]
    cell_ref[0] = (offset >> 3).astype(jnp.float32)
    cell_ref[1] = (offset & 7).astype(jnp.float32)
    cell_ref[2], cell_ref[3] = halves(grad)
    cell_ref[4], cell_ref[5] = halves(grad * grad)
    grad = stacked(grad)
    moves = moves_ref[...]
    bit = 0
    while 2**bit < grad.shape[0]:
        grad = jnp.where((moves & 2**bit) != 0, from_below(grad, 2**bit), grad)
        bit += 1
    stray_ref[0], stray_ref[1] = halves(grad)
    stray_ref[2], stray_ref[3] = halves(grad * grad)
    zero = jnp.zeros((), jnp.bfloat16)
    width = grad_ref.shape[1]
    ids = lax.broadcasted_iota(jnp.int32, (16, width), 0)
    group_ids = ids.astype(jnp.float32).astype(jnp.bfloat16)
    within_ids = (ids & 7).astype(jnp.float32).astype(jnp.bfloat16)

    def home_rows(index):
        left = []
        right = []
        for step in range(HOME_ROWS):
            row = pl.ds(index * HOME_ROWS + step, 1)
            group_hit = spread_rows(cell_ref[0, row, :]) == group_ids
            within_hit = spread_rows(cell_ref[1, row, :]) == within_ids
            left.append(jnp.where(group_hit, jnp.ones((), jnp.bfloat16), zero))
            weights = [
                pair_rows(cell_ref[2 + part, row, :], cell_ref[3 + part, row, :])
                for part in (0, 2)
            ]
            right.append(
                jnp.concatenate([jnp.where(within_hit, w, zero) for w in weights], axis=0)
            )
        return lax.dot_general(
            jnp.concatenate(left, axis=1),
            jnp.concatenate(right, axis=1),
            (((1,), (1,)), ((), ())),
            preferred_element_type=jnp.float32,
        )

    home = home_rows(0)
    for index in range(1, grad_ref.shape[0] // HOME_ROWS):
        home = home + home_rows(index)
    part = lax.broadcasted_iota(jnp.int32, (32, 2 * LANES), 0)
    zone = lax.broadcasted_iota(jnp.int32, (32, 2 * LANES), 1)
    chosen = ((part & 7) == (zone & 7)) & ((part >= 16) == (zone >= LANES))
    home = jnp.dot(
        home,
        jnp.where(chosen, 1.0, 0.0),
        precision=lax.Precision.HIGHEST,
        preferred_element_type=jnp.float32,
    )
    group = lax.broadcasted_iota(jnp.int32, (16, 2 * LANES), 0)
    zone = lax.broadcasted_iota(jnp.int32, (16, 2 * LANES), 1)
    home = jnp.sum(jnp.where(((zone >> 3) & 15) == group, home, 0.0), axis=0, keepdims=True)
    home = halves(home[:, :LANES]) + halves(home[:, LANES:])

    def stray_rows(start, count):
        rows = [pl.ds(start + step, 1) for step in range(count)]
        return [
            (device_ref[row, :], lane_ref[row, :], *(stray_ref[i, row, :] for i in range(4)))
            for row in rows
        ]

    total_ref[...] = zone_sums(
        stray_rows(0, BASE_ROWS) + [(home_ref[0:1, :], home_ref[1:2, :], *home)]
    )

    def one_chunk(index, carry):
        total_ref[...] += zone_sums(stray_rows(BASE_ROWS + index * CHUNK, CHUNK))
        return carry

    chunks = jnp.max(home_ref[2:3, :]).astype(jnp.int32)
    lax.fori_loop(0, chunks, one_chunk, 0)
    own_ref[...] = total_ref[0:LANES, :]
    other_ref[...] = total_ref[LANES:, :]


def zone_partials(grad, label, moves, device, lane, home):
    half = jax.ShapeDtypeStruct((LANES, 2 * LANES), jnp.float32)
    return pl.pallas_call(
        zone_kernel,
        out_shape=(half, half),
        in_specs=[VMEM] * 6,
        out_specs=(VMEM,) * 2,
        scratch_shapes=[
            pltpu.VMEM((256, 2 * LANES), jnp.float32),
            pltpu.VMEM((4, grad.size // LANES, LANES), jnp.float32),
            pltpu.VMEM((6,) + grad.shape, jnp.float32),
        ],
        compiler_params=ROOMY,
        name="zone_partials",
    )(grad, label, moves, device, lane, home)


def parcel_kernel(own_ref, other_ref, edge_ref, out_ref):
    chips = own_ref.shape[0]
    sums = own_ref[...] + other_ref[...]
    out_ref[pl.ds(0, chips, stride=4), :] = sums[:, :LANES]
    out_ref[pl.ds(1, chips, stride=4), :] = sums[:, LANES:]
    for part in range(2):
        edge = jnp.broadcast_to(edge_ref[part : part + 1, :], (chips, LANES))
        out_ref[pl.ds(2 + part, chips, stride=4), :] = edge


def parcels(own, other, edge):
    return pl.pallas_call(
        parcel_kernel,
        out_shape=jax.ShapeDtypeStruct((4 * own.shape[0], LANES), jnp.float32),
        in_specs=[VMEM] * 3,
        out_specs=VMEM,
        compiler_params=ROOMY,
        name="parcels",
    )(own, other, edge)


def result_kernel(arrived_ref, rate_ref, push_ref, grad_ref, curve_ref, reach_ref):
    rows = arrived_ref.shape[0]
    sums = arrived_ref[0:8, :]
    for start in range(8, rows, 8):
        sums = sums + arrived_ref[start : start + 8, :]
    grad_ref[...] = (sums[0:1, :] + sums[4:5, :])[:, :SPAN]
    curve_ref[...] = (sums[1:2, :] + sums[5:6, :])[:, :SPAN]
    basin, chip = lax.axis_index("basin"), lax.axis_index("chip")
    basins, chips = lax.axis_size("basin"), lax.axis_size("chip")
    incoming = jnp.zeros((1, LANES), jnp.float32)
    for hop in reversed(range(1, basins)):
        there = jnp.where(basin + hop < basins, 1.0, 0.0)
        row = 4 * (jnp.minimum(basin + hop, basins - 1) * chips + chip)
        rate = arrived_ref[pl.ds(row + 2, 1), :]
        push = arrived_ref[pl.ds(row + 3, 1), :]
        incoming = there * (rate * incoming + push)
    reach_ref[...] = rate_ref[...] * incoming + push_ref[...]


def results(arrived, rate, push):
    zone = jax.ShapeDtypeStruct((1, SPAN), jnp.float32)
    return pl.pallas_call(
        result_kernel,
        out_shape=(zone, zone, jax.ShapeDtypeStruct(rate.shape, jnp.float32)),
        in_specs=[VMEM] * 3,
        out_specs=(VMEM,) * 3,
        compiler_params=ROOMY,
        name="results",
    )(arrived, rate, push)


def reach_kernel(adjoint_ref, cell_ref, keep_ref, forcing_ref, rate_ref, push_ref, edge_ref):
    rows, columns = adjoint_ref.shape
    upper, lower = halves(adjoint_ref[...])
    table = jnp.concatenate([upper, lower], axis=0).astype(jnp.bfloat16)
    reaches = cell_ref.shape[0]
    width = cell_ref.shape[1]
    values = []
    for reach in range(0, reaches, 4):
        cells = jnp.concatenate([cell_ref[reach + i : reach + i + 1, :] for i in range(4)], axis=1)
        column = (cells & (columns - 1)).astype(jnp.float32)
        hot = jnp.concatenate(
            [one_hot(spread_rows(column - part * 256.0), 256) for part in range(columns // 256)],
            axis=0,
        )
        picked = jnp.dot(table, hot, preferred_element_type=jnp.float32)
        picked = picked[:rows] + picked[rows:]
        row_hit = (cells >> 9) == lax.broadcasted_iota(jnp.int32, (rows, 4 * width), 0)
        found = jnp.sum(jnp.where(row_hit, picked, 0.0), axis=0, keepdims=True)
        values += [found[:, i * width : (i + 1) * width] for i in range(4)]
    rate = jnp.ones((1, width), jnp.float32)
    push = jnp.zeros((1, width), jnp.float32)
    for reach in reversed(range(reaches)):
        keep = keep_ref[reach : reach + 1, :]
        push = keep * push + (forcing_ref[reach : reach + 1, :] + levee_gain * values[reach])
        rate = keep * rate
        rate_ref[reach : reach + 1, :] = rate
        push_ref[reach : reach + 1, :] = push
    edge_ref[0:1, :] = rate
    edge_ref[1:2, :] = push


def reach_maps(adjoint, cells, keep, forcing):
    shape = jax.ShapeDtypeStruct(cells.shape, jnp.float32)
    return pl.pallas_call(
        reach_kernel,
        out_shape=(shape, shape, jax.ShapeDtypeStruct((2, cells.shape[1]), jnp.float32)),
        in_specs=[VMEM] * 4,
        out_specs=(VMEM, VMEM, VMEM),
        compiler_params=ROOMY,
        name="reach_maps",
    )(adjoint, cells, keep, forcing)


def swapped(value):
    return lax.ppermute(value, "core", [(0, 1), (1, 0)])


def exchanged_away(value):
    chips, cores = lax.axis_size("chip"), lax.axis_size("core")
    edges = [(i, i + 1) for i in range(1, chips * cores - 1, 2)]
    return lax.ppermute(value, ("chip", "core"), edges + [(j, i) for i, j in edges])


def per_device(
    depth_start, roughness, depth_seed, zone_label, owner_slot, retention, forcing, levee_cell
):
    depth, rough, seed, label, owner_slot, to_chip, to_away = fetched(
        depth_start[0],
        roughness[0],
        depth_seed[0],
        zone_label[0],
        owner_slot.reshape(-1, LANES),
    )
    from_away = exchanged_away(to_away)
    from_chip = swapped(to_chip)
    moves, device, lane, home = slots_of(owner_slot, label)
    grad, adjoint = window(depth, rough, seed, from_chip, from_away)
    own, other = zone_partials(grad, label, moves, device, lane, home)
    other = swapped(other)
    rate, push, edge = reach_maps(adjoint, levee_cell, retention, forcing)
    sent = parcels(own, other, edge).reshape(-1, 4, LANES)
    arrived = lax.all_to_all(sent, ("basin", "chip"), 0, 0, tiled=True)
    grad, curve, reach_adjoint = results(arrived.reshape(-1, LANES), rate, push)
    return (grad.reshape(-1), curve.reshape(-1), reach_adjoint)


def solution(mesh):
    basins, tiles = mesh.devices.shape
    fine = jax.sharding.Mesh(
        mesh.devices.reshape(basins, tiles // 2, 2), ("basin", "chip", "core")
    )
    tile = ("chip", "core")
    cells = P("basin", tile, None)
    reaches = P("basin", tile)
    zones = P(("basin", "chip", "core"))
    return jax.shard_map(
        per_device,
        mesh=fine,
        in_specs=(cells, cells, cells, cells, P(), reaches, reaches, reaches),
        out_specs=(zones, zones, reaches),
        check_vma=False,
    )
```

```python
import functools

import jax
import jax.numpy as jnp
from jax import lax
from jax.experimental import pallas as pl
from jax.experimental.pallas import tpu as pltpu
from jax.sharding import PartitionSpec as P

STEPS = 4
HALO = STEPS
SPAN = 127
LANES = 128

courant = 0.24
rough_ref = 0.025
levee_gain = 0.1

VMEM = pl.BlockSpec(memory_space=pltpu.VMEM)
ROOMY = pltpu.CompilerParams(vmem_limit_bytes=48 * 2**20)


def iota_bf16(shape, offset=0):
    ids = lax.broadcasted_iota(jnp.int32, shape, len(shape) - 2)
    if len(shape) == 3:
        ids = ids + shape[1] * lax.broadcasted_iota(jnp.int32, shape, 0)
    return (ids + offset).astype(jnp.float32).astype(jnp.bfloat16)


def spread_rows(row):
    return jnp.broadcast_to(row, (16, row.shape[1])).astype(jnp.bfloat16)


def one_hot(spread, count, weights=None):
    width = spread.shape[1]
    ids = iota_bf16((count // 16, 16, width))
    hit = spread[None] == ids
    zero = jnp.zeros((), jnp.bfloat16)
    if weights is None:
        return jnp.where(hit, jnp.ones((), jnp.bfloat16), zero).reshape(count, width)
    return [jnp.where(hit, w[None], zero).reshape(count, width) for w in weights]


def stacked(x):
    return jnp.concatenate(
        [x[:, start : start + LANES] for start in range(0, x.shape[1], LANES)], axis=0
    )


def from_below(x, distance):
    return pltpu.roll(x, x.shape[0] - distance, 0)


HBM = pl.BlockSpec(memory_space=pltpu.HBM)


FETCH = pltpu.CompilerParams(vmem_limit_bytes=55800000)


def front_kernel(*refs):
    count = (len(refs) - 3) // 2
    sources, kept = refs[:count], refs[count : 2 * count]
    chip_ref, away_ref, arrived = refs[2 * count :]
    copies = [
        pltpu.make_async_copy(source, place, arrived.at[index])
        for index, (source, place) in enumerate(zip(sources, kept))
    ]
    for copy in copies:
        copy.start()
    first_core = lax.axis_index("core") == 0
    for part in range(3):
        copies[part].wait()
        ref = kept[part]
        rows = slice(part * HALO, (part + 1) * HALO)
        top = ref[0:HALO, :]
        bottom = ref[ref.shape[0] - HALO :, :]
        chip_ref[rows, :] = jnp.where(first_core, bottom, top)
        away_ref[rows, :] = jnp.where(first_core, top, bottom)
    for copy in copies[3:]:
        copy.wait()


def fetched(*arrays):
    edge = jax.ShapeDtypeStruct((3 * HALO, arrays[0].shape[1]), jnp.float32)
    kept = tuple(jax.ShapeDtypeStruct(x.shape, x.dtype) for x in arrays)
    return pl.pallas_call(
        front_kernel,
        out_shape=kept + (edge, edge),
        in_specs=[HBM] * len(arrays),
        out_specs=(VMEM,) * (len(arrays) + 2),
        scratch_shapes=[pltpu.SemaphoreType.DMA((len(arrays),))],
        compiler_params=FETCH,
        name="fetch_and_edges",
    )(*arrays)


ABSENT = 2**15 - 1


def own_first_zone():
    chip = lax.axis_index("basin") * lax.axis_size("chip") + lax.axis_index("chip")
    return (chip * lax.axis_size("core") + lax.axis_index("core")) * SPAN


BASE_ROWS = 48
CHUNK = 8


def slot_kernel(
    owner_ref,
    label_ref,
    moves_ref,
    device_ref,
    lane_ref,
    home_ref,
    table_ref,
    turned_ref,
    packed_ref,
):
    first_zone = own_first_zone()
    core = lax.axis_index("core").astype(jnp.float32)
    table_ref[...] = jnp.full(table_ref.shape, 256.0 * SPAN, jnp.float32)
    table_ref[0 : owner_ref.shape[0], :] = owner_ref[...].astype(jnp.float32)

    def placed(slots):
        owners = jnp.floor((slots + 0.5) * (1.0 / SPAN))
        lanes = slots - owners * SPAN
        chips = jnp.floor(owners * 0.5)
        swapped = jnp.abs((owners - 2.0 * chips) - core)
        return jnp.where(owners < 256.0, chips + 128.0 * swapped, 256.0), lanes

    owners, lanes = placed(jnp.transpose(table_ref[...]))
    turned_ref[:, 0:256] = (owners * LANES).astype(jnp.bfloat16)
    turned_ref[:, 256:512] = lanes.astype(jnp.bfloat16)

    home_row = first_zone // LANES
    shift = first_zone % LANES
    back = jnp.where(shift == 0, 0, LANES - shift)
    pair = table_ref[pl.ds(home_row, 1), :], table_ref[pl.ds(home_row + 1, 1), :]
    pair = [pltpu.roll(jnp.broadcast_to(row, (8, LANES)), back, 1) for row in pair]
    spot = lax.broadcasted_iota(jnp.int32, (8, LANES), 1)
    home = jnp.where(spot + shift < LANES, pair[0], pair[1])
    home_device, home_lane = placed(jnp.where(spot < SPAN, home, 256.0 * SPAN))
    home_ref[0:1, :] = home_device[0:1]
    home_ref[1:2, :] = home_lane[0:1]

    label = stacked(label_ref[...])
    count = label.shape[0]
    offset = label - first_zone
    at_home = (offset >= 0) & (offset < SPAN)
    at_home_count = jnp.where(at_home, 1.0, 0.0)
    row_ids = lax.broadcasted_iota(jnp.int32, (count, count), 0)
    column_ids = lax.broadcasted_iota(jnp.int32, (count, count), 1)
    earlier = jnp.where(column_ids < row_ids, 1.0, 0.0).astype(jnp.bfloat16)
    gaps = jnp.dot(
        earlier, at_home_count.astype(jnp.bfloat16), preferred_element_type=jnp.float32
    ).astype(jnp.int32)
    packed = jnp.where(at_home, ABSENT, gaps * (ABSENT + 1) + label)
    moves = jnp.zeros(packed.shape, jnp.int32)
    bit = 0
    while 2**bit < count:
        marker = (ABSENT + 1) * 2**bit
        near = from_below(packed, 2**bit)
        taken = (near & marker) != 0
        left = (packed & marker) != 0
        packed = jnp.where(taken, near, jnp.where(left, ABSENT, packed))
        moves = jnp.where(taken, moves + 2**bit, moves)
        bit += 1
    moves_ref[...] = moves
    packed_ref[...] = packed & ABSENT
    most = count - jnp.min(jnp.sum(at_home_count, axis=0, keepdims=True)).astype(jnp.int32)
    chunks = jnp.maximum((most - BASE_ROWS + CHUNK - 1) // CHUNK, 0)
    home_ref[2:3, :] = jnp.full((1, LANES), chunks.astype(jnp.float32))

    def look_up(first, rows):
        for start in range(0, rows, 4):
            places = [pl.ds(first + start + i, 1) for i in range(4)]
            group_label = jnp.concatenate([packed_ref[place, :] for place in places], axis=1)
            width = group_label.shape[1]
            group = one_hot(spread_rows((group_label >> 7).astype(jnp.float32)), 256)
            found = jnp.dot(
                turned_ref[...],
                jnp.concatenate([group, group], axis=0),
                preferred_element_type=jnp.float32,
            )
            hit = (group_label & 127) == lax.broadcasted_iota(jnp.int32, (LANES, width), 0)
            slot = jnp.sum(jnp.where(hit, found, 0.0), axis=0, keepdims=True)
            owner = jnp.floor(slot * (1.0 / LANES))
            lane = slot - owner * LANES
            for i, place in enumerate(places):
                device_ref[place, :] = owner[:, i * LANES : (i + 1) * LANES]
                lane_ref[place, :] = lane[:, i * LANES : (i + 1) * LANES]

    def one_chunk(index, carry):
        look_up(BASE_ROWS + index * CHUNK, CHUNK)
        return carry

    look_up(0, BASE_ROWS)
    lax.fori_loop(0, chunks, one_chunk, 0)


def slots_of(owner_slot, label):
    count = label.size // LANES
    stack = jax.ShapeDtypeStruct((count, LANES), jnp.float32)
    return pl.pallas_call(
        slot_kernel,
        out_shape=(
            jax.ShapeDtypeStruct((count, LANES), jnp.int32),
            stack,
            stack,
            jax.ShapeDtypeStruct((8, LANES), jnp.float32),
        ),
        in_specs=[VMEM, VMEM],
        out_specs=(VMEM,) * 4,
        scratch_shapes=[
            pltpu.VMEM((256, LANES), jnp.float32),
            pltpu.VMEM((LANES, 512), jnp.bfloat16),
            pltpu.VMEM((count, LANES), jnp.int32),
        ],
        compiler_params=ROOMY,
        cost_estimate=pl.CostEstimate(
            flops=2 * 256 * 256 * label.size // 4, bytes_accessed=16 * label.size, transcendentals=0
        ),
        name="slot_lookup",
    )(owner_slot, label)


def below(x):
    return pltpu.roll(x, x.shape[0] - 1, 0)


def above(x):
    return pltpu.roll(x, 1, 0)


def rightward(x):
    return pltpu.roll(x, x.shape[1] - 1, 1)


def leftward(x):
    return pltpu.roll(x, 1, 1)


def window(depth, rough, adjoint):
    rows, columns = depth.shape
    conduct = jnp.where(rough > 0, rough_ref / jnp.where(rough > 0, rough, 1.0), 0.0)
    not_last = lax.broadcasted_iota(jnp.int32, (rows, columns), 1) < columns - 1
    under = below(conduct)
    beside = rightward(conduct)
    down_face = (conduct > 0) & (under > 0)
    side_face = (conduct > 0) & (beside > 0) & not_last
    down_weight = jnp.where(down_face, (0.5 * courant) * (conduct + under), 0.0)
    side_weight = jnp.where(side_face, (0.5 * courant) * (conduct + beside), 0.0)

    def steps(field):
        return below(field) - field, rightward(field) - field

    def advanced(field, down_step, side_step):
        down_flux = down_weight * down_step
        side_flux = side_weight * side_step
        return field + ((down_flux - above(down_flux)) + (side_flux - leftward(side_flux)))

    depth_steps = []
    for section in range(STEPS):
        depth_steps.append(steps(depth))
        if section < STEPS - 1:
            depth = advanced(depth, *depth_steps[-1])
    down_total = jnp.zeros((rows, columns), jnp.float32)
    side_total = jnp.zeros((rows, columns), jnp.float32)
    for section in reversed(range(STEPS)):
        down_step, side_step = steps(adjoint)
        down_total = down_total + depth_steps[section][0] * down_step
        side_total = side_total + depth_steps[section][1] * side_step
        adjoint = advanced(adjoint, down_step, side_step)
    down_total = jnp.where(down_face, down_total, 0.0)
    side_total = jnp.where(side_face, side_total, 0.0)
    total = (down_total + above(down_total)) + (side_total + leftward(side_total))
    return (0.5 * courant) * conduct * total, adjoint


def halves(x):
    upper = x.astype(jnp.bfloat16).astype(jnp.float32)
    return upper, x - upper


HOME_ROWS = 16


def zone_sums(rows):
    left = []
    right = []
    for device, lane, *values in rows:
        left.append(one_hot(spread_rows(device), 256))
        weights = [spread_rows(part) for part in values]
        right.append(jnp.concatenate(one_hot(spread_rows(lane), LANES, weights), axis=0))
    both = lax.dot_general(
        jnp.concatenate(left, axis=1),
        jnp.concatenate(right, axis=1),
        (((1,), (1,)), ((), ())),
        preferred_element_type=jnp.float32,
    )
    return jnp.concatenate(
        [
            both[:, 0:LANES] + both[:, LANES : 2 * LANES],
            both[:, 2 * LANES : 3 * LANES] + both[:, 3 * LANES :],
        ],
        axis=1,
    )


def pair_rows(upper, lower):
    width = upper.shape[1]
    pair = [jnp.broadcast_to(part, (8, width)) for part in (upper, lower)]
    return jnp.concatenate(pair, axis=0).astype(jnp.bfloat16)


def set_cells(cell_ref, offset, grad):
    cell_ref[0] = (offset >> 3).astype(jnp.float32)
    cell_ref[1] = (offset & 7).astype(jnp.float32)
    cell_ref[2], cell_ref[3] = halves(grad)
    cell_ref[4], cell_ref[5] = halves(grad * grad)


def home_products(cell_ref, first, count):
    zero = jnp.zeros((), jnp.bfloat16)
    width = cell_ref.shape[2]
    ids = lax.broadcasted_iota(jnp.int32, (16, width), 0)
    group_ids = ids.astype(jnp.float32).astype(jnp.bfloat16)
    within_ids = (ids & 7).astype(jnp.float32).astype(jnp.bfloat16)
    left = []
    right = []
    for step in range(count):
        row = slice(first + step, first + step + 1)
        group_hit = spread_rows(cell_ref[0, row, :]) == group_ids
        within_hit = spread_rows(cell_ref[1, row, :]) == within_ids
        left.append(jnp.where(group_hit, jnp.ones((), jnp.bfloat16), zero))
        weights = [
            pair_rows(cell_ref[2 + part, row, :], cell_ref[3 + part, row, :]) for part in (0, 2)
        ]
        right.append(jnp.concatenate([jnp.where(within_hit, w, zero) for w in weights], axis=0))
    return lax.dot_general(
        jnp.concatenate(left, axis=1),
        jnp.concatenate(right, axis=1),
        (((1,), (1,)), ((), ())),
        preferred_element_type=jnp.float32,
    )


RIM = 2 * HALO


def inner_kernel(
    depth_ref, rough_ref_, seed_ref, label_ref, grad_ref, adjoint_ref, home_ref, cell_ref
):
    grad, adjoint = window(depth_ref[...], rough_ref_[...], seed_ref[...])
    grad_ref[...] = grad
    adjoint_ref[...] = adjoint
    rows = grad.shape[0]
    inside = slice(RIM, rows - RIM)
    set_cells(cell_ref, (label_ref[...] - own_first_zone())[inside], grad[inside])
    home = home_products(cell_ref, 0, HOME_ROWS)
    for first in range(HOME_ROWS, rows - 2 * RIM, HOME_ROWS):
        home = home + home_products(cell_ref, first, HOME_ROWS)
    home_ref[...] = home


def inner_part(depth, rough, seed, label):
    shape = jax.ShapeDtypeStruct(depth.shape, jnp.float32)
    return pl.pallas_call(
        inner_kernel,
        out_shape=(shape, shape, jax.ShapeDtypeStruct((16, 32), jnp.float32)),
        in_specs=[VMEM] * 4,
        out_specs=(VMEM,) * 3,
        scratch_shapes=[pltpu.VMEM((6, depth.shape[0] - 2 * RIM, depth.shape[1]), jnp.float32)],
        compiler_params=ROOMY,
        cost_estimate=pl.CostEstimate(
            flops=2 * 256 * 64 * depth.size, bytes_accessed=20 * depth.size, transcendentals=0
        ),
        name="inner_rows",
    )(depth, rough, seed, label)


def zone_kernel(
    depth_ref,
    rough_ref_,
    seed_ref,
    chip_ref,
    away_ref,
    inner_grad_ref,
    inner_adjoint_ref,
    inner_home_ref,
    label_ref,
    moves_ref,
    device_ref,
    lane_ref,
    home_ref,
    own_ref,
    other_ref,
    adjoint_ref,
    total_ref,
    stray_ref,
    cell_ref,
):
    first_core = lax.axis_index("core") == 0
    rows = depth_ref.shape[0]
    near = RIM + HALO

    def rim(part, ref):
        halo = slice(part * HALO, (part + 1) * HALO)
        chip, away = chip_ref[halo, :], away_ref[halo, :]
        low = jnp.where(first_core, away, chip)
        high = jnp.where(first_core, chip, away)
        return jnp.concatenate([low, ref[0:near, :], ref[rows - near : rows, :], high], axis=0)

    rim_grad, rim_adjoint = window(rim(0, depth_ref), rim(1, rough_ref_), rim(2, seed_ref))
    top = slice(HALO, HALO + RIM)
    bottom = slice(near + 2 * HALO, near + 2 * HALO + RIM)
    inside = slice(RIM, rows - RIM)
    adjoint_ref[...] = jnp.concatenate(
        [rim_adjoint[top], inner_adjoint_ref[inside, :], rim_adjoint[bottom]], axis=0
    )
    offset = label_ref[...] - own_first_zone()
    set_cells(
        cell_ref,
        jnp.concatenate([offset[:RIM], offset[rows - RIM :]], axis=0),
        jnp.concatenate([rim_grad[top], rim_grad[bottom]], axis=0),
    )
    grad = jnp.concatenate(
        [rim_grad[top], inner_grad_ref[inside, :], rim_grad[bottom]], axis=0
    )
    grad = stacked(grad)
    moves = moves_ref[...]
    bit = 0
    while 2**bit < grad.shape[0]:
        grad = jnp.where((moves & 2**bit) != 0, from_below(grad, 2**bit), grad)
        bit += 1
    stray_ref[0], stray_ref[1] = halves(grad)
    stray_ref[2], stray_ref[3] = halves(grad * grad)
    home = inner_home_ref[...] + home_products(cell_ref, 0, 2 * RIM)
    part = lax.broadcasted_iota(jnp.int32, (32, 2 * LANES), 0)
    zone = lax.broadcasted_iota(jnp.int32, (32, 2 * LANES), 1)
    chosen = ((part & 7) == (zone & 7)) & ((part >= 16) == (zone >= LANES))
    home = jnp.dot(
        home,
        jnp.where(chosen, 1.0, 0.0),
        precision=lax.Precision.HIGHEST,
        preferred_element_type=jnp.float32,
    )
    group = lax.broadcasted_iota(jnp.int32, (16, 2 * LANES), 0)
    zone = lax.broadcasted_iota(jnp.int32, (16, 2 * LANES), 1)
    home = jnp.sum(jnp.where(((zone >> 3) & 15) == group, home, 0.0), axis=0, keepdims=True)
    home = halves(home[:, :LANES]) + halves(home[:, LANES:])

    def stray_rows(start, count):
        rows = [pl.ds(start + step, 1) for step in range(count)]
        return [
            (device_ref[row, :], lane_ref[row, :], *(stray_ref[i, row, :] for i in range(4)))
            for row in rows
        ]

    total_ref[...] = zone_sums(
        stray_rows(0, BASE_ROWS) + [(home_ref[0:1, :], home_ref[1:2, :], *home)]
    )

    def one_chunk(index, carry):
        total_ref[...] += zone_sums(stray_rows(BASE_ROWS + index * CHUNK, CHUNK))
        return carry

    chunks = jnp.max(home_ref[2:3, :]).astype(jnp.int32)
    lax.fori_loop(0, chunks, one_chunk, 0)
    own_ref[...] = total_ref[0:LANES, :]
    other_ref[...] = total_ref[LANES:, :]


def zone_partials(depth, *others):
    half = jax.ShapeDtypeStruct((LANES, 2 * LANES), jnp.float32)
    return pl.pallas_call(
        zone_kernel,
        out_shape=(half, half, jax.ShapeDtypeStruct(depth.shape, jnp.float32)),
        in_specs=[VMEM] * (1 + len(others)),
        out_specs=(VMEM,) * 3,
        scratch_shapes=[
            pltpu.VMEM((256, 2 * LANES), jnp.float32),
            pltpu.VMEM((4, depth.size // LANES, LANES), jnp.float32),
            pltpu.VMEM((6, 2 * RIM, depth.shape[1]), jnp.float32),
        ],
        compiler_params=ROOMY,
        name="zone_partials",
    )(depth, *others)


def parcel_kernel(own_ref, other_ref, edge_ref, out_ref):
    chips = own_ref.shape[0]
    sums = own_ref[...] + other_ref[...]
    out_ref[pl.ds(0, chips, stride=4), :] = sums[:, :LANES]
    out_ref[pl.ds(1, chips, stride=4), :] = sums[:, LANES:]
    for part in range(2):
        edge = jnp.broadcast_to(edge_ref[part : part + 1, :], (chips, LANES))
        out_ref[pl.ds(2 + part, chips, stride=4), :] = edge


def parcels(own, other, edge):
    return pl.pallas_call(
        parcel_kernel,
        out_shape=jax.ShapeDtypeStruct((4 * own.shape[0], LANES), jnp.float32),
        in_specs=[VMEM] * 3,
        out_specs=VMEM,
        compiler_params=ROOMY,
        name="parcels",
    )(own, other, edge)


def result_kernel(arrived_ref, rate_ref, push_ref, grad_ref, curve_ref, reach_ref):
    rows = arrived_ref.shape[0]
    sums = arrived_ref[0:8, :]
    for start in range(8, rows, 8):
        sums = sums + arrived_ref[start : start + 8, :]
    grad_ref[...] = (sums[0:1, :] + sums[4:5, :])[:, :SPAN]
    curve_ref[...] = (sums[1:2, :] + sums[5:6, :])[:, :SPAN]
    basin, chip = lax.axis_index("basin"), lax.axis_index("chip")
    basins, chips = lax.axis_size("basin"), lax.axis_size("chip")
    incoming = jnp.zeros((1, LANES), jnp.float32)
    for hop in reversed(range(1, basins)):
        there = jnp.where(basin + hop < basins, 1.0, 0.0)
        row = 4 * (jnp.minimum(basin + hop, basins - 1) * chips + chip)
        rate = arrived_ref[pl.ds(row + 2, 1), :]
        push = arrived_ref[pl.ds(row + 3, 1), :]
        incoming = there * (rate * incoming + push)
    reach_ref[...] = rate_ref[...] * incoming + push_ref[...]


def results(arrived, rate, push):
    zone = jax.ShapeDtypeStruct((1, SPAN), jnp.float32)
    return pl.pallas_call(
        result_kernel,
        out_shape=(zone, zone, jax.ShapeDtypeStruct(rate.shape, jnp.float32)),
        in_specs=[VMEM] * 3,
        out_specs=(VMEM,) * 3,
        compiler_params=ROOMY,
        name="results",
    )(arrived, rate, push)


def reach_kernel(adjoint_ref, cell_ref, keep_ref, forcing_ref, rate_ref, push_ref, edge_ref):
    rows, columns = adjoint_ref.shape
    upper, lower = halves(adjoint_ref[...])
    table = jnp.concatenate([upper, lower], axis=0).astype(jnp.bfloat16)
    reaches = cell_ref.shape[0]
    width = cell_ref.shape[1]
    values = []
    for reach in range(0, reaches, 4):
        cells = jnp.concatenate([cell_ref[reach + i : reach + i + 1, :] for i in range(4)], axis=1)
        column = (cells & (columns - 1)).astype(jnp.float32)
        hot = jnp.concatenate(
            [one_hot(spread_rows(column - part * 256.0), 256) for part in range(columns // 256)],
            axis=0,
        )
        picked = jnp.dot(table, hot, preferred_element_type=jnp.float32)
        picked = picked[:rows] + picked[rows:]
        row_hit = (cells >> 9) == lax.broadcasted_iota(jnp.int32, (rows, 4 * width), 0)
        found = jnp.sum(jnp.where(row_hit, picked, 0.0), axis=0, keepdims=True)
        values += [found[:, i * width : (i + 1) * width] for i in range(4)]
    rate = jnp.ones((1, width), jnp.float32)
    push = jnp.zeros((1, width), jnp.float32)
    for reach in reversed(range(reaches)):
        keep = keep_ref[reach : reach + 1, :]
        push = keep * push + (forcing_ref[reach : reach + 1, :] + levee_gain * values[reach])
        rate = keep * rate
        rate_ref[reach : reach + 1, :] = rate
        push_ref[reach : reach + 1, :] = push
    edge_ref[0:1, :] = rate
    edge_ref[1:2, :] = push


def reach_maps(adjoint, cells, keep, forcing):
    shape = jax.ShapeDtypeStruct(cells.shape, jnp.float32)
    return pl.pallas_call(
        reach_kernel,
        out_shape=(shape, shape, jax.ShapeDtypeStruct((2, cells.shape[1]), jnp.float32)),
        in_specs=[VMEM] * 4,
        out_specs=(VMEM, VMEM, VMEM),
        compiler_params=ROOMY,
        name="reach_maps",
    )(adjoint, cells, keep, forcing)


def swapped(value):
    return lax.ppermute(value, "core", [(0, 1), (1, 0)])


def exchanged_away(value):
    chips, cores = lax.axis_size("chip"), lax.axis_size("core")
    edges = [(i, i + 1) for i in range(1, chips * cores - 1, 2)]
    return lax.ppermute(value, ("chip", "core"), edges + [(j, i) for i, j in edges])


def per_device(
    depth_start, roughness, depth_seed, zone_label, owner_slot, retention, forcing, levee_cell
):
    depth, rough, seed, label, owner_slot, to_chip, to_away = fetched(
        depth_start[0],
        roughness[0],
        depth_seed[0],
        zone_label[0],
        owner_slot.reshape(-1, LANES),
    )
    from_away = exchanged_away(to_away)
    from_chip = swapped(to_chip)
    moves, device, lane, home = slots_of(owner_slot, label)
    inner = inner_part(depth, rough, seed, label)
    own, other, adjoint = zone_partials(
        depth, rough, seed, from_chip, from_away, *inner, label, moves, device, lane, home
    )
    other = swapped(other)
    rate, push, edge = reach_maps(adjoint, levee_cell, retention, forcing)
    sent = parcels(own, other, edge).reshape(-1, 4, LANES)
    arrived = lax.all_to_all(sent, ("basin", "chip"), 0, 0, tiled=True)
    grad, curve, reach_adjoint = results(arrived.reshape(-1, LANES), rate, push)
    return (grad.reshape(-1), curve.reshape(-1), reach_adjoint)


def solution(mesh):
    basins, tiles = mesh.devices.shape
    fine = jax.sharding.Mesh(
        mesh.devices.reshape(basins, tiles // 2, 2), ("basin", "chip", "core")
    )
    tile = ("chip", "core")
    cells = P("basin", tile, None)
    reaches = P("basin", tile)
    zones = P(("basin", "chip", "core"))
    return jax.shard_map(
        per_device,
        mesh=fine,
        in_specs=(cells, cells, cells, cells, P(), reaches, reaches, reaches),
        out_specs=(zones, zones, reaches),
        check_vma=False,
    )
```

```python
import functools

import jax
import jax.numpy as jnp
from jax import lax
from jax.experimental import pallas as pl
from jax.experimental.pallas import tpu as pltpu
from jax.sharding import PartitionSpec as P

STEPS = 4
HALO = STEPS
SPAN = 127
LANES = 128

courant = 0.24
rough_ref = 0.025
levee_gain = 0.1

VMEM = pl.BlockSpec(memory_space=pltpu.VMEM)
ROOMY = pltpu.CompilerParams(vmem_limit_bytes=48 * 2**20)


def iota_bf16(shape, offset=0):
    ids = lax.broadcasted_iota(jnp.int32, shape, len(shape) - 2)
    if len(shape) == 3:
        ids = ids + shape[1] * lax.broadcasted_iota(jnp.int32, shape, 0)
    return (ids + offset).astype(jnp.float32).astype(jnp.bfloat16)


def spread_rows(row):
    return jnp.broadcast_to(row, (16, row.shape[1])).astype(jnp.bfloat16)


def one_hot(spread, count, weights=None):
    width = spread.shape[1]
    ids = iota_bf16((count // 16, 16, width))
    hit = spread[None] == ids
    zero = jnp.zeros((), jnp.bfloat16)
    if weights is None:
        return jnp.where(hit, jnp.ones((), jnp.bfloat16), zero).reshape(count, width)
    return [jnp.where(hit, w[None], zero).reshape(count, width) for w in weights]


def stacked(x):
    return jnp.concatenate(
        [x[:, start : start + LANES] for start in range(0, x.shape[1], LANES)], axis=0
    )


def from_below(x, distance):
    return pltpu.roll(x, x.shape[0] - distance, 0)


HBM = pl.BlockSpec(memory_space=pltpu.HBM)


FETCH = pltpu.CompilerParams(vmem_limit_bytes=55800000)


def front_kernel(*refs):
    count = (len(refs) - 3) // 2
    sources, kept = refs[:count], refs[count : 2 * count]
    chip_ref, away_ref, arrived = refs[2 * count :]
    copies = [
        pltpu.make_async_copy(source, place, arrived.at[index])
        for index, (source, place) in enumerate(zip(sources, kept))
    ]
    for copy in copies:
        copy.start()
    first_core = lax.axis_index("core") == 0
    for part in range(3):
        copies[part].wait()
        ref = kept[part]
        rows = slice(part * HALO, (part + 1) * HALO)
        top = ref[0:HALO, :]
        bottom = ref[ref.shape[0] - HALO :, :]
        chip_ref[rows, :] = jnp.where(first_core, bottom, top)
        away_ref[rows, :] = jnp.where(first_core, top, bottom)
    for copy in copies[3:]:
        copy.wait()


def fetched(*arrays):
    edge = jax.ShapeDtypeStruct((3 * HALO, arrays[0].shape[1]), jnp.float32)
    kept = tuple(jax.ShapeDtypeStruct(x.shape, x.dtype) for x in arrays)
    return pl.pallas_call(
        front_kernel,
        out_shape=kept + (edge, edge),
        in_specs=[HBM] * len(arrays),
        out_specs=(VMEM,) * (len(arrays) + 2),
        scratch_shapes=[pltpu.SemaphoreType.DMA((len(arrays),))],
        compiler_params=FETCH,
        name="fetch_and_edges",
    )(*arrays)


ABSENT = 2**15 - 1


def own_first_zone():
    chip = lax.axis_index("basin") * lax.axis_size("chip") + lax.axis_index("chip")
    return (chip * lax.axis_size("core") + lax.axis_index("core")) * SPAN


BASE_ROWS = 48
CHUNK = 8


def slot_kernel(
    owner_ref,
    label_ref,
    moves_ref,
    device_ref,
    lane_ref,
    home_ref,
    table_ref,
    turned_ref,
    packed_ref,
):
    first_zone = own_first_zone()
    core = lax.axis_index("core").astype(jnp.float32)
    table_ref[...] = jnp.full(table_ref.shape, 256.0 * SPAN, jnp.float32)
    table_ref[0 : owner_ref.shape[0], :] = owner_ref[...].astype(jnp.float32)

    def placed(slots):
        owners = jnp.floor((slots + 0.5) * (1.0 / SPAN))
        lanes = slots - owners * SPAN
        chips = jnp.floor(owners * 0.5)
        swapped = jnp.abs((owners - 2.0 * chips) - core)
        return jnp.where(owners < 256.0, chips + 128.0 * swapped, 256.0), lanes

    owners, lanes = placed(jnp.transpose(table_ref[...]))
    turned_ref[:, 0:256] = (owners * LANES).astype(jnp.bfloat16)
    turned_ref[:, 256:512] = lanes.astype(jnp.bfloat16)

    home_row = first_zone // LANES
    shift = first_zone % LANES
    back = jnp.where(shift == 0, 0, LANES - shift)
    pair = table_ref[pl.ds(home_row, 1), :], table_ref[pl.ds(home_row + 1, 1), :]
    pair = [pltpu.roll(jnp.broadcast_to(row, (8, LANES)), back, 1) for row in pair]
    spot = lax.broadcasted_iota(jnp.int32, (8, LANES), 1)
    home = jnp.where(spot + shift < LANES, pair[0], pair[1])
    home_device, home_lane = placed(jnp.where(spot < SPAN, home, 256.0 * SPAN))
    home_ref[0:1, :] = home_device[0:1]
    home_ref[1:2, :] = home_lane[0:1]

    label = stacked(label_ref[...])
    count = label.shape[0]
    offset = label - first_zone
    at_home = (offset >= 0) & (offset < SPAN)
    at_home_count = jnp.where(at_home, 1.0, 0.0)
    row_ids = lax.broadcasted_iota(jnp.int32, (count, count), 0)
    column_ids = lax.broadcasted_iota(jnp.int32, (count, count), 1)
    earlier = jnp.where(column_ids < row_ids, 1.0, 0.0).astype(jnp.bfloat16)
    gaps = jnp.dot(
        earlier, at_home_count.astype(jnp.bfloat16), preferred_element_type=jnp.float32
    ).astype(jnp.int32)
    packed = jnp.where(at_home, ABSENT, gaps * (ABSENT + 1) + label)
    moves = jnp.zeros(packed.shape, jnp.int32)
    bit = 0
    while 2**bit < count:
        marker = (ABSENT + 1) * 2**bit
        near = from_below(packed, 2**bit)
        taken = (near & marker) != 0
        left = (packed & marker) != 0
        packed = jnp.where(taken, near, jnp.where(left, ABSENT, packed))
        moves = jnp.where(taken, moves + 2**bit, moves)
        bit += 1
    moves_ref[...] = moves
    packed_ref[...] = packed & ABSENT
    most = count - jnp.min(jnp.sum(at_home_count, axis=0, keepdims=True)).astype(jnp.int32)
    chunks = jnp.maximum((most - BASE_ROWS + CHUNK - 1) // CHUNK, 0)
    home_ref[2:3, :] = jnp.full((1, LANES), chunks.astype(jnp.float32))

    def look_up(first, rows):
        for start in range(0, rows, 4):
            places = [pl.ds(first + start + i, 1) for i in range(4)]
            group_label = jnp.concatenate([packed_ref[place, :] for place in places], axis=1)
            width = group_label.shape[1]
            group = one_hot(spread_rows((group_label >> 7).astype(jnp.float32)), 256)
            found = jnp.dot(
                turned_ref[...],
                jnp.concatenate([group, group], axis=0),
                preferred_element_type=jnp.float32,
            )
            hit = (group_label & 127) == lax.broadcasted_iota(jnp.int32, (LANES, width), 0)
            slot = jnp.sum(jnp.where(hit, found, 0.0), axis=0, keepdims=True)
            owner = jnp.floor(slot * (1.0 / LANES))
            lane = slot - owner * LANES
            for i, place in enumerate(places):
                device_ref[place, :] = owner[:, i * LANES : (i + 1) * LANES]
                lane_ref[place, :] = lane[:, i * LANES : (i + 1) * LANES]

    def one_chunk(index, carry):
        look_up(BASE_ROWS + index * CHUNK, CHUNK)
        return carry

    look_up(0, BASE_ROWS)
    lax.fori_loop(0, chunks, one_chunk, 0)


def slots_of(owner_slot, label):
    count = label.size // LANES
    stack = jax.ShapeDtypeStruct((count, LANES), jnp.float32)
    return pl.pallas_call(
        slot_kernel,
        out_shape=(
            jax.ShapeDtypeStruct((count, LANES), jnp.int32),
            stack,
            stack,
            jax.ShapeDtypeStruct((8, LANES), jnp.float32),
        ),
        in_specs=[VMEM, VMEM],
        out_specs=(VMEM,) * 4,
        scratch_shapes=[
            pltpu.VMEM((256, LANES), jnp.float32),
            pltpu.VMEM((LANES, 512), jnp.bfloat16),
            pltpu.VMEM((count, LANES), jnp.int32),
        ],
        compiler_params=ROOMY,
        cost_estimate=pl.CostEstimate(
            flops=2 * 256 * 256 * label.size // 4, bytes_accessed=16 * label.size, transcendentals=0
        ),
        name="slot_lookup",
    )(owner_slot, label)


def below(x):
    return pltpu.roll(x, x.shape[0] - 1, 0)


def above(x):
    return pltpu.roll(x, 1, 0)


def rightward(x):
    return pltpu.roll(x, x.shape[1] - 1, 1)


def leftward(x):
    return pltpu.roll(x, 1, 1)


def window(depth, rough, adjoint):
    rows, columns = depth.shape
    conduct = jnp.where(rough > 0, rough_ref / jnp.where(rough > 0, rough, 1.0), 0.0)
    not_last = lax.broadcasted_iota(jnp.int32, (rows, columns), 1) < columns - 1
    under = below(conduct)
    beside = rightward(conduct)
    down_face = (conduct > 0) & (under > 0)
    side_face = (conduct > 0) & (beside > 0) & not_last
    down_weight = jnp.where(down_face, (0.5 * courant) * (conduct + under), 0.0)
    side_weight = jnp.where(side_face, (0.5 * courant) * (conduct + beside), 0.0)

    def steps(field):
        return below(field) - field, rightward(field) - field

    def advanced(field, down_step, side_step):
        down_flux = down_weight * down_step
        side_flux = side_weight * side_step
        return field + ((down_flux - above(down_flux)) + (side_flux - leftward(side_flux)))

    depth_steps = []
    for section in range(STEPS):
        depth_steps.append(steps(depth))
        if section < STEPS - 1:
            depth = advanced(depth, *depth_steps[-1])
    down_total = jnp.zeros((rows, columns), jnp.float32)
    side_total = jnp.zeros((rows, columns), jnp.float32)
    for section in reversed(range(STEPS)):
        down_step, side_step = steps(adjoint)
        down_total = down_total + depth_steps[section][0] * down_step
        side_total = side_total + depth_steps[section][1] * side_step
        adjoint = advanced(adjoint, down_step, side_step)
    down_total = jnp.where(down_face, down_total, 0.0)
    side_total = jnp.where(side_face, side_total, 0.0)
    total = (down_total + above(down_total)) + (side_total + leftward(side_total))
    return (0.5 * courant) * conduct * total, adjoint


def halves(x):
    upper = x.astype(jnp.bfloat16).astype(jnp.float32)
    return upper, x - upper


HOME_ROWS = 16


def zone_sums(rows):
    left = []
    right = []
    for device, lane, *values in rows:
        left.append(one_hot(spread_rows(device), 256))
        weights = [spread_rows(part) for part in values]
        right.append(jnp.concatenate(one_hot(spread_rows(lane), LANES, weights), axis=0))
    both = lax.dot_general(
        jnp.concatenate(left, axis=1),
        jnp.concatenate(right, axis=1),
        (((1,), (1,)), ((), ())),
        preferred_element_type=jnp.float32,
    )
    return jnp.concatenate(
        [
            both[:, 0:LANES] + both[:, LANES : 2 * LANES],
            both[:, 2 * LANES : 3 * LANES] + both[:, 3 * LANES :],
        ],
        axis=1,
    )


def pair_rows(upper, lower):
    width = upper.shape[1]
    pair = [jnp.broadcast_to(part, (8, width)) for part in (upper, lower)]
    return jnp.concatenate(pair, axis=0).astype(jnp.bfloat16)


def set_cells(cell_ref, offset, grad):
    cell_ref[0] = (offset >> 3).astype(jnp.float32)
    cell_ref[1] = (offset & 7).astype(jnp.float32)
    cell_ref[2], cell_ref[3] = halves(grad)
    cell_ref[4], cell_ref[5] = halves(grad * grad)


def home_products(cell_ref, first, count):
    zero = jnp.zeros((), jnp.bfloat16)
    width = cell_ref.shape[2]
    ids = lax.broadcasted_iota(jnp.int32, (16, width), 0)
    group_ids = ids.astype(jnp.float32).astype(jnp.bfloat16)
    within_ids = (ids & 7).astype(jnp.float32).astype(jnp.bfloat16)
    left = []
    right = []
    for step in range(count):
        row = slice(first + step, first + step + 1)
        group_hit = spread_rows(cell_ref[0, row, :]) == group_ids
        within_hit = spread_rows(cell_ref[1, row, :]) == within_ids
        left.append(jnp.where(group_hit, jnp.ones((), jnp.bfloat16), zero))
        weights = [
            pair_rows(cell_ref[2 + part, row, :], cell_ref[3 + part, row, :]) for part in (0, 2)
        ]
        right.append(jnp.concatenate([jnp.where(within_hit, w, zero) for w in weights], axis=0))
    return lax.dot_general(
        jnp.concatenate(left, axis=1),
        jnp.concatenate(right, axis=1),
        (((1,), (1,)), ((), ())),
        preferred_element_type=jnp.float32,
    )


RIM = 2 * HALO


def inner_kernel(
    depth_ref, rough_ref_, seed_ref, label_ref, grad_ref, adjoint_ref, home_ref, cell_ref
):
    grad, adjoint = window(depth_ref[...], rough_ref_[...], seed_ref[...])
    grad_ref[...] = grad
    adjoint_ref[...] = adjoint
    rows = grad.shape[0]
    inside = slice(RIM, rows - RIM)
    set_cells(cell_ref, (label_ref[...] - own_first_zone())[inside], grad[inside])
    home = home_products(cell_ref, 0, HOME_ROWS)
    for first in range(HOME_ROWS, rows - 2 * RIM, HOME_ROWS):
        home = home + home_products(cell_ref, first, HOME_ROWS)
    home_ref[...] = home


def inner_part(depth, rough, seed, label):
    shape = jax.ShapeDtypeStruct(depth.shape, jnp.float32)
    return pl.pallas_call(
        inner_kernel,
        out_shape=(shape, shape, jax.ShapeDtypeStruct((16, 32), jnp.float32)),
        in_specs=[VMEM] * 4,
        out_specs=(VMEM,) * 3,
        scratch_shapes=[pltpu.VMEM((6, depth.shape[0] - 2 * RIM, depth.shape[1]), jnp.float32)],
        compiler_params=ROOMY,
        cost_estimate=pl.CostEstimate(
            flops=2 * 256 * 64 * depth.size, bytes_accessed=20 * depth.size, transcendentals=0
        ),
        name="inner_rows",
    )(depth, rough, seed, label)


def zone_kernel(
    depth_ref,
    rough_ref_,
    seed_ref,
    chip_ref,
    away_ref,
    inner_grad_ref,
    inner_adjoint_ref,
    inner_home_ref,
    label_ref,
    moves_ref,
    device_ref,
    lane_ref,
    home_ref,
    own_ref,
    other_ref,
    adjoint_ref,
    total_ref,
    stray_ref,
    cell_ref,
):
    first_core = lax.axis_index("core") == 0
    chip_index, chips = lax.axis_index("chip"), lax.axis_size("chip")
    has_low = jnp.where(first_core & (chip_index == 0), 0.0, 1.0)
    has_high = jnp.where(first_core | (chip_index < chips - 1), 1.0, 0.0)
    rows = depth_ref.shape[0]
    near = RIM + HALO

    def rim(part, ref):
        halo = slice(part * HALO, (part + 1) * HALO)
        chip, away = chip_ref[halo, :], away_ref[halo, :]
        low = jnp.where(first_core, away, chip)
        high = jnp.where(first_core, chip, away)
        if part == 1:
            low, high = low * has_low, high * has_high
        return jnp.concatenate([low, ref[0:near, :], ref[rows - near : rows, :], high], axis=0)

    rim_grad, rim_adjoint = window(rim(0, depth_ref), rim(1, rough_ref_), rim(2, seed_ref))
    top = slice(HALO, HALO + RIM)
    bottom = slice(near + 2 * HALO, near + 2 * HALO + RIM)
    inside = slice(RIM, rows - RIM)
    adjoint_ref[...] = jnp.concatenate(
        [rim_adjoint[top], inner_adjoint_ref[inside, :], rim_adjoint[bottom]], axis=0
    )
    offset = label_ref[...] - own_first_zone()
    set_cells(
        cell_ref,
        jnp.concatenate([offset[:RIM], offset[rows - RIM :]], axis=0),
        jnp.concatenate([rim_grad[top], rim_grad[bottom]], axis=0),
    )
    grad = jnp.concatenate(
        [rim_grad[top], inner_grad_ref[inside, :], rim_grad[bottom]], axis=0
    )
    grad = stacked(grad)
    moves = moves_ref[...]
    bit = 0
    while 2**bit < grad.shape[0]:
        grad = jnp.where((moves & 2**bit) != 0, from_below(grad, 2**bit), grad)
        bit += 1
    stray_ref[0], stray_ref[1] = halves(grad)
    stray_ref[2], stray_ref[3] = halves(grad * grad)
    home = inner_home_ref[...] + home_products(cell_ref, 0, 2 * RIM)
    part = lax.broadcasted_iota(jnp.int32, (32, 2 * LANES), 0)
    zone = lax.broadcasted_iota(jnp.int32, (32, 2 * LANES), 1)
    chosen = ((part & 7) == (zone & 7)) & ((part >= 16) == (zone >= LANES))
    home = jnp.dot(
        home,
        jnp.where(chosen, 1.0, 0.0),
        precision=lax.Precision.HIGHEST,
        preferred_element_type=jnp.float32,
    )
    group = lax.broadcasted_iota(jnp.int32, (16, 2 * LANES), 0)
    zone = lax.broadcasted_iota(jnp.int32, (16, 2 * LANES), 1)
    home = jnp.sum(jnp.where(((zone >> 3) & 15) == group, home, 0.0), axis=0, keepdims=True)
    home = halves(home[:, :LANES]) + halves(home[:, LANES:])

    def stray_rows(start, count):
        rows = [pl.ds(start + step, 1) for step in range(count)]
        return [
            (device_ref[row, :], lane_ref[row, :], *(stray_ref[i, row, :] for i in range(4)))
            for row in rows
        ]

    total_ref[...] = zone_sums(
        stray_rows(0, BASE_ROWS) + [(home_ref[0:1, :], home_ref[1:2, :], *home)]
    )

    def one_chunk(index, carry):
        total_ref[...] += zone_sums(stray_rows(BASE_ROWS + index * CHUNK, CHUNK))
        return carry

    chunks = jnp.max(home_ref[2:3, :]).astype(jnp.int32)
    lax.fori_loop(0, chunks, one_chunk, 0)
    own_ref[...] = total_ref[0:LANES, :]
    other_ref[...] = total_ref[LANES:, :]


def zone_partials(depth, *others):
    half = jax.ShapeDtypeStruct((LANES, 2 * LANES), jnp.float32)
    return pl.pallas_call(
        zone_kernel,
        out_shape=(half, half, jax.ShapeDtypeStruct(depth.shape, jnp.float32)),
        in_specs=[VMEM] * (1 + len(others)),
        out_specs=(VMEM,) * 3,
        scratch_shapes=[
            pltpu.VMEM((256, 2 * LANES), jnp.float32),
            pltpu.VMEM((4, depth.size // LANES, LANES), jnp.float32),
            pltpu.VMEM((6, 2 * RIM, depth.shape[1]), jnp.float32),
        ],
        compiler_params=ROOMY,
        name="zone_partials",
    )(depth, *others)


def parcel_kernel(own_ref, other_ref, edge_ref, out_ref):
    chips = own_ref.shape[0]
    sums = own_ref[...] + other_ref[...]
    out_ref[pl.ds(0, chips, stride=4), :] = sums[:, :LANES]
    out_ref[pl.ds(1, chips, stride=4), :] = sums[:, LANES:]
    for part in range(2):
        edge = jnp.broadcast_to(edge_ref[part : part + 1, :], (chips, LANES))
        out_ref[pl.ds(2 + part, chips, stride=4), :] = edge


def parcels(own, other, edge):
    return pl.pallas_call(
        parcel_kernel,
        out_shape=jax.ShapeDtypeStruct((4 * own.shape[0], LANES), jnp.float32),
        in_specs=[VMEM] * 3,
        out_specs=VMEM,
        compiler_params=ROOMY,
        name="parcels",
    )(own, other, edge)


def result_kernel(arrived_ref, rate_ref, push_ref, grad_ref, curve_ref, reach_ref):
    rows = arrived_ref.shape[0]
    sums = arrived_ref[0:8, :]
    for start in range(8, rows, 8):
        sums = sums + arrived_ref[start : start + 8, :]
    grad_ref[...] = (sums[0:1, :] + sums[4:5, :])[:, :SPAN]
    curve_ref[...] = (sums[1:2, :] + sums[5:6, :])[:, :SPAN]
    basin, chip = lax.axis_index("basin"), lax.axis_index("chip")
    basins, chips = lax.axis_size("basin"), lax.axis_size("chip")
    incoming = jnp.zeros((1, LANES), jnp.float32)
    for hop in reversed(range(1, basins)):
        there = jnp.where(basin + hop < basins, 1.0, 0.0)
        row = 4 * (jnp.minimum(basin + hop, basins - 1) * chips + chip)
        rate = arrived_ref[pl.ds(row + 2, 1), :]
        push = arrived_ref[pl.ds(row + 3, 1), :]
        incoming = there * (rate * incoming + push)
    reach_ref[...] = rate_ref[...] * incoming + push_ref[...]


def results(arrived, rate, push):
    zone = jax.ShapeDtypeStruct((1, SPAN), jnp.float32)
    return pl.pallas_call(
        result_kernel,
        out_shape=(zone, zone, jax.ShapeDtypeStruct(rate.shape, jnp.float32)),
        in_specs=[VMEM] * 3,
        out_specs=(VMEM,) * 3,
        compiler_params=ROOMY,
        name="results",
    )(arrived, rate, push)


def reach_kernel(adjoint_ref, cell_ref, keep_ref, forcing_ref, rate_ref, push_ref, edge_ref):
    rows, columns = adjoint_ref.shape
    upper, lower = halves(adjoint_ref[...])
    table = jnp.concatenate([upper, lower], axis=0).astype(jnp.bfloat16)
    reaches = cell_ref.shape[0]
    width = cell_ref.shape[1]
    values = []
    for reach in range(0, reaches, 4):
        cells = jnp.concatenate([cell_ref[reach + i : reach + i + 1, :] for i in range(4)], axis=1)
        column = (cells & (columns - 1)).astype(jnp.float32)
        hot = jnp.concatenate(
            [one_hot(spread_rows(column - part * 256.0), 256) for part in range(columns // 256)],
            axis=0,
        )
        picked = jnp.dot(table, hot, preferred_element_type=jnp.float32)
        picked = picked[:rows] + picked[rows:]
        row_hit = (cells >> 9) == lax.broadcasted_iota(jnp.int32, (rows, 4 * width), 0)
        found = jnp.sum(jnp.where(row_hit, picked, 0.0), axis=0, keepdims=True)
        values += [found[:, i * width : (i + 1) * width] for i in range(4)]
    rate = jnp.ones((1, width), jnp.float32)
    push = jnp.zeros((1, width), jnp.float32)
    for reach in reversed(range(reaches)):
        keep = keep_ref[reach : reach + 1, :]
        push = keep * push + (forcing_ref[reach : reach + 1, :] + levee_gain * values[reach])
        rate = keep * rate
        rate_ref[reach : reach + 1, :] = rate
        push_ref[reach : reach + 1, :] = push
    edge_ref[0:1, :] = rate
    edge_ref[1:2, :] = push


def reach_maps(adjoint, cells, keep, forcing):
    shape = jax.ShapeDtypeStruct(cells.shape, jnp.float32)
    return pl.pallas_call(
        reach_kernel,
        out_shape=(shape, shape, jax.ShapeDtypeStruct((2, cells.shape[1]), jnp.float32)),
        in_specs=[VMEM] * 4,
        out_specs=(VMEM, VMEM, VMEM),
        compiler_params=ROOMY,
        name="reach_maps",
    )(adjoint, cells, keep, forcing)


def swapped(value):
    return lax.ppermute(value, "core", [(0, 1), (1, 0)])


def exchanged_away(value):
    tiles = lax.axis_size("chip") * lax.axis_size("core")
    pairs = [(i, (i + 1 if i % 2 else i - 1) % tiles) for i in range(tiles)]
    return lax.ppermute(value, ("chip", "core"), pairs)


def per_device(
    depth_start, roughness, depth_seed, zone_label, owner_slot, retention, forcing, levee_cell
):
    depth, rough, seed, label, owner_slot, to_chip, to_away = fetched(
        depth_start[0],
        roughness[0],
        depth_seed[0],
        zone_label[0],
        owner_slot.reshape(-1, LANES),
    )
    from_away = exchanged_away(to_away)
    from_chip = swapped(to_chip)
    moves, device, lane, home = slots_of(owner_slot, label)
    inner = inner_part(depth, rough, seed, label)
    own, other, adjoint = zone_partials(
        depth, rough, seed, from_chip, from_away, *inner, label, moves, device, lane, home
    )
    other = swapped(other)
    rate, push, edge = reach_maps(adjoint, levee_cell, retention, forcing)
    sent = parcels(own, other, edge).reshape(-1, 4, LANES)
    arrived = lax.all_to_all(sent, ("basin", "chip"), 0, 0, tiled=True)
    grad, curve, reach_adjoint = results(arrived.reshape(-1, LANES), rate, push)
    return (grad.reshape(-1), curve.reshape(-1), reach_adjoint)


def solution(mesh):
    basins, tiles = mesh.devices.shape
    fine = jax.sharding.Mesh(
        mesh.devices.reshape(basins, tiles // 2, 2), ("basin", "chip", "core")
    )
    tile = ("chip", "core")
    cells = P("basin", tile, None)
    reaches = P("basin", tile)
    zones = P(("basin", "chip", "core"))
    return jax.shard_map(
        per_device,
        mesh=fine,
        in_specs=(cells, cells, cells, cells, P(), reaches, reaches, reaches),
        out_specs=(zones, zones, reaches),
        check_vma=False,
    )
```

```python
import functools

import jax
import jax.numpy as jnp
from jax import lax
from jax.experimental import pallas as pl
from jax.experimental.pallas import tpu as pltpu
from jax.sharding import PartitionSpec as P

STEPS = 4
HALO = STEPS
SPAN = 127
LANES = 128

courant = 0.24
rough_ref = 0.025
levee_gain = 0.1

VMEM = pl.BlockSpec(memory_space=pltpu.VMEM)
ROOMY = pltpu.CompilerParams(vmem_limit_bytes=48 * 2**20)


def iota_bf16(shape, offset=0):
    ids = lax.broadcasted_iota(jnp.int32, shape, len(shape) - 2)
    if len(shape) == 3:
        ids = ids + shape[1] * lax.broadcasted_iota(jnp.int32, shape, 0)
    return (ids + offset).astype(jnp.float32).astype(jnp.bfloat16)


def spread_rows(row):
    return jnp.broadcast_to(row, (16, row.shape[1])).astype(jnp.bfloat16)


def one_hot(spread, count, weights=None):
    width = spread.shape[1]
    ids = iota_bf16((count // 16, 16, width))
    hit = spread[None] == ids
    zero = jnp.zeros((), jnp.bfloat16)
    if weights is None:
        return jnp.where(hit, jnp.ones((), jnp.bfloat16), zero).reshape(count, width)
    return [jnp.where(hit, w[None], zero).reshape(count, width) for w in weights]


def stacked(x):
    return jnp.concatenate(
        [x[:, start : start + LANES] for start in range(0, x.shape[1], LANES)], axis=0
    )


def from_below(x, distance):
    return pltpu.roll(x, x.shape[0] - distance, 0)


HBM = pl.BlockSpec(memory_space=pltpu.HBM)


FETCH = pltpu.CompilerParams(vmem_limit_bytes=55800000)


def front_kernel(*refs):
    count = (len(refs) - 3) // 2
    sources, kept = refs[:count], refs[count : 2 * count]
    chip_ref, away_ref, arrived = refs[2 * count :]
    copies = [
        pltpu.make_async_copy(source, place, arrived.at[index])
        for index, (source, place) in enumerate(zip(sources, kept))
    ]
    for copy in copies:
        copy.start()
    first_core = lax.axis_index("core") == 0
    for part in range(3):
        copies[part].wait()
        ref = kept[part]
        rows = slice(part * HALO, (part + 1) * HALO)
        top = ref[0:HALO, :]
        bottom = ref[ref.shape[0] - HALO :, :]
        chip_ref[rows, :] = jnp.where(first_core, bottom, top)
        away_ref[rows, :] = jnp.where(first_core, top, bottom)
    for copy in copies[3:]:
        copy.wait()


def fetched(*arrays):
    edge = jax.ShapeDtypeStruct((3 * HALO, arrays[0].shape[1]), jnp.float32)
    kept = tuple(jax.ShapeDtypeStruct(x.shape, x.dtype) for x in arrays)
    return pl.pallas_call(
        front_kernel,
        out_shape=kept + (edge, edge),
        in_specs=[HBM] * len(arrays),
        out_specs=(VMEM,) * (len(arrays) + 2),
        scratch_shapes=[pltpu.SemaphoreType.DMA((len(arrays),))],
        compiler_params=FETCH,
        name="fetch_and_edges",
    )(*arrays)


ABSENT = 2**15 - 1


def split_rows(x):
    rows = x.shape[0]
    inner = stacked(x[RIM : rows - RIM])
    rim = stacked(jnp.concatenate([x[:RIM], x[rows - RIM :]], axis=0))
    return inner, rim


def compacted(x, moves):
    bit = 0
    while 2**bit < x.shape[0]:
        x = jnp.where((moves & 2**bit) != 0, from_below(x, 2**bit), x)
        bit += 1
    return x


def set_strays(stray_ref, grad, moves):
    grad = compacted(grad, moves)
    stray_ref[0], stray_ref[1] = halves(grad)
    stray_ref[2], stray_ref[3] = halves(grad * grad)


def own_first_zone():
    chip = lax.axis_index("basin") * lax.axis_size("chip") + lax.axis_index("chip")
    return (chip * lax.axis_size("core") + lax.axis_index("core")) * SPAN


INNER_ROWS = 40
RIM_ROWS = 16
INNER_STEP = 8
RIM_STEP = 4
RIM = 2 * HALO


def slot_kernel(
    owner_ref,
    label_ref,
    moves_ref,
    device_ref,
    lane_ref,
    home_ref,
    table_ref,
    turned_ref,
    packed_ref,
):
    first_zone = own_first_zone()
    core = lax.axis_index("core").astype(jnp.float32)
    table_ref[...] = jnp.full(table_ref.shape, 256.0 * SPAN, jnp.float32)
    table_ref[0 : owner_ref.shape[0], :] = owner_ref[...].astype(jnp.float32)

    def placed(slots):
        owners = jnp.floor((slots + 0.5) * (1.0 / SPAN))
        lanes = slots - owners * SPAN
        chips = jnp.floor(owners * 0.5)
        swapped = jnp.abs((owners - 2.0 * chips) - core)
        return jnp.where(owners < 256.0, chips + 128.0 * swapped, 256.0), lanes

    owners, lanes = placed(jnp.transpose(table_ref[...]))
    turned_ref[:, 0:256] = (owners * LANES).astype(jnp.bfloat16)
    turned_ref[:, 256:512] = lanes.astype(jnp.bfloat16)

    home_row = first_zone // LANES
    shift = first_zone % LANES
    back = jnp.where(shift == 0, 0, LANES - shift)
    pair = table_ref[pl.ds(home_row, 1), :], table_ref[pl.ds(home_row + 1, 1), :]
    pair = [pltpu.roll(jnp.broadcast_to(row, (8, LANES)), back, 1) for row in pair]
    spot = lax.broadcasted_iota(jnp.int32, (8, LANES), 1)
    home = jnp.where(spot + shift < LANES, pair[0], pair[1])
    home_device, home_lane = placed(jnp.where(spot < SPAN, home, 256.0 * SPAN))
    home_ref[0:1, :] = home_device[0:1]
    home_ref[1:2, :] = home_lane[0:1]

    def compact(label):
        count = label.shape[0]
        offset = label - first_zone
        at_home = (offset >= 0) & (offset < SPAN)
        at_home_count = jnp.where(at_home, 1.0, 0.0)
        row_ids = lax.broadcasted_iota(jnp.int32, (count, count), 0)
        column_ids = lax.broadcasted_iota(jnp.int32, (count, count), 1)
        earlier = jnp.where(column_ids < row_ids, 1.0, 0.0).astype(jnp.bfloat16)
        gaps = jnp.dot(
            earlier, at_home_count.astype(jnp.bfloat16), preferred_element_type=jnp.float32
        ).astype(jnp.int32)
        packed = jnp.where(at_home, ABSENT, gaps * (ABSENT + 1) + label)
        moves = jnp.zeros(packed.shape, jnp.int32)
        bit = 0
        while 2**bit < count:
            marker = (ABSENT + 1) * 2**bit
            near = from_below(packed, 2**bit)
            taken = (near & marker) != 0
            left = (packed & marker) != 0
            packed = jnp.where(taken, near, jnp.where(left, ABSENT, packed))
            moves = jnp.where(taken, moves + 2**bit, moves)
            bit += 1
        most = count - jnp.min(jnp.sum(at_home_count, axis=0, keepdims=True)).astype(jnp.int32)
        return packed & ABSENT, moves, most

    inner_label, rim_label = split_rows(label_ref[...])
    inner_count = inner_label.shape[0]
    packed, moves, inner_most = compact(inner_label)
    packed_ref[0:inner_count, :] = packed
    moves_ref[0:inner_count, :] = moves
    packed, moves, rim_most = compact(rim_label)
    packed_ref[inner_count:, :] = packed
    moves_ref[inner_count:, :] = moves
    inner_steps = jnp.maximum((inner_most - INNER_ROWS + INNER_STEP - 1) // INNER_STEP, 0)
    rim_steps = jnp.maximum((rim_most - RIM_ROWS + RIM_STEP - 1) // RIM_STEP, 0)
    home_ref[2:3, :] = jnp.full((1, LANES), inner_steps.astype(jnp.float32))
    home_ref[3:4, :] = jnp.full((1, LANES), rim_steps.astype(jnp.float32))

    def look_up(first, rows):
        for start in range(0, rows, 4):
            places = [pl.ds(first + start + i, 1) for i in range(4)]
            group_label = jnp.concatenate([packed_ref[place, :] for place in places], axis=1)
            width = group_label.shape[1]
            group = one_hot(spread_rows((group_label >> 7).astype(jnp.float32)), 256)
            found = jnp.dot(
                turned_ref[...],
                jnp.concatenate([group, group], axis=0),
                preferred_element_type=jnp.float32,
            )
            hit = (group_label & 127) == lax.broadcasted_iota(jnp.int32, (LANES, width), 0)
            slot = jnp.sum(jnp.where(hit, found, 0.0), axis=0, keepdims=True)
            owner = jnp.floor(slot * (1.0 / LANES))
            lane = slot - owner * LANES
            for i, place in enumerate(places):
                device_ref[place, :] = owner[:, i * LANES : (i + 1) * LANES]
                lane_ref[place, :] = lane[:, i * LANES : (i + 1) * LANES]

    def more_inner(index, carry):
        look_up(INNER_ROWS + index * INNER_STEP, INNER_STEP)
        return carry

    def more_rim(index, carry):
        look_up(inner_count + RIM_ROWS + index * RIM_STEP, RIM_STEP)
        return carry

    look_up(0, INNER_ROWS)
    look_up(inner_count, RIM_ROWS)
    lax.fori_loop(0, inner_steps, more_inner, 0)
    lax.fori_loop(0, rim_steps, more_rim, 0)


def slots_of(owner_slot, label):
    count = label.size // LANES
    stack = jax.ShapeDtypeStruct((count, LANES), jnp.float32)
    return pl.pallas_call(
        slot_kernel,
        out_shape=(
            jax.ShapeDtypeStruct((count, LANES), jnp.int32),
            stack,
            stack,
            jax.ShapeDtypeStruct((8, LANES), jnp.float32),
        ),
        in_specs=[VMEM, VMEM],
        out_specs=(VMEM,) * 4,
        scratch_shapes=[
            pltpu.VMEM((256, LANES), jnp.float32),
            pltpu.VMEM((LANES, 512), jnp.bfloat16),
            pltpu.VMEM((count, LANES), jnp.int32),
        ],
        compiler_params=ROOMY,
        cost_estimate=pl.CostEstimate(
            flops=2 * 256 * 256 * label.size // 4, bytes_accessed=16 * label.size, transcendentals=0
        ),
        name="slot_lookup",
    )(owner_slot, label)


def below(x):
    return pltpu.roll(x, x.shape[0] - 1, 0)


def above(x):
    return pltpu.roll(x, 1, 0)


def rightward(x):
    return pltpu.roll(x, x.shape[1] - 1, 1)


def leftward(x):
    return pltpu.roll(x, 1, 1)


def window(depth, rough, adjoint):
    rows, columns = depth.shape
    conduct = jnp.where(rough > 0, rough_ref / jnp.where(rough > 0, rough, 1.0), 0.0)
    not_last = lax.broadcasted_iota(jnp.int32, (rows, columns), 1) < columns - 1
    under = below(conduct)
    beside = rightward(conduct)
    down_face = (conduct > 0) & (under > 0)
    side_face = (conduct > 0) & (beside > 0) & not_last
    down_weight = jnp.where(down_face, (0.5 * courant) * (conduct + under), 0.0)
    side_weight = jnp.where(side_face, (0.5 * courant) * (conduct + beside), 0.0)

    def steps(field):
        return below(field) - field, rightward(field) - field

    def advanced(field, down_step, side_step):
        down_flux = down_weight * down_step
        side_flux = side_weight * side_step
        return field + ((down_flux - above(down_flux)) + (side_flux - leftward(side_flux)))

    depth_steps = []
    for section in range(STEPS):
        depth_steps.append(steps(depth))
        if section < STEPS - 1:
            depth = advanced(depth, *depth_steps[-1])
    down_total = jnp.zeros((rows, columns), jnp.float32)
    side_total = jnp.zeros((rows, columns), jnp.float32)
    for section in reversed(range(STEPS)):
        down_step, side_step = steps(adjoint)
        down_total = down_total + depth_steps[section][0] * down_step
        side_total = side_total + depth_steps[section][1] * side_step
        adjoint = advanced(adjoint, down_step, side_step)
    down_total = jnp.where(down_face, down_total, 0.0)
    side_total = jnp.where(side_face, side_total, 0.0)
    total = (down_total + above(down_total)) + (side_total + leftward(side_total))
    return (0.5 * courant) * conduct * total, adjoint


def halves(x):
    upper = x.astype(jnp.bfloat16).astype(jnp.float32)
    return upper, x - upper


HOME_ROWS = 16


def zone_sums(rows):
    left = []
    right = []
    for device, lane, *values in rows:
        left.append(one_hot(spread_rows(device), 256))
        weights = [spread_rows(part) for part in values]
        right.append(jnp.concatenate(one_hot(spread_rows(lane), LANES, weights), axis=0))
    both = lax.dot_general(
        jnp.concatenate(left, axis=1),
        jnp.concatenate(right, axis=1),
        (((1,), (1,)), ((), ())),
        preferred_element_type=jnp.float32,
    )
    return jnp.concatenate(
        [
            both[:, 0:LANES] + both[:, LANES : 2 * LANES],
            both[:, 2 * LANES : 3 * LANES] + both[:, 3 * LANES :],
        ],
        axis=1,
    )


def pair_rows(upper, lower):
    width = upper.shape[1]
    pair = [jnp.broadcast_to(part, (8, width)) for part in (upper, lower)]
    return jnp.concatenate(pair, axis=0).astype(jnp.bfloat16)


def set_cells(cell_ref, offset, grad):
    cell_ref[0] = (offset >> 3).astype(jnp.float32)
    cell_ref[1] = (offset & 7).astype(jnp.float32)
    cell_ref[2], cell_ref[3] = halves(grad)
    cell_ref[4], cell_ref[5] = halves(grad * grad)


def home_products(cell_ref, first, count):
    zero = jnp.zeros((), jnp.bfloat16)
    width = cell_ref.shape[2]
    ids = lax.broadcasted_iota(jnp.int32, (16, width), 0)
    group_ids = ids.astype(jnp.float32).astype(jnp.bfloat16)
    within_ids = (ids & 7).astype(jnp.float32).astype(jnp.bfloat16)
    left = []
    right = []
    for step in range(count):
        row = slice(first + step, first + step + 1)
        group_hit = spread_rows(cell_ref[0, row, :]) == group_ids
        within_hit = spread_rows(cell_ref[1, row, :]) == within_ids
        left.append(jnp.where(group_hit, jnp.ones((), jnp.bfloat16), zero))
        weights = [
            pair_rows(cell_ref[2 + part, row, :], cell_ref[3 + part, row, :]) for part in (0, 2)
        ]
        right.append(jnp.concatenate([jnp.where(within_hit, w, zero) for w in weights], axis=0))
    return lax.dot_general(
        jnp.concatenate(left, axis=1),
        jnp.concatenate(right, axis=1),
        (((1,), (1,)), ((), ())),
        preferred_element_type=jnp.float32,
    )


def stray_rows(refs, first, start, count):
    device_ref, lane_ref, stray_ref = refs
    rows = []
    for step in range(count):
        slot = pl.ds(first + start + step, 1)
        value = pl.ds(start + step, 1)
        values = [stray_ref[part, value, :] for part in range(4)]
        rows.append((device_ref[slot, :], lane_ref[slot, :], *values))
    return rows


def inner_kernel(
    depth_ref,
    rough_ref_,
    seed_ref,
    label_ref,
    moves_ref,
    device_ref,
    lane_ref,
    home_ref,
    total_ref,
    adjoint_ref,
    products_ref,
    cell_ref,
    stray_ref,
):
    grad, adjoint = window(depth_ref[...], rough_ref_[...], seed_ref[...])
    adjoint_ref[...] = adjoint
    rows = grad.shape[0]
    inside = slice(RIM, rows - RIM)
    inner_grad, _ = split_rows(grad)
    set_strays(stray_ref, inner_grad, moves_ref[0 : inner_grad.shape[0], :])
    set_cells(cell_ref, (label_ref[...] - own_first_zone())[inside], grad[inside])
    home = home_products(cell_ref, 0, HOME_ROWS)
    for first in range(HOME_ROWS, rows - 2 * RIM, HOME_ROWS):
        home = home + home_products(cell_ref, first, HOME_ROWS)
    products_ref[...] = home
    refs = device_ref, lane_ref, stray_ref
    total_ref[...] = zone_sums(stray_rows(refs, 0, 0, INNER_ROWS))

    def more(index, carry):
        start = INNER_ROWS + index * INNER_STEP
        total_ref[...] += zone_sums(stray_rows(refs, 0, start, INNER_STEP))
        return carry

    lax.fori_loop(0, jnp.max(home_ref[2:3, :]).astype(jnp.int32), more, 0)


def inner_part(depth, rough, seed, label, *slots):
    inner_rows = depth.shape[0] - 2 * RIM
    return pl.pallas_call(
        inner_kernel,
        out_shape=(
            jax.ShapeDtypeStruct((256, 2 * LANES), jnp.float32),
            jax.ShapeDtypeStruct(depth.shape, jnp.float32),
            jax.ShapeDtypeStruct((16, 32), jnp.float32),
        ),
        in_specs=[VMEM] * (4 + len(slots)),
        out_specs=(VMEM,) * 3,
        scratch_shapes=[
            pltpu.VMEM((6, inner_rows, depth.shape[1]), jnp.float32),
            pltpu.VMEM((4, inner_rows * depth.shape[1] // LANES, LANES), jnp.float32),
        ],
        compiler_params=ROOMY,
        cost_estimate=pl.CostEstimate(
            flops=2 * 256 * 128 * depth.size, bytes_accessed=20 * depth.size, transcendentals=0
        ),
        name="inner_rows",
    )(depth, rough, seed, label, *slots)


def zone_kernel(
    depth_ref,
    rough_ref_,
    seed_ref,
    chip_ref,
    away_ref,
    inner_total_ref,
    inner_adjoint_ref,
    inner_home_ref,
    label_ref,
    moves_ref,
    device_ref,
    lane_ref,
    home_ref,
    own_ref,
    other_ref,
    adjoint_ref,
    total_ref,
    stray_ref,
    cell_ref,
):
    first_core = lax.axis_index("core") == 0
    chip_index, chips = lax.axis_index("chip"), lax.axis_size("chip")
    has_low = jnp.where(first_core & (chip_index == 0), 0.0, 1.0)
    has_high = jnp.where(first_core | (chip_index < chips - 1), 1.0, 0.0)
    rows = depth_ref.shape[0]
    near = RIM + HALO

    def rim(part, ref):
        halo = slice(part * HALO, (part + 1) * HALO)
        chip, away = chip_ref[halo, :], away_ref[halo, :]
        low = jnp.where(first_core, away, chip)
        high = jnp.where(first_core, chip, away)
        if part == 1:
            low, high = low * has_low, high * has_high
        return jnp.concatenate([low, ref[0:near, :], ref[rows - near : rows, :], high], axis=0)

    rim_grad, rim_adjoint = window(rim(0, depth_ref), rim(1, rough_ref_), rim(2, seed_ref))
    top = slice(HALO, HALO + RIM)
    bottom = slice(near + 2 * HALO, near + 2 * HALO + RIM)
    inside = slice(RIM, rows - RIM)
    adjoint_ref[...] = jnp.concatenate(
        [rim_adjoint[top], inner_adjoint_ref[inside, :], rim_adjoint[bottom]], axis=0
    )
    offset = label_ref[...] - own_first_zone()
    set_cells(
        cell_ref,
        jnp.concatenate([offset[:RIM], offset[rows - RIM :]], axis=0),
        jnp.concatenate([rim_grad[top], rim_grad[bottom]], axis=0),
    )
    first = moves_ref.shape[0] - stray_ref.shape[1]
    rim_grad = jnp.concatenate([rim_grad[top], rim_grad[bottom]], axis=0)
    set_strays(stray_ref, stacked(rim_grad), moves_ref[first:, :])
    home = inner_home_ref[...] + home_products(cell_ref, 0, 2 * RIM)
    part = lax.broadcasted_iota(jnp.int32, (32, 2 * LANES), 0)
    zone = lax.broadcasted_iota(jnp.int32, (32, 2 * LANES), 1)
    chosen = ((part & 7) == (zone & 7)) & ((part >= 16) == (zone >= LANES))
    home = jnp.dot(
        home,
        jnp.where(chosen, 1.0, 0.0),
        precision=lax.Precision.HIGHEST,
        preferred_element_type=jnp.float32,
    )
    group = lax.broadcasted_iota(jnp.int32, (16, 2 * LANES), 0)
    zone = lax.broadcasted_iota(jnp.int32, (16, 2 * LANES), 1)
    home = jnp.sum(jnp.where(((zone >> 3) & 15) == group, home, 0.0), axis=0, keepdims=True)
    home = halves(home[:, :LANES]) + halves(home[:, LANES:])

    refs = device_ref, lane_ref, stray_ref
    total_ref[...] = inner_total_ref[...] + zone_sums(
        stray_rows(refs, first, 0, RIM_ROWS) + [(home_ref[0:1, :], home_ref[1:2, :], *home)]
    )

    def more(index, carry):
        start = RIM_ROWS + index * RIM_STEP
        total_ref[...] += zone_sums(stray_rows(refs, first, start, RIM_STEP))
        return carry

    lax.fori_loop(0, jnp.max(home_ref[3:4, :]).astype(jnp.int32), more, 0)
    own_ref[...] = total_ref[0:LANES, :]
    other_ref[...] = total_ref[LANES:, :]


def zone_partials(depth, *others):
    half = jax.ShapeDtypeStruct((LANES, 2 * LANES), jnp.float32)
    return pl.pallas_call(
        zone_kernel,
        out_shape=(half, half, jax.ShapeDtypeStruct(depth.shape, jnp.float32)),
        in_specs=[VMEM] * (1 + len(others)),
        out_specs=(VMEM,) * 3,
        scratch_shapes=[
            pltpu.VMEM((256, 2 * LANES), jnp.float32),
            pltpu.VMEM((4, 2 * RIM * depth.shape[1] // LANES, LANES), jnp.float32),
            pltpu.VMEM((6, 2 * RIM, depth.shape[1]), jnp.float32),
        ],
        compiler_params=ROOMY,
        name="zone_partials",
    )(depth, *others)


def parcel_kernel(own_ref, other_ref, edge_ref, out_ref):
    chips = own_ref.shape[0]
    sums = own_ref[...] + other_ref[...]
    out_ref[pl.ds(0, chips, stride=4), :] = sums[:, :LANES]
    out_ref[pl.ds(1, chips, stride=4), :] = sums[:, LANES:]
    for part in range(2):
        edge = jnp.broadcast_to(edge_ref[part : part + 1, :], (chips, LANES))
        out_ref[pl.ds(2 + part, chips, stride=4), :] = edge


def parcels(own, other, edge):
    return pl.pallas_call(
        parcel_kernel,
        out_shape=jax.ShapeDtypeStruct((4 * own.shape[0], LANES), jnp.float32),
        in_specs=[VMEM] * 3,
        out_specs=VMEM,
        compiler_params=ROOMY,
        name="parcels",
    )(own, other, edge)


def result_kernel(arrived_ref, rate_ref, push_ref, grad_ref, curve_ref, reach_ref):
    rows = arrived_ref.shape[0]
    sums = arrived_ref[0:8, :]
    for start in range(8, rows, 8):
        sums = sums + arrived_ref[start : start + 8, :]
    grad_ref[...] = (sums[0:1, :] + sums[4:5, :])[:, :SPAN]
    curve_ref[...] = (sums[1:2, :] + sums[5:6, :])[:, :SPAN]
    basin, chip = lax.axis_index("basin"), lax.axis_index("chip")
    basins, chips = lax.axis_size("basin"), lax.axis_size("chip")
    incoming = jnp.zeros((1, LANES), jnp.float32)
    for hop in reversed(range(1, basins)):
        there = jnp.where(basin + hop < basins, 1.0, 0.0)
        row = 4 * (jnp.minimum(basin + hop, basins - 1) * chips + chip)
        rate = arrived_ref[pl.ds(row + 2, 1), :]
        push = arrived_ref[pl.ds(row + 3, 1), :]
        incoming = there * (rate * incoming + push)
    reach_ref[...] = rate_ref[...] * incoming + push_ref[...]


def results(arrived, rate, push):
    zone = jax.ShapeDtypeStruct((1, SPAN), jnp.float32)
    return pl.pallas_call(
        result_kernel,
        out_shape=(zone, zone, jax.ShapeDtypeStruct(rate.shape, jnp.float32)),
        in_specs=[VMEM] * 3,
        out_specs=(VMEM,) * 3,
        compiler_params=ROOMY,
        name="results",
    )(arrived, rate, push)


def reach_kernel(adjoint_ref, cell_ref, keep_ref, forcing_ref, rate_ref, push_ref, edge_ref):
    rows, columns = adjoint_ref.shape
    upper, lower = halves(adjoint_ref[...])
    table = jnp.concatenate([upper, lower], axis=0).astype(jnp.bfloat16)
    reaches = cell_ref.shape[0]
    width = cell_ref.shape[1]
    values = []
    for reach in range(0, reaches, 4):
        cells = jnp.concatenate([cell_ref[reach + i : reach + i + 1, :] for i in range(4)], axis=1)
        column = (cells & (columns - 1)).astype(jnp.float32)
        hot = jnp.concatenate(
            [one_hot(spread_rows(column - part * 256.0), 256) for part in range(columns // 256)],
            axis=0,
        )
        picked = jnp.dot(table, hot, preferred_element_type=jnp.float32)
        picked = picked[:rows] + picked[rows:]
        row_hit = (cells >> 9) == lax.broadcasted_iota(jnp.int32, (rows, 4 * width), 0)
        found = jnp.sum(jnp.where(row_hit, picked, 0.0), axis=0, keepdims=True)
        values += [found[:, i * width : (i + 1) * width] for i in range(4)]
    rate = jnp.ones((1, width), jnp.float32)
    push = jnp.zeros((1, width), jnp.float32)
    for reach in reversed(range(reaches)):
        keep = keep_ref[reach : reach + 1, :]
        push = keep * push + (forcing_ref[reach : reach + 1, :] + levee_gain * values[reach])
        rate = keep * rate
        rate_ref[reach : reach + 1, :] = rate
        push_ref[reach : reach + 1, :] = push
    edge_ref[0:1, :] = rate
    edge_ref[1:2, :] = push


def reach_maps(adjoint, cells, keep, forcing):
    shape = jax.ShapeDtypeStruct(cells.shape, jnp.float32)
    return pl.pallas_call(
        reach_kernel,
        out_shape=(shape, shape, jax.ShapeDtypeStruct((2, cells.shape[1]), jnp.float32)),
        in_specs=[VMEM] * 4,
        out_specs=(VMEM, VMEM, VMEM),
        compiler_params=ROOMY,
        name="reach_maps",
    )(adjoint, cells, keep, forcing)


def swapped(value):
    return lax.ppermute(value, "core", [(0, 1), (1, 0)])


def exchanged_away(value):
    tiles = lax.axis_size("chip") * lax.axis_size("core")
    pairs = [(i, (i + 1 if i % 2 else i - 1) % tiles) for i in range(tiles)]
    return lax.ppermute(value, ("chip", "core"), pairs)


def per_device(
    depth_start, roughness, depth_seed, zone_label, owner_slot, retention, forcing, levee_cell
):
    depth, rough, seed, label, owner_slot, to_chip, to_away = fetched(
        depth_start[0],
        roughness[0],
        depth_seed[0],
        zone_label[0],
        owner_slot.reshape(-1, LANES),
    )
    from_away = exchanged_away(to_away)
    from_chip = swapped(to_chip)
    moves, device, lane, home = slots_of(owner_slot, label)
    inner = inner_part(depth, rough, seed, label, moves, device, lane, home)
    own, other, adjoint = zone_partials(
        depth, rough, seed, from_chip, from_away, *inner, label, moves, device, lane, home
    )
    other = swapped(other)
    rate, push, edge = reach_maps(adjoint, levee_cell, retention, forcing)
    sent = parcels(own, other, edge).reshape(-1, 4, LANES)
    arrived = lax.all_to_all(sent, ("basin", "chip"), 0, 0, tiled=True)
    grad, curve, reach_adjoint = results(arrived.reshape(-1, LANES), rate, push)
    return (grad.reshape(-1), curve.reshape(-1), reach_adjoint)


def solution(mesh):
    basins, tiles = mesh.devices.shape
    fine = jax.sharding.Mesh(
        mesh.devices.reshape(basins, tiles // 2, 2), ("basin", "chip", "core")
    )
    tile = ("chip", "core")
    cells = P("basin", tile, None)
    reaches = P("basin", tile)
    zones = P(("basin", "chip", "core"))
    return jax.shard_map(
        per_device,
        mesh=fine,
        in_specs=(cells, cells, cells, cells, P(), reaches, reaches, reaches),
        out_specs=(zones, zones, reaches),
        check_vma=False,
    )
```

```python
import functools

import jax
import jax.numpy as jnp
from jax import lax
from jax.experimental import pallas as pl
from jax.experimental.pallas import tpu as pltpu
from jax.sharding import PartitionSpec as P

STEPS = 4
HALO = STEPS
SPAN = 127
LANES = 128

courant = 0.24
rough_ref = 0.025
levee_gain = 0.1

VMEM = pl.BlockSpec(memory_space=pltpu.VMEM)
ROOMY = pltpu.CompilerParams(vmem_limit_bytes=48 * 2**20)


def iota_bf16(shape, offset=0):
    ids = lax.broadcasted_iota(jnp.int32, shape, len(shape) - 2)
    if len(shape) == 3:
        ids = ids + shape[1] * lax.broadcasted_iota(jnp.int32, shape, 0)
    return (ids + offset).astype(jnp.float32).astype(jnp.bfloat16)


def spread_rows(row):
    return jnp.broadcast_to(row, (16, row.shape[1])).astype(jnp.bfloat16)


def one_hot(spread, count, weights=None):
    width = spread.shape[1]
    ids = iota_bf16((count // 16, 16, width))
    hit = spread[None] == ids
    zero = jnp.zeros((), jnp.bfloat16)
    if weights is None:
        return jnp.where(hit, jnp.ones((), jnp.bfloat16), zero).reshape(count, width)
    return [jnp.where(hit, w[None], zero).reshape(count, width) for w in weights]


def stacked(x):
    return jnp.concatenate(
        [x[:, start : start + LANES] for start in range(0, x.shape[1], LANES)], axis=0
    )


def from_below(x, distance):
    return pltpu.roll(x, x.shape[0] - distance, 0)


HBM = pl.BlockSpec(memory_space=pltpu.HBM)


FETCH = pltpu.CompilerParams(vmem_limit_bytes=55800000)


def front_kernel(*refs):
    count = (len(refs) - 3) // 2
    sources, kept = refs[:count], refs[count : 2 * count]
    chip_ref, away_ref, arrived = refs[2 * count :]
    copies = [
        pltpu.make_async_copy(source, place, arrived.at[index])
        for index, (source, place) in enumerate(zip(sources, kept))
    ]
    for copy in copies:
        copy.start()
    first_core = lax.axis_index("core") == 0
    for part in range(3):
        copies[part].wait()
        ref = kept[part]
        rows = slice(part * HALO, (part + 1) * HALO)
        top = ref[0:HALO, :]
        bottom = ref[ref.shape[0] - HALO :, :]
        chip_ref[rows, :] = jnp.where(first_core, bottom, top)
        away_ref[rows, :] = jnp.where(first_core, top, bottom)
    for copy in copies[3:]:
        copy.wait()


def fetched(*arrays):
    edge = jax.ShapeDtypeStruct((3 * HALO, arrays[0].shape[1]), jnp.float32)
    kept = tuple(jax.ShapeDtypeStruct(x.shape, x.dtype) for x in arrays)
    return pl.pallas_call(
        front_kernel,
        out_shape=kept + (edge, edge),
        in_specs=[HBM] * len(arrays),
        out_specs=(VMEM,) * (len(arrays) + 2),
        scratch_shapes=[pltpu.SemaphoreType.DMA((len(arrays),))],
        compiler_params=FETCH,
        name="fetch_and_edges",
    )(*arrays)


ABSENT = 2**15 - 1


def split_rows(x):
    rows = x.shape[0]
    inner = stacked(x[RIM : rows - RIM])
    rim = stacked(jnp.concatenate([x[:RIM], x[rows - RIM :]], axis=0))
    return inner, rim


def compacted(x, moves):
    bit = 0
    while 2**bit < x.shape[0]:
        x = jnp.where((moves & 2**bit) != 0, from_below(x, 2**bit), x)
        bit += 1
    return x


def set_strays(stray_ref, grad, moves):
    grad = compacted(grad, moves)
    stray_ref[0], stray_ref[1] = halves(grad)
    stray_ref[2], stray_ref[3] = halves(grad * grad)


def own_first_zone():
    chip = lax.axis_index("basin") * lax.axis_size("chip") + lax.axis_index("chip")
    return (chip * lax.axis_size("core") + lax.axis_index("core")) * SPAN


INNER_ROWS = 40
RIM_ROWS = 16
INNER_STEP = 8
RIM_STEP = 4
RIM = 2 * HALO


def slot_kernel(
    owner_ref,
    label_ref,
    moves_ref,
    device_ref,
    lane_ref,
    home_ref,
    table_ref,
    turned_ref,
    packed_ref,
):
    first_zone = own_first_zone()
    core = lax.axis_index("core").astype(jnp.float32)
    table_ref[...] = jnp.full(table_ref.shape, 256.0 * SPAN, jnp.float32)
    table_ref[0 : owner_ref.shape[0], :] = owner_ref[...].astype(jnp.float32)

    def placed(slots):
        owners = jnp.floor((slots + 0.5) * (1.0 / SPAN))
        lanes = slots - owners * SPAN
        chips = jnp.floor(owners * 0.5)
        swapped = jnp.abs((owners - 2.0 * chips) - core)
        return jnp.where(owners < 256.0, chips + 128.0 * swapped, 256.0), lanes

    owners, lanes = placed(jnp.transpose(table_ref[...]))
    turned_ref[:, 0:256] = (owners * LANES).astype(jnp.bfloat16)
    turned_ref[:, 256:512] = lanes.astype(jnp.bfloat16)

    home_row = first_zone // LANES
    shift = first_zone % LANES
    back = jnp.where(shift == 0, 0, LANES - shift)
    pair = table_ref[pl.ds(home_row, 1), :], table_ref[pl.ds(home_row + 1, 1), :]
    pair = [pltpu.roll(jnp.broadcast_to(row, (8, LANES)), back, 1) for row in pair]
    spot = lax.broadcasted_iota(jnp.int32, (8, LANES), 1)
    home = jnp.where(spot + shift < LANES, pair[0], pair[1])
    home_device, home_lane = placed(jnp.where(spot < SPAN, home, 256.0 * SPAN))
    home_ref[0:1, :] = home_device[0:1]
    home_ref[1:2, :] = home_lane[0:1]

    def compact(label):
        count = label.shape[0]
        offset = label - first_zone
        at_home = (offset >= 0) & (offset < SPAN)
        at_home_count = jnp.where(at_home, 1.0, 0.0)
        row_ids = lax.broadcasted_iota(jnp.int32, (count, count), 0)
        column_ids = lax.broadcasted_iota(jnp.int32, (count, count), 1)
        earlier = jnp.where(column_ids < row_ids, 1.0, 0.0).astype(jnp.bfloat16)
        gaps = jnp.dot(
            earlier, at_home_count.astype(jnp.bfloat16), preferred_element_type=jnp.float32
        ).astype(jnp.int32)
        packed = jnp.where(at_home, ABSENT, gaps * (ABSENT + 1) + label)
        moves = jnp.zeros(packed.shape, jnp.int32)
        bit = 0
        while 2**bit < count:
            marker = (ABSENT + 1) * 2**bit
            near = from_below(packed, 2**bit)
            taken = (near & marker) != 0
            left = (packed & marker) != 0
            packed = jnp.where(taken, near, jnp.where(left, ABSENT, packed))
            moves = jnp.where(taken, moves + 2**bit, moves)
            bit += 1
        most = count - jnp.min(jnp.sum(at_home_count, axis=0, keepdims=True)).astype(jnp.int32)
        return packed & ABSENT, moves, most

    inner_label, rim_label = split_rows(label_ref[...])
    inner_count = inner_label.shape[0]
    packed, moves, inner_most = compact(inner_label)
    packed_ref[0:inner_count, :] = packed
    moves_ref[0:inner_count, :] = moves
    packed, moves, rim_most = compact(rim_label)
    packed_ref[inner_count:, :] = packed
    moves_ref[inner_count:, :] = moves
    inner_steps = jnp.maximum((inner_most - INNER_ROWS + INNER_STEP - 1) // INNER_STEP, 0)
    rim_steps = jnp.maximum((rim_most - RIM_ROWS + RIM_STEP - 1) // RIM_STEP, 0)
    home_ref[2:3, :] = jnp.full((1, LANES), inner_steps.astype(jnp.float32))
    home_ref[3:4, :] = jnp.full((1, LANES), rim_steps.astype(jnp.float32))

    def look_up(first, rows):
        for start in range(0, rows, 4):
            places = [pl.ds(first + start + i, 1) for i in range(4)]
            group_label = jnp.concatenate([packed_ref[place, :] for place in places], axis=1)
            width = group_label.shape[1]
            group = one_hot(spread_rows((group_label >> 7).astype(jnp.float32)), 256)
            found = jnp.dot(
                turned_ref[...],
                jnp.concatenate([group, group], axis=0),
                preferred_element_type=jnp.float32,
            )
            hit = (group_label & 127) == lax.broadcasted_iota(jnp.int32, (LANES, width), 0)
            slot = jnp.sum(jnp.where(hit, found, 0.0), axis=0, keepdims=True)
            owner = jnp.floor(slot * (1.0 / LANES))
            lane = slot - owner * LANES
            for i, place in enumerate(places):
                device_ref[place, :] = owner[:, i * LANES : (i + 1) * LANES]
                lane_ref[place, :] = lane[:, i * LANES : (i + 1) * LANES]

    def more_inner(index, carry):
        look_up(INNER_ROWS + index * INNER_STEP, INNER_STEP)
        return carry

    def more_rim(index, carry):
        look_up(inner_count + RIM_ROWS + index * RIM_STEP, RIM_STEP)
        return carry

    look_up(0, INNER_ROWS)
    look_up(inner_count, RIM_ROWS)
    lax.fori_loop(0, inner_steps, more_inner, 0)
    lax.fori_loop(0, rim_steps, more_rim, 0)


def slots_of(owner_slot, label):
    count = label.size // LANES
    stack = jax.ShapeDtypeStruct((count, LANES), jnp.float32)
    return pl.pallas_call(
        slot_kernel,
        out_shape=(
            jax.ShapeDtypeStruct((count, LANES), jnp.int32),
            stack,
            stack,
            jax.ShapeDtypeStruct((8, LANES), jnp.float32),
        ),
        in_specs=[VMEM, VMEM],
        out_specs=(VMEM,) * 4,
        scratch_shapes=[
            pltpu.VMEM((256, LANES), jnp.float32),
            pltpu.VMEM((LANES, 512), jnp.bfloat16),
            pltpu.VMEM((count, LANES), jnp.int32),
        ],
        compiler_params=ROOMY,
        cost_estimate=pl.CostEstimate(
            flops=2 * 256 * 256 * label.size // 4, bytes_accessed=16 * label.size, transcendentals=0
        ),
        name="slot_lookup",
    )(owner_slot, label)


def below(x):
    return pltpu.roll(x, x.shape[0] - 1, 0)


def above(x):
    return pltpu.roll(x, 1, 0)


def rightward(x):
    return pltpu.roll(x, x.shape[1] - 1, 1)


def leftward(x):
    return pltpu.roll(x, 1, 1)


def window(depth, rough, adjoint):
    rows, columns = depth.shape
    conduct = jnp.where(rough > 0, rough_ref / jnp.where(rough > 0, rough, 1.0), 0.0)
    not_last = lax.broadcasted_iota(jnp.int32, (rows, columns), 1) < columns - 1
    under = below(conduct)
    beside = rightward(conduct)
    down_face = (conduct > 0) & (under > 0)
    side_face = (conduct > 0) & (beside > 0) & not_last
    down_weight = jnp.where(down_face, (0.5 * courant) * (conduct + under), 0.0)
    side_weight = jnp.where(side_face, (0.5 * courant) * (conduct + beside), 0.0)

    def steps(field):
        return below(field) - field, rightward(field) - field

    def advanced(field, down_step, side_step):
        down_flux = down_weight * down_step
        side_flux = side_weight * side_step
        return field + ((down_flux - above(down_flux)) + (side_flux - leftward(side_flux)))

    depth_steps = []
    for section in range(STEPS):
        depth_steps.append(steps(depth))
        if section < STEPS - 1:
            depth = advanced(depth, *depth_steps[-1])
    down_total = jnp.zeros((rows, columns), jnp.float32)
    side_total = jnp.zeros((rows, columns), jnp.float32)
    for section in reversed(range(STEPS)):
        down_step, side_step = steps(adjoint)
        down_total = down_total + depth_steps[section][0] * down_step
        side_total = side_total + depth_steps[section][1] * side_step
        adjoint = advanced(adjoint, down_step, side_step)
    down_total = jnp.where(down_face, down_total, 0.0)
    side_total = jnp.where(side_face, side_total, 0.0)
    total = (down_total + above(down_total)) + (side_total + leftward(side_total))
    return (0.5 * courant) * conduct * total, adjoint


def halves(x):
    upper = x.astype(jnp.bfloat16).astype(jnp.float32)
    return upper, x - upper


HOME_ROWS = 16


def zone_sums(rows):
    left = []
    right = []
    for device, lane, *values in rows:
        left.append(one_hot(spread_rows(device), 256))
        weights = [spread_rows(part) for part in values]
        right.append(jnp.concatenate(one_hot(spread_rows(lane), LANES, weights), axis=0))
    both = lax.dot_general(
        jnp.concatenate(left, axis=1),
        jnp.concatenate(right, axis=1),
        (((1,), (1,)), ((), ())),
        preferred_element_type=jnp.float32,
    )
    return jnp.concatenate(
        [
            both[:, 0:LANES] + both[:, LANES : 2 * LANES],
            both[:, 2 * LANES : 3 * LANES] + both[:, 3 * LANES :],
        ],
        axis=1,
    )


def pair_rows(upper, lower):
    width = upper.shape[1]
    pair = [jnp.broadcast_to(part, (8, width)) for part in (upper, lower)]
    return jnp.concatenate(pair, axis=0).astype(jnp.bfloat16)


def set_cells(cell_ref, offset, grad):
    cell_ref[0] = (offset >> 3).astype(jnp.float32)
    cell_ref[1] = (offset & 7).astype(jnp.float32)
    cell_ref[2], cell_ref[3] = halves(grad)
    cell_ref[4], cell_ref[5] = halves(grad * grad)


def home_products(cell_ref, first, count):
    zero = jnp.zeros((), jnp.bfloat16)
    width = cell_ref.shape[2]
    ids = lax.broadcasted_iota(jnp.int32, (16, width), 0)
    group_ids = ids.astype(jnp.float32).astype(jnp.bfloat16)
    within_ids = (ids & 7).astype(jnp.float32).astype(jnp.bfloat16)
    left = []
    right = []
    for step in range(count):
        row = slice(first + step, first + step + 1)
        group_hit = spread_rows(cell_ref[0, row, :]) == group_ids
        within_hit = spread_rows(cell_ref[1, row, :]) == within_ids
        left.append(jnp.where(group_hit, jnp.ones((), jnp.bfloat16), zero))
        weights = [
            pair_rows(cell_ref[2 + part, row, :], cell_ref[3 + part, row, :]) for part in (0, 2)
        ]
        right.append(jnp.concatenate([jnp.where(within_hit, w, zero) for w in weights], axis=0))
    return lax.dot_general(
        jnp.concatenate(left, axis=1),
        jnp.concatenate(right, axis=1),
        (((1,), (1,)), ((), ())),
        preferred_element_type=jnp.float32,
    )


def stray_rows(refs, first, start, count):
    device_ref, lane_ref, stray_ref = refs
    rows = []
    for step in range(count):
        slot = pl.ds(first + start + step, 1)
        value = pl.ds(start + step, 1)
        values = [stray_ref[part, value, :] for part in range(4)]
        rows.append((device_ref[slot, :], lane_ref[slot, :], *values))
    return rows


def inner_kernel(
    depth_ref,
    rough_ref_,
    seed_ref,
    label_ref,
    moves_ref,
    device_ref,
    lane_ref,
    home_ref,
    total_ref,
    adjoint_ref,
    products_ref,
    cell_ref,
    stray_ref,
):
    grad, adjoint = window(depth_ref[...], rough_ref_[...], seed_ref[...])
    adjoint_ref[...] = adjoint
    rows = grad.shape[0]
    inside = slice(RIM, rows - RIM)
    inner_grad, _ = split_rows(grad)
    set_strays(stray_ref, inner_grad, moves_ref[0 : inner_grad.shape[0], :])
    set_cells(cell_ref, (label_ref[...] - own_first_zone())[inside], grad[inside])
    home = home_products(cell_ref, 0, HOME_ROWS)
    for first in range(HOME_ROWS, rows - 2 * RIM, HOME_ROWS):
        home = home + home_products(cell_ref, first, HOME_ROWS)
    products_ref[...] = home
    refs = device_ref, lane_ref, stray_ref
    total_ref[...] = zone_sums(stray_rows(refs, 0, 0, INNER_ROWS))

    def more(index, carry):
        start = INNER_ROWS + index * INNER_STEP
        total_ref[...] += zone_sums(stray_rows(refs, 0, start, INNER_STEP))
        return carry

    lax.fori_loop(0, jnp.max(home_ref[2:3, :]).astype(jnp.int32), more, 0)


def inner_part(depth, rough, seed, label, *slots):
    inner_rows = depth.shape[0] - 2 * RIM
    return pl.pallas_call(
        inner_kernel,
        out_shape=(
            jax.ShapeDtypeStruct((256, 2 * LANES), jnp.float32),
            jax.ShapeDtypeStruct(depth.shape, jnp.float32),
            jax.ShapeDtypeStruct((16, 32), jnp.float32),
        ),
        in_specs=[VMEM] * (4 + len(slots)),
        out_specs=(VMEM,) * 3,
        scratch_shapes=[
            pltpu.VMEM((6, inner_rows, depth.shape[1]), jnp.float32),
            pltpu.VMEM((4, inner_rows * depth.shape[1] // LANES, LANES), jnp.float32),
        ],
        compiler_params=ROOMY,
        cost_estimate=pl.CostEstimate(
            flops=2 * 256 * 128 * depth.size, bytes_accessed=20 * depth.size, transcendentals=0
        ),
        name="inner_rows",
    )(depth, rough, seed, label, *slots)


def zone_kernel(
    depth_ref,
    rough_ref_,
    seed_ref,
    chip_ref,
    away_ref,
    inner_total_ref,
    inner_adjoint_ref,
    inner_home_ref,
    label_ref,
    moves_ref,
    device_ref,
    lane_ref,
    home_ref,
    own_ref,
    other_ref,
    adjoint_ref,
    total_ref,
    stray_ref,
    cell_ref,
):
    first_core = lax.axis_index("core") == 0
    chip_index, chips = lax.axis_index("chip"), lax.axis_size("chip")
    has_low = jnp.where(first_core & (chip_index == 0), 0.0, 1.0)
    has_high = jnp.where(first_core | (chip_index < chips - 1), 1.0, 0.0)
    rows = depth_ref.shape[0]
    near = RIM + HALO

    def rim(part, ref):
        halo = slice(part * HALO, (part + 1) * HALO)
        chip, away = chip_ref[halo, :], away_ref[halo, :]
        low = jnp.where(first_core, away, chip)
        high = jnp.where(first_core, chip, away)
        if part == 1:
            low, high = low * has_low, high * has_high
        return jnp.concatenate([low, ref[0:near, :], ref[rows - near : rows, :], high], axis=0)

    rim_grad, rim_adjoint = window(rim(0, depth_ref), rim(1, rough_ref_), rim(2, seed_ref))
    top = slice(HALO, HALO + RIM)
    bottom = slice(near + 2 * HALO, near + 2 * HALO + RIM)
    inside = slice(RIM, rows - RIM)
    adjoint_ref[...] = jnp.concatenate(
        [rim_adjoint[top], inner_adjoint_ref[inside, :], rim_adjoint[bottom]], axis=0
    )
    offset = label_ref[...] - own_first_zone()
    set_cells(
        cell_ref,
        jnp.concatenate([offset[:RIM], offset[rows - RIM :]], axis=0),
        jnp.concatenate([rim_grad[top], rim_grad[bottom]], axis=0),
    )
    first = moves_ref.shape[0] - stray_ref.shape[1]
    rim_grad = jnp.concatenate([rim_grad[top], rim_grad[bottom]], axis=0)
    set_strays(stray_ref, stacked(rim_grad), moves_ref[first:, :])
    home = inner_home_ref[...] + home_products(cell_ref, 0, 2 * RIM)
    part = lax.broadcasted_iota(jnp.int32, (32, 2 * LANES), 0)
    zone = lax.broadcasted_iota(jnp.int32, (32, 2 * LANES), 1)
    chosen = ((part & 7) == (zone & 7)) & ((part >= 16) == (zone >= LANES))
    home = jnp.dot(
        home,
        jnp.where(chosen, 1.0, 0.0),
        precision=lax.Precision.HIGHEST,
        preferred_element_type=jnp.float32,
    )
    group = lax.broadcasted_iota(jnp.int32, (16, 2 * LANES), 0)
    zone = lax.broadcasted_iota(jnp.int32, (16, 2 * LANES), 1)
    home = jnp.sum(jnp.where(((zone >> 3) & 15) == group, home, 0.0), axis=0, keepdims=True)
    home = halves(home[:, :LANES]) + halves(home[:, LANES:])

    refs = device_ref, lane_ref, stray_ref
    total_ref[...] = inner_total_ref[...] + zone_sums(
        stray_rows(refs, first, 0, RIM_ROWS) + [(home_ref[0:1, :], home_ref[1:2, :], *home)]
    )

    def more(index, carry):
        start = RIM_ROWS + index * RIM_STEP
        total_ref[...] += zone_sums(stray_rows(refs, first, start, RIM_STEP))
        return carry

    lax.fori_loop(0, jnp.max(home_ref[3:4, :]).astype(jnp.int32), more, 0)
    own_ref[...] = total_ref[0:LANES, :]
    other_ref[...] = total_ref[LANES:, :]


def zone_partials(depth, *others):
    half = jax.ShapeDtypeStruct((LANES, 2 * LANES), jnp.float32)
    return pl.pallas_call(
        zone_kernel,
        out_shape=(half, half, jax.ShapeDtypeStruct(depth.shape, jnp.float32)),
        in_specs=[VMEM] * (1 + len(others)),
        out_specs=(VMEM,) * 3,
        scratch_shapes=[
            pltpu.VMEM((256, 2 * LANES), jnp.float32),
            pltpu.VMEM((4, 2 * RIM * depth.shape[1] // LANES, LANES), jnp.float32),
            pltpu.VMEM((6, 2 * RIM, depth.shape[1]), jnp.float32),
        ],
        compiler_params=ROOMY,
        name="zone_partials",
    )(depth, *others)


def parcel_kernel(own_ref, other_ref, edge_ref, out_ref):
    chips = own_ref.shape[0]
    sums = own_ref[...] + other_ref[...]
    out_ref[pl.ds(0, chips, stride=4), :] = sums[:, :LANES]
    out_ref[pl.ds(1, chips, stride=4), :] = sums[:, LANES:]
    for part in range(2):
        edge = jnp.broadcast_to(edge_ref[part : part + 1, :], (chips, LANES))
        out_ref[pl.ds(2 + part, chips, stride=4), :] = edge


def parcels(own, other, edge):
    return pl.pallas_call(
        parcel_kernel,
        out_shape=jax.ShapeDtypeStruct((4 * own.shape[0], LANES), jnp.float32),
        in_specs=[VMEM] * 3,
        out_specs=VMEM,
        compiler_params=ROOMY,
        name="parcels",
    )(own, other, edge)


def result_kernel(arrived_ref, rate_ref, push_ref, grad_ref, curve_ref, reach_ref):
    rows = arrived_ref.shape[0]
    sums = arrived_ref[0:8, :]
    for start in range(8, rows, 8):
        sums = sums + arrived_ref[start : start + 8, :]
    grad_ref[...] = (sums[0:1, :] + sums[4:5, :])[:, :SPAN]
    curve_ref[...] = (sums[1:2, :] + sums[5:6, :])[:, :SPAN]
    basin, chip = lax.axis_index("basin"), lax.axis_index("chip")
    basins, chips = lax.axis_size("basin"), lax.axis_size("chip")
    incoming = jnp.zeros((1, LANES), jnp.float32)
    for hop in reversed(range(1, basins)):
        there = jnp.where(basin + hop < basins, 1.0, 0.0)
        row = 4 * (jnp.minimum(basin + hop, basins - 1) * chips + chip)
        rate = arrived_ref[pl.ds(row + 2, 1), :]
        push = arrived_ref[pl.ds(row + 3, 1), :]
        incoming = there * (rate * incoming + push)
    reach_ref[...] = rate_ref[...] * incoming + push_ref[...]


def results(arrived, rate, push):
    zone = jax.ShapeDtypeStruct((1, SPAN), jnp.float32)
    return pl.pallas_call(
        result_kernel,
        out_shape=(zone, zone, jax.ShapeDtypeStruct(rate.shape, jnp.float32)),
        in_specs=[VMEM] * 3,
        out_specs=(VMEM,) * 3,
        compiler_params=ROOMY,
        name="results",
    )(arrived, rate, push)


def reach_kernel(adjoint_ref, cell_ref, keep_ref, forcing_ref, rate_ref, push_ref, edge_ref):
    rows, columns = adjoint_ref.shape
    upper, lower = halves(adjoint_ref[...])
    table = jnp.concatenate([upper, lower], axis=0).astype(jnp.bfloat16)
    reaches = cell_ref.shape[0]
    width = cell_ref.shape[1]
    values = []
    for reach in range(0, reaches, 4):
        cells = jnp.concatenate([cell_ref[reach + i : reach + i + 1, :] for i in range(4)], axis=1)
        column = (cells & (columns - 1)).astype(jnp.float32)
        hot = jnp.concatenate(
            [one_hot(spread_rows(column - part * 256.0), 256) for part in range(columns // 256)],
            axis=0,
        )
        picked = jnp.dot(table, hot, preferred_element_type=jnp.float32)
        picked = picked[:rows] + picked[rows:]
        row_hit = (cells >> 9) == lax.broadcasted_iota(jnp.int32, (rows, 4 * width), 0)
        found = jnp.sum(jnp.where(row_hit, picked, 0.0), axis=0, keepdims=True)
        values += [found[:, i * width : (i + 1) * width] for i in range(4)]
    rate = jnp.ones((1, width), jnp.float32)
    push = jnp.zeros((1, width), jnp.float32)
    for reach in reversed(range(reaches)):
        keep = keep_ref[reach : reach + 1, :]
        push = keep * push + (forcing_ref[reach : reach + 1, :] + levee_gain * values[reach])
        rate = keep * rate
        rate_ref[reach : reach + 1, :] = rate
        push_ref[reach : reach + 1, :] = push
    edge_ref[0:1, :] = rate
    edge_ref[1:2, :] = push


def reach_maps(adjoint, cells, keep, forcing):
    shape = jax.ShapeDtypeStruct(cells.shape, jnp.float32)
    return pl.pallas_call(
        reach_kernel,
        out_shape=(shape, shape, jax.ShapeDtypeStruct((2, cells.shape[1]), jnp.float32)),
        in_specs=[VMEM] * 4,
        out_specs=(VMEM, VMEM, VMEM),
        compiler_params=ROOMY,
        name="reach_maps",
    )(adjoint, cells, keep, forcing)


def swapped(value):
    return lax.ppermute(value, "core", [(0, 1), (1, 0)])


def exchanged_away(value):
    tiles = lax.axis_size("chip") * lax.axis_size("core")
    pairs = [(i, (i + 1 if i % 2 else i - 1) % tiles) for i in range(tiles)]
    return lax.ppermute(value, ("chip", "core"), pairs)


def per_device(
    depth_start, roughness, depth_seed, zone_label, owner_slot, retention, forcing, levee_cell
):
    depth, rough, seed, label, owner_slot, to_chip, to_away = fetched(
        depth_start[0],
        roughness[0],
        depth_seed[0],
        zone_label[0],
        owner_slot.reshape(-1, LANES),
    )
    from_away = exchanged_away(to_away)
    moves, device, lane, home = slots_of(owner_slot, label)
    to_chip, home = lax.optimization_barrier((to_chip, home))
    from_chip = swapped(to_chip)
    inner = inner_part(depth, rough, seed, label, moves, device, lane, home)
    own, other, adjoint = zone_partials(
        depth, rough, seed, from_chip, from_away, *inner, label, moves, device, lane, home
    )
    other = swapped(other)
    rate, push, edge = reach_maps(adjoint, levee_cell, retention, forcing)
    sent = parcels(own, other, edge).reshape(-1, 4, LANES)
    arrived = lax.all_to_all(sent, ("basin", "chip"), 0, 0, tiled=True)
    grad, curve, reach_adjoint = results(arrived.reshape(-1, LANES), rate, push)
    return (grad.reshape(-1), curve.reshape(-1), reach_adjoint)


def solution(mesh):
    basins, tiles = mesh.devices.shape
    fine = jax.sharding.Mesh(
        mesh.devices.reshape(basins, tiles // 2, 2), ("basin", "chip", "core")
    )
    tile = ("chip", "core")
    cells = P("basin", tile, None)
    reaches = P("basin", tile)
    zones = P(("basin", "chip", "core"))
    return jax.shard_map(
        per_device,
        mesh=fine,
        in_specs=(cells, cells, cells, cells, P(), reaches, reaches, reaches),
        out_specs=(zones, zones, reaches),
        check_vma=False,
    )
```

```python
import functools

import jax
import jax.numpy as jnp
from jax import lax
from jax.experimental import pallas as pl
from jax.experimental.pallas import tpu as pltpu
from jax.sharding import PartitionSpec as P

STEPS = 4
HALO = STEPS
SPAN = 127
LANES = 128

courant = 0.24
rough_ref = 0.025
levee_gain = 0.1

VMEM = pl.BlockSpec(memory_space=pltpu.VMEM)
ROOMY = pltpu.CompilerParams(vmem_limit_bytes=48 * 2**20)


def iota_bf16(shape, offset=0):
    ids = lax.broadcasted_iota(jnp.int32, shape, len(shape) - 2)
    if len(shape) == 3:
        ids = ids + shape[1] * lax.broadcasted_iota(jnp.int32, shape, 0)
    return (ids + offset).astype(jnp.float32).astype(jnp.bfloat16)


def spread_rows(row):
    return jnp.broadcast_to(row, (16, row.shape[1])).astype(jnp.bfloat16)


def one_hot(spread, count, weights=None):
    width = spread.shape[1]
    ids = iota_bf16((count // 16, 16, width))
    hit = spread[None] == ids
    zero = jnp.zeros((), jnp.bfloat16)
    if weights is None:
        return jnp.where(hit, jnp.ones((), jnp.bfloat16), zero).reshape(count, width)
    return [jnp.where(hit, w[None], zero).reshape(count, width) for w in weights]


def stacked(x):
    return jnp.concatenate(
        [x[:, start : start + LANES] for start in range(0, x.shape[1], LANES)], axis=0
    )


def from_below(x, distance):
    return pltpu.roll(x, x.shape[0] - distance, 0)


HBM = pl.BlockSpec(memory_space=pltpu.HBM)


FETCH = pltpu.CompilerParams(vmem_limit_bytes=55800000)


def front_kernel(*refs):
    count = (len(refs) - 3) // 2
    sources, kept = refs[:count], refs[count : 2 * count]
    chip_ref, away_ref, arrived = refs[2 * count :]
    copies = [
        pltpu.make_async_copy(source, place, arrived.at[index])
        for index, (source, place) in enumerate(zip(sources, kept))
    ]
    for copy in copies:
        copy.start()
    first_core = lax.axis_index("core") == 0
    for part in range(3):
        copies[part].wait()
        ref = kept[part]
        rows = slice(part * HALO, (part + 1) * HALO)
        top = ref[0:HALO, :]
        bottom = ref[ref.shape[0] - HALO :, :]
        chip_ref[rows, :] = jnp.where(first_core, bottom, top)
        away_ref[rows, :] = jnp.where(first_core, top, bottom)
    for copy in copies[3:]:
        copy.wait()


def fetched(*arrays):
    edge = jax.ShapeDtypeStruct((3 * HALO, arrays[0].shape[1]), jnp.float32)
    kept = tuple(jax.ShapeDtypeStruct(x.shape, x.dtype) for x in arrays)
    return pl.pallas_call(
        front_kernel,
        out_shape=kept + (edge, edge),
        in_specs=[HBM] * len(arrays),
        out_specs=(VMEM,) * (len(arrays) + 2),
        scratch_shapes=[pltpu.SemaphoreType.DMA((len(arrays),))],
        compiler_params=FETCH,
        name="fetch_and_edges",
    )(*arrays)


ABSENT = 2**15 - 1


def split_rows(x):
    rows = x.shape[0]
    inner = stacked(x[RIM : rows - RIM])
    rim = stacked(jnp.concatenate([x[:RIM], x[rows - RIM :]], axis=0))
    return inner, rim


def compacted(x, moves):
    bit = 0
    while 2**bit < x.shape[0]:
        x = jnp.where((moves & 2**bit) != 0, from_below(x, 2**bit), x)
        bit += 1
    return x


def set_strays(stray_ref, grad, moves):
    grad = compacted(grad, moves)
    stray_ref[0], stray_ref[1] = halves(grad)
    stray_ref[2], stray_ref[3] = halves(grad * grad)


def own_first_zone():
    chip = lax.axis_index("basin") * lax.axis_size("chip") + lax.axis_index("chip")
    return (chip * lax.axis_size("core") + lax.axis_index("core")) * SPAN


INNER_ROWS = 40
RIM_ROWS = 20
INNER_STEP = 4
RIM_STEP = 4
RIM = 2 * HALO


def slot_kernel(
    owner_ref,
    label_ref,
    moves_ref,
    device_ref,
    lane_ref,
    home_ref,
    table_ref,
    turned_ref,
    packed_ref,
):
    first_zone = own_first_zone()
    core = lax.axis_index("core").astype(jnp.float32)
    table_ref[...] = jnp.full(table_ref.shape, 256.0 * SPAN, jnp.float32)
    table_ref[0 : owner_ref.shape[0], :] = owner_ref[...].astype(jnp.float32)

    def placed(slots):
        owners = jnp.floor((slots + 0.5) * (1.0 / SPAN))
        lanes = slots - owners * SPAN
        chips = jnp.floor(owners * 0.5)
        swapped = jnp.abs((owners - 2.0 * chips) - core)
        return jnp.where(owners < 256.0, chips + 128.0 * swapped, 256.0), lanes

    owners, lanes = placed(jnp.transpose(table_ref[...]))
    turned_ref[:, 0:256] = (owners * LANES).astype(jnp.bfloat16)
    turned_ref[:, 256:512] = lanes.astype(jnp.bfloat16)

    home_row = first_zone // LANES
    shift = first_zone % LANES
    back = jnp.where(shift == 0, 0, LANES - shift)
    pair = table_ref[pl.ds(home_row, 1), :], table_ref[pl.ds(home_row + 1, 1), :]
    pair = [pltpu.roll(jnp.broadcast_to(row, (8, LANES)), back, 1) for row in pair]
    spot = lax.broadcasted_iota(jnp.int32, (8, LANES), 1)
    home = jnp.where(spot + shift < LANES, pair[0], pair[1])
    home_device, home_lane = placed(jnp.where(spot < SPAN, home, 256.0 * SPAN))
    home_ref[0:1, :] = home_device[0:1]
    home_ref[1:2, :] = home_lane[0:1]

    def compact(label):
        count = label.shape[0]
        offset = label - first_zone
        at_home = (offset >= 0) & (offset < SPAN)
        at_home_count = jnp.where(at_home, 1.0, 0.0)
        row_ids = lax.broadcasted_iota(jnp.int32, (count, count), 0)
        column_ids = lax.broadcasted_iota(jnp.int32, (count, count), 1)
        earlier = jnp.where(column_ids < row_ids, 1.0, 0.0).astype(jnp.bfloat16)
        gaps = jnp.dot(
            earlier, at_home_count.astype(jnp.bfloat16), preferred_element_type=jnp.float32
        ).astype(jnp.int32)
        packed = jnp.where(at_home, ABSENT, gaps * (ABSENT + 1) + label)
        moves = jnp.zeros(packed.shape, jnp.int32)
        bit = 0
        while 2**bit < count:
            marker = (ABSENT + 1) * 2**bit
            near = from_below(packed, 2**bit)
            taken = (near & marker) != 0
            left = (packed & marker) != 0
            packed = jnp.where(taken, near, jnp.where(left, ABSENT, packed))
            moves = jnp.where(taken, moves + 2**bit, moves)
            bit += 1
        most = count - jnp.min(jnp.sum(at_home_count, axis=0, keepdims=True)).astype(jnp.int32)
        return packed & ABSENT, moves, most

    inner_label, rim_label = split_rows(label_ref[...])
    inner_count = inner_label.shape[0]
    packed, moves, inner_most = compact(inner_label)
    packed_ref[0:inner_count, :] = packed
    moves_ref[0:inner_count, :] = moves
    packed, moves, rim_most = compact(rim_label)
    packed_ref[inner_count:, :] = packed
    moves_ref[inner_count:, :] = moves
    inner_steps = jnp.maximum((inner_most - INNER_ROWS + INNER_STEP - 1) // INNER_STEP, 0)
    rim_steps = jnp.maximum((rim_most - RIM_ROWS + RIM_STEP - 1) // RIM_STEP, 0)
    home_ref[2:3, :] = jnp.full((1, LANES), inner_steps.astype(jnp.float32))
    home_ref[3:4, :] = jnp.full((1, LANES), rim_steps.astype(jnp.float32))

    def look_up(first, rows):
        for start in range(0, rows, 4):
            places = [pl.ds(first + start + i, 1) for i in range(4)]
            group_label = jnp.concatenate([packed_ref[place, :] for place in places], axis=1)
            width = group_label.shape[1]
            group = one_hot(spread_rows((group_label >> 7).astype(jnp.float32)), 256)
            found = jnp.dot(
                turned_ref[...],
                jnp.concatenate([group, group], axis=0),
                preferred_element_type=jnp.float32,
            )
            hit = (group_label & 127) == lax.broadcasted_iota(jnp.int32, (LANES, width), 0)
            slot = jnp.sum(jnp.where(hit, found, 0.0), axis=0, keepdims=True)
            owner = jnp.floor(slot * (1.0 / LANES))
            lane = slot - owner * LANES
            for i, place in enumerate(places):
                device_ref[place, :] = owner[:, i * LANES : (i + 1) * LANES]
                lane_ref[place, :] = lane[:, i * LANES : (i + 1) * LANES]

    def more_inner(index, carry):
        look_up(INNER_ROWS + index * INNER_STEP, INNER_STEP)
        return carry

    def more_rim(index, carry):
        look_up(inner_count + RIM_ROWS + index * RIM_STEP, RIM_STEP)
        return carry

    look_up(0, INNER_ROWS)
    look_up(inner_count, RIM_ROWS)
    lax.fori_loop(0, inner_steps, more_inner, 0)
    lax.fori_loop(0, rim_steps, more_rim, 0)


def slots_of(owner_slot, label):
    count = label.size // LANES
    stack = jax.ShapeDtypeStruct((count, LANES), jnp.float32)
    return pl.pallas_call(
        slot_kernel,
        out_shape=(
            jax.ShapeDtypeStruct((count, LANES), jnp.int32),
            stack,
            stack,
            jax.ShapeDtypeStruct((8, LANES), jnp.float32),
        ),
        in_specs=[VMEM, VMEM],
        out_specs=(VMEM,) * 4,
        scratch_shapes=[
            pltpu.VMEM((256, LANES), jnp.float32),
            pltpu.VMEM((LANES, 512), jnp.bfloat16),
            pltpu.VMEM((count, LANES), jnp.int32),
        ],
        compiler_params=ROOMY,
        cost_estimate=pl.CostEstimate(
            flops=2 * 256 * 256 * label.size // 4, bytes_accessed=16 * label.size, transcendentals=0
        ),
        name="slot_lookup",
    )(owner_slot, label)


def below(x):
    return pltpu.roll(x, x.shape[0] - 1, 0)


def above(x):
    return pltpu.roll(x, 1, 0)


def rightward(x):
    return pltpu.roll(x, x.shape[1] - 1, 1)


def leftward(x):
    return pltpu.roll(x, 1, 1)


def window(depth, rough, adjoint):
    rows, columns = depth.shape
    conduct = jnp.where(rough > 0, rough_ref / jnp.where(rough > 0, rough, 1.0), 0.0)
    not_last = lax.broadcasted_iota(jnp.int32, (rows, columns), 1) < columns - 1
    under = below(conduct)
    beside = rightward(conduct)
    down_face = (conduct > 0) & (under > 0)
    side_face = (conduct > 0) & (beside > 0) & not_last
    down_weight = jnp.where(down_face, (0.5 * courant) * (conduct + under), 0.0)
    side_weight = jnp.where(side_face, (0.5 * courant) * (conduct + beside), 0.0)

    def steps(field):
        return below(field) - field, rightward(field) - field

    def advanced(field, down_step, side_step):
        down_flux = down_weight * down_step
        side_flux = side_weight * side_step
        return field + ((down_flux - above(down_flux)) + (side_flux - leftward(side_flux)))

    depth_steps = []
    for section in range(STEPS):
        depth_steps.append(steps(depth))
        if section < STEPS - 1:
            depth = advanced(depth, *depth_steps[-1])
    down_total = jnp.zeros((rows, columns), jnp.float32)
    side_total = jnp.zeros((rows, columns), jnp.float32)
    for section in reversed(range(STEPS)):
        down_step, side_step = steps(adjoint)
        down_total = down_total + depth_steps[section][0] * down_step
        side_total = side_total + depth_steps[section][1] * side_step
        adjoint = advanced(adjoint, down_step, side_step)
    down_total = jnp.where(down_face, down_total, 0.0)
    side_total = jnp.where(side_face, side_total, 0.0)
    total = (down_total + above(down_total)) + (side_total + leftward(side_total))
    return (0.5 * courant) * conduct * total, adjoint


def halves(x):
    upper = x.astype(jnp.bfloat16).astype(jnp.float32)
    return upper, x - upper


HOME_ROWS = 16


def zone_sums(rows):
    left = []
    right = []
    for device, lane, *values in rows:
        left.append(one_hot(spread_rows(device), 256))
        weights = [spread_rows(part) for part in values]
        right.append(jnp.concatenate(one_hot(spread_rows(lane), LANES, weights), axis=0))
    both = lax.dot_general(
        jnp.concatenate(left, axis=1),
        jnp.concatenate(right, axis=1),
        (((1,), (1,)), ((), ())),
        preferred_element_type=jnp.float32,
    )
    return jnp.concatenate(
        [
            both[:, 0:LANES] + both[:, LANES : 2 * LANES],
            both[:, 2 * LANES : 3 * LANES] + both[:, 3 * LANES :],
        ],
        axis=1,
    )


def pair_rows(upper, lower):
    width = upper.shape[1]
    pair = [jnp.broadcast_to(part, (8, width)) for part in (upper, lower)]
    return jnp.concatenate(pair, axis=0).astype(jnp.bfloat16)


def set_cells(cell_ref, offset, grad):
    cell_ref[0] = (offset >> 3).astype(jnp.float32)
    cell_ref[1] = (offset & 7).astype(jnp.float32)
    cell_ref[2], cell_ref[3] = halves(grad)
    cell_ref[4], cell_ref[5] = halves(grad * grad)


def home_products(cell_ref, first, count):
    zero = jnp.zeros((), jnp.bfloat16)
    width = cell_ref.shape[2]
    ids = lax.broadcasted_iota(jnp.int32, (16, width), 0)
    group_ids = ids.astype(jnp.float32).astype(jnp.bfloat16)
    within_ids = (ids & 7).astype(jnp.float32).astype(jnp.bfloat16)
    left = []
    right = []
    for step in range(count):
        row = slice(first + step, first + step + 1)
        group_hit = spread_rows(cell_ref[0, row, :]) == group_ids
        within_hit = spread_rows(cell_ref[1, row, :]) == within_ids
        left.append(jnp.where(group_hit, jnp.ones((), jnp.bfloat16), zero))
        weights = [
            pair_rows(cell_ref[2 + part, row, :], cell_ref[3 + part, row, :]) for part in (0, 2)
        ]
        right.append(jnp.concatenate([jnp.where(within_hit, w, zero) for w in weights], axis=0))
    return lax.dot_general(
        jnp.concatenate(left, axis=1),
        jnp.concatenate(right, axis=1),
        (((1,), (1,)), ((), ())),
        preferred_element_type=jnp.float32,
    )


def stray_rows(refs, first, start, count):
    device_ref, lane_ref, stray_ref = refs
    rows = []
    for step in range(count):
        slot = pl.ds(first + start + step, 1)
        value = pl.ds(start + step, 1)
        values = [stray_ref[part, value, :] for part in range(4)]
        rows.append((device_ref[slot, :], lane_ref[slot, :], *values))
    return rows


def inner_kernel(
    depth_ref,
    rough_ref_,
    seed_ref,
    label_ref,
    moves_ref,
    device_ref,
    lane_ref,
    home_ref,
    total_ref,
    adjoint_ref,
    products_ref,
    cell_ref,
    stray_ref,
):
    grad, adjoint = window(depth_ref[...], rough_ref_[...], seed_ref[...])
    adjoint_ref[...] = adjoint
    rows = grad.shape[0]
    inside = slice(RIM, rows - RIM)
    inner_grad, _ = split_rows(grad)
    set_strays(stray_ref, inner_grad, moves_ref[0 : inner_grad.shape[0], :])
    set_cells(cell_ref, (label_ref[...] - own_first_zone())[inside], grad[inside])
    home = home_products(cell_ref, 0, HOME_ROWS)
    for first in range(HOME_ROWS, rows - 2 * RIM, HOME_ROWS):
        home = home + home_products(cell_ref, first, HOME_ROWS)
    products_ref[...] = home
    refs = device_ref, lane_ref, stray_ref
    total_ref[...] = zone_sums(stray_rows(refs, 0, 0, INNER_ROWS))

    def more(index, carry):
        start = INNER_ROWS + index * INNER_STEP
        total_ref[...] += zone_sums(stray_rows(refs, 0, start, INNER_STEP))
        return carry

    lax.fori_loop(0, jnp.max(home_ref[2:3, :]).astype(jnp.int32), more, 0)


def inner_part(depth, rough, seed, label, *slots):
    inner_rows = depth.shape[0] - 2 * RIM
    return pl.pallas_call(
        inner_kernel,
        out_shape=(
            jax.ShapeDtypeStruct((256, 2 * LANES), jnp.float32),
            jax.ShapeDtypeStruct(depth.shape, jnp.float32),
            jax.ShapeDtypeStruct((16, 32), jnp.float32),
        ),
        in_specs=[VMEM] * (4 + len(slots)),
        out_specs=(VMEM,) * 3,
        scratch_shapes=[
            pltpu.VMEM((6, inner_rows, depth.shape[1]), jnp.float32),
            pltpu.VMEM((4, inner_rows * depth.shape[1] // LANES, LANES), jnp.float32),
        ],
        compiler_params=ROOMY,
        cost_estimate=pl.CostEstimate(
            flops=2 * 256 * 128 * depth.size, bytes_accessed=20 * depth.size, transcendentals=0
        ),
        name="inner_rows",
    )(depth, rough, seed, label, *slots)


def zone_kernel(
    depth_ref,
    rough_ref_,
    seed_ref,
    chip_ref,
    away_ref,
    inner_total_ref,
    inner_adjoint_ref,
    inner_home_ref,
    label_ref,
    moves_ref,
    device_ref,
    lane_ref,
    home_ref,
    own_ref,
    other_ref,
    adjoint_ref,
    total_ref,
    stray_ref,
    cell_ref,
):
    first_core = lax.axis_index("core") == 0
    chip_index, chips = lax.axis_index("chip"), lax.axis_size("chip")
    has_low = jnp.where(first_core & (chip_index == 0), 0.0, 1.0)
    has_high = jnp.where(first_core | (chip_index < chips - 1), 1.0, 0.0)
    rows = depth_ref.shape[0]
    near = RIM + HALO

    def rim(part, ref):
        halo = slice(part * HALO, (part + 1) * HALO)
        chip, away = chip_ref[halo, :], away_ref[halo, :]
        low = jnp.where(first_core, away, chip)
        high = jnp.where(first_core, chip, away)
        if part == 1:
            low, high = low * has_low, high * has_high
        return jnp.concatenate([low, ref[0:near, :], ref[rows - near : rows, :], high], axis=0)

    rim_grad, rim_adjoint = window(rim(0, depth_ref), rim(1, rough_ref_), rim(2, seed_ref))
    top = slice(HALO, HALO + RIM)
    bottom = slice(near + 2 * HALO, near + 2 * HALO + RIM)
    inside = slice(RIM, rows - RIM)
    adjoint_ref[...] = jnp.concatenate(
        [rim_adjoint[top], inner_adjoint_ref[inside, :], rim_adjoint[bottom]], axis=0
    )
    offset = label_ref[...] - own_first_zone()
    set_cells(
        cell_ref,
        jnp.concatenate([offset[:RIM], offset[rows - RIM :]], axis=0),
        jnp.concatenate([rim_grad[top], rim_grad[bottom]], axis=0),
    )
    first = moves_ref.shape[0] - stray_ref.shape[1]
    rim_grad = jnp.concatenate([rim_grad[top], rim_grad[bottom]], axis=0)
    set_strays(stray_ref, stacked(rim_grad), moves_ref[first:, :])
    home = inner_home_ref[...] + home_products(cell_ref, 0, 2 * RIM)
    part = lax.broadcasted_iota(jnp.int32, (32, 2 * LANES), 0)
    zone = lax.broadcasted_iota(jnp.int32, (32, 2 * LANES), 1)
    chosen = ((part & 7) == (zone & 7)) & ((part >= 16) == (zone >= LANES))
    home = jnp.dot(
        home,
        jnp.where(chosen, 1.0, 0.0),
        precision=lax.Precision.HIGHEST,
        preferred_element_type=jnp.float32,
    )
    group = lax.broadcasted_iota(jnp.int32, (16, 2 * LANES), 0)
    zone = lax.broadcasted_iota(jnp.int32, (16, 2 * LANES), 1)
    home = jnp.sum(jnp.where(((zone >> 3) & 15) == group, home, 0.0), axis=0, keepdims=True)
    home = halves(home[:, :LANES]) + halves(home[:, LANES:])

    refs = device_ref, lane_ref, stray_ref
    total_ref[...] = inner_total_ref[...] + zone_sums(
        stray_rows(refs, first, 0, RIM_ROWS) + [(home_ref[0:1, :], home_ref[1:2, :], *home)]
    )

    def more(index, carry):
        start = RIM_ROWS + index * RIM_STEP
        total_ref[...] += zone_sums(stray_rows(refs, first, start, RIM_STEP))
        return carry

    lax.fori_loop(0, jnp.max(home_ref[3:4, :]).astype(jnp.int32), more, 0)
    own_ref[...] = total_ref[0:LANES, :]
    other_ref[...] = total_ref[LANES:, :]


def zone_partials(depth, *others):
    half = jax.ShapeDtypeStruct((LANES, 2 * LANES), jnp.float32)
    return pl.pallas_call(
        zone_kernel,
        out_shape=(half, half, jax.ShapeDtypeStruct(depth.shape, jnp.float32)),
        in_specs=[VMEM] * (1 + len(others)),
        out_specs=(VMEM,) * 3,
        scratch_shapes=[
            pltpu.VMEM((256, 2 * LANES), jnp.float32),
            pltpu.VMEM((4, 2 * RIM * depth.shape[1] // LANES, LANES), jnp.float32),
            pltpu.VMEM((6, 2 * RIM, depth.shape[1]), jnp.float32),
        ],
        compiler_params=ROOMY,
        name="zone_partials",
    )(depth, *others)


def parcel_kernel(own_ref, other_ref, edge_ref, out_ref):
    chips = own_ref.shape[0]
    sums = own_ref[...] + other_ref[...]
    out_ref[pl.ds(0, chips, stride=4), :] = sums[:, :LANES]
    out_ref[pl.ds(1, chips, stride=4), :] = sums[:, LANES:]
    for part in range(2):
        edge = jnp.broadcast_to(edge_ref[part : part + 1, :], (chips, LANES))
        out_ref[pl.ds(2 + part, chips, stride=4), :] = edge


def parcels(own, other, edge):
    return pl.pallas_call(
        parcel_kernel,
        out_shape=jax.ShapeDtypeStruct((4 * own.shape[0], LANES), jnp.float32),
        in_specs=[VMEM] * 3,
        out_specs=VMEM,
        compiler_params=ROOMY,
        name="parcels",
    )(own, other, edge)


def result_kernel(arrived_ref, rate_ref, push_ref, grad_ref, curve_ref, reach_ref):
    rows = arrived_ref.shape[0]
    sums = arrived_ref[0:8, :]
    for start in range(8, rows, 8):
        sums = sums + arrived_ref[start : start + 8, :]
    grad_ref[...] = (sums[0:1, :] + sums[4:5, :])[:, :SPAN]
    curve_ref[...] = (sums[1:2, :] + sums[5:6, :])[:, :SPAN]
    basin, chip = lax.axis_index("basin"), lax.axis_index("chip")
    basins, chips = lax.axis_size("basin"), lax.axis_size("chip")
    incoming = jnp.zeros((1, LANES), jnp.float32)
    for hop in reversed(range(1, basins)):
        there = jnp.where(basin + hop < basins, 1.0, 0.0)
        row = 4 * (jnp.minimum(basin + hop, basins - 1) * chips + chip)
        rate = arrived_ref[pl.ds(row + 2, 1), :]
        push = arrived_ref[pl.ds(row + 3, 1), :]
        incoming = there * (rate * incoming + push)
    reach_ref[...] = rate_ref[...] * incoming + push_ref[...]


def results(arrived, rate, push):
    zone = jax.ShapeDtypeStruct((1, SPAN), jnp.float32)
    return pl.pallas_call(
        result_kernel,
        out_shape=(zone, zone, jax.ShapeDtypeStruct(rate.shape, jnp.float32)),
        in_specs=[VMEM] * 3,
        out_specs=(VMEM,) * 3,
        compiler_params=ROOMY,
        name="results",
    )(arrived, rate, push)


def reach_kernel(adjoint_ref, cell_ref, keep_ref, forcing_ref, rate_ref, push_ref, edge_ref):
    rows, columns = adjoint_ref.shape
    upper, lower = halves(adjoint_ref[...])
    table = jnp.concatenate([upper, lower], axis=0).astype(jnp.bfloat16)
    reaches = cell_ref.shape[0]
    width = cell_ref.shape[1]
    values = []
    for reach in range(0, reaches, 4):
        cells = jnp.concatenate([cell_ref[reach + i : reach + i + 1, :] for i in range(4)], axis=1)
        column = (cells & (columns - 1)).astype(jnp.float32)
        hot = jnp.concatenate(
            [one_hot(spread_rows(column - part * 256.0), 256) for part in range(columns // 256)],
            axis=0,
        )
        picked = jnp.dot(table, hot, preferred_element_type=jnp.float32)
        picked = picked[:rows] + picked[rows:]
        row_hit = (cells >> 9) == lax.broadcasted_iota(jnp.int32, (rows, 4 * width), 0)
        found = jnp.sum(jnp.where(row_hit, picked, 0.0), axis=0, keepdims=True)
        values += [found[:, i * width : (i + 1) * width] for i in range(4)]
    rate = jnp.ones((1, width), jnp.float32)
    push = jnp.zeros((1, width), jnp.float32)
    for reach in reversed(range(reaches)):
        keep = keep_ref[reach : reach + 1, :]
        push = keep * push + (forcing_ref[reach : reach + 1, :] + levee_gain * values[reach])
        rate = keep * rate
        rate_ref[reach : reach + 1, :] = rate
        push_ref[reach : reach + 1, :] = push
    edge_ref[0:1, :] = rate
    edge_ref[1:2, :] = push


def reach_maps(adjoint, cells, keep, forcing):
    shape = jax.ShapeDtypeStruct(cells.shape, jnp.float32)
    return pl.pallas_call(
        reach_kernel,
        out_shape=(shape, shape, jax.ShapeDtypeStruct((2, cells.shape[1]), jnp.float32)),
        in_specs=[VMEM] * 4,
        out_specs=(VMEM, VMEM, VMEM),
        compiler_params=ROOMY,
        name="reach_maps",
    )(adjoint, cells, keep, forcing)


def swapped(value):
    return lax.ppermute(value, "core", [(0, 1), (1, 0)])


def exchanged_away(value):
    tiles = lax.axis_size("chip") * lax.axis_size("core")
    pairs = [(i, (i + 1 if i % 2 else i - 1) % tiles) for i in range(tiles)]
    return lax.ppermute(value, ("chip", "core"), pairs)


def per_device(
    depth_start, roughness, depth_seed, zone_label, owner_slot, retention, forcing, levee_cell
):
    depth, rough, seed, label, owner_slot, to_chip, to_away = fetched(
        depth_start[0],
        roughness[0],
        depth_seed[0],
        zone_label[0],
        owner_slot.reshape(-1, LANES),
    )
    from_away = exchanged_away(to_away)
    moves, device, lane, home = slots_of(owner_slot, label)
    to_chip, home = lax.optimization_barrier((to_chip, home))
    from_chip = swapped(to_chip)
    inner = inner_part(depth, rough, seed, label, moves, device, lane, home)
    own, other, adjoint = zone_partials(
        depth, rough, seed, from_chip, from_away, *inner, label, moves, device, lane, home
    )
    other = swapped(other)
    rate, push, edge = reach_maps(adjoint, levee_cell, retention, forcing)
    sent = parcels(own, other, edge).reshape(-1, 4, LANES)
    arrived = lax.all_to_all(sent, ("basin", "chip"), 0, 0, tiled=True)
    grad, curve, reach_adjoint = results(arrived.reshape(-1, LANES), rate, push)
    return (grad.reshape(-1), curve.reshape(-1), reach_adjoint)


def solution(mesh):
    basins, tiles = mesh.devices.shape
    fine = jax.sharding.Mesh(
        mesh.devices.reshape(basins, tiles // 2, 2), ("basin", "chip", "core")
    )
    tile = ("chip", "core")
    cells = P("basin", tile, None)
    reaches = P("basin", tile)
    zones = P(("basin", "chip", "core"))
    return jax.shard_map(
        per_device,
        mesh=fine,
        in_specs=(cells, cells, cells, cells, P(), reaches, reaches, reaches),
        out_specs=(zones, zones, reaches),
        check_vma=False,
    )
```

```python
import functools

import jax
import jax.numpy as jnp
from jax import lax
from jax.experimental import pallas as pl
from jax.experimental.pallas import tpu as pltpu
from jax.sharding import PartitionSpec as P

STEPS = 4
HALO = STEPS
SPAN = 127
LANES = 128

courant = 0.24
rough_ref = 0.025
levee_gain = 0.1

VMEM = pl.BlockSpec(memory_space=pltpu.VMEM)
ROOMY = pltpu.CompilerParams(vmem_limit_bytes=48 * 2**20)


def iota_bf16(shape, offset=0):
    ids = lax.broadcasted_iota(jnp.int32, shape, len(shape) - 2)
    if len(shape) == 3:
        ids = ids + shape[1] * lax.broadcasted_iota(jnp.int32, shape, 0)
    return (ids + offset).astype(jnp.float32).astype(jnp.bfloat16)


def spread_rows(row):
    return jnp.broadcast_to(row, (16, row.shape[1])).astype(jnp.bfloat16)


def one_hot(spread, count, weights=None):
    width = spread.shape[1]
    ids = iota_bf16((count // 16, 16, width))
    hit = spread[None] == ids
    zero = jnp.zeros((), jnp.bfloat16)
    if weights is None:
        return jnp.where(hit, jnp.ones((), jnp.bfloat16), zero).reshape(count, width)
    return [jnp.where(hit, w[None], zero).reshape(count, width) for w in weights]


def stacked(x):
    return jnp.concatenate(
        [x[:, start : start + LANES] for start in range(0, x.shape[1], LANES)], axis=0
    )


def from_below(x, distance):
    return pltpu.roll(x, x.shape[0] - distance, 0)


HBM = pl.BlockSpec(memory_space=pltpu.HBM)


FETCH = pltpu.CompilerParams(vmem_limit_bytes=55800000)


def front_kernel(*refs):
    count = (len(refs) - 3) // 2
    sources, kept = refs[:count], refs[count : 2 * count]
    chip_ref, away_ref, arrived = refs[2 * count :]
    copies = [
        pltpu.make_async_copy(source, place, arrived.at[index])
        for index, (source, place) in enumerate(zip(sources, kept))
    ]
    for copy in copies:
        copy.start()
    first_core = lax.axis_index("core") == 0
    for part in range(3):
        copies[part].wait()
        ref = kept[part]
        rows = slice(part * HALO, (part + 1) * HALO)
        top = ref[0:HALO, :]
        bottom = ref[ref.shape[0] - HALO :, :]
        chip_ref[rows, :] = jnp.where(first_core, bottom, top)
        away_ref[rows, :] = jnp.where(first_core, top, bottom)
    for copy in copies[3:]:
        copy.wait()


def fetched(*arrays):
    edge = jax.ShapeDtypeStruct((3 * HALO, arrays[0].shape[1]), jnp.float32)
    kept = tuple(jax.ShapeDtypeStruct(x.shape, x.dtype) for x in arrays)
    return pl.pallas_call(
        front_kernel,
        out_shape=kept + (edge, edge),
        in_specs=[HBM] * len(arrays),
        out_specs=(VMEM,) * (len(arrays) + 2),
        scratch_shapes=[pltpu.SemaphoreType.DMA((len(arrays),))],
        compiler_params=FETCH,
        name="fetch_and_edges",
    )(*arrays)


ABSENT = 2**15 - 1


def split_rows(x):
    rows = x.shape[0]
    inner = stacked(x[RIM : rows - RIM])
    rim = stacked(jnp.concatenate([x[:RIM], x[rows - RIM :]], axis=0))
    return inner, rim


def compacted(x, moves):
    bit = 0
    while 2**bit < x.shape[0]:
        x = jnp.where((moves & 2**bit) != 0, from_below(x, 2**bit), x)
        bit += 1
    return x


def set_strays(stray_ref, grad, moves):
    grad = compacted(grad, moves)
    stray_ref[0], stray_ref[1] = halves(grad)
    stray_ref[2], stray_ref[3] = halves(grad * grad)


def own_first_zone():
    chip = lax.axis_index("basin") * lax.axis_size("chip") + lax.axis_index("chip")
    return (chip * lax.axis_size("core") + lax.axis_index("core")) * SPAN


INNER_ROWS = 40
RIM_ROWS = 20
INNER_STEP = 4
RIM_STEP = 4
RIM = 2 * HALO


def slot_kernel(
    owner_ref,
    label_ref,
    moves_ref,
    device_ref,
    lane_ref,
    home_ref,
    table_ref,
    turned_ref,
    packed_ref,
):
    first_zone = own_first_zone()
    core = lax.axis_index("core").astype(jnp.float32)
    table_ref[...] = jnp.full(table_ref.shape, 256.0 * SPAN, jnp.float32)
    table_ref[0 : owner_ref.shape[0], :] = owner_ref[...].astype(jnp.float32)

    def placed(slots):
        owners = jnp.floor((slots + 0.5) * (1.0 / SPAN))
        lanes = slots - owners * SPAN
        chips = jnp.floor(owners * 0.5)
        swapped = jnp.abs((owners - 2.0 * chips) - core)
        basins, per_basin = lax.axis_size("basin"), lax.axis_size("chip")
        basin = jnp.floor(chips * (1.0 / per_basin))
        place = (chips - per_basin * basin) * basins + basin
        return jnp.where(owners < 256.0, place + 128.0 * swapped, 256.0), lanes

    owners, lanes = placed(jnp.transpose(table_ref[...]))
    turned_ref[:, 0:256] = (owners * LANES).astype(jnp.bfloat16)
    turned_ref[:, 256:512] = lanes.astype(jnp.bfloat16)

    home_row = first_zone // LANES
    shift = first_zone % LANES
    back = jnp.where(shift == 0, 0, LANES - shift)
    pair = table_ref[pl.ds(home_row, 1), :], table_ref[pl.ds(home_row + 1, 1), :]
    pair = [pltpu.roll(jnp.broadcast_to(row, (8, LANES)), back, 1) for row in pair]
    spot = lax.broadcasted_iota(jnp.int32, (8, LANES), 1)
    home = jnp.where(spot + shift < LANES, pair[0], pair[1])
    home_device, home_lane = placed(jnp.where(spot < SPAN, home, 256.0 * SPAN))
    home_ref[0:1, :] = home_device[0:1]
    home_ref[1:2, :] = home_lane[0:1]

    def compact(label):
        count = label.shape[0]
        offset = label - first_zone
        at_home = (offset >= 0) & (offset < SPAN)
        at_home_count = jnp.where(at_home, 1.0, 0.0)
        row_ids = lax.broadcasted_iota(jnp.int32, (count, count), 0)
        column_ids = lax.broadcasted_iota(jnp.int32, (count, count), 1)
        earlier = jnp.where(column_ids < row_ids, 1.0, 0.0).astype(jnp.bfloat16)
        gaps = jnp.dot(
            earlier, at_home_count.astype(jnp.bfloat16), preferred_element_type=jnp.float32
        ).astype(jnp.int32)
        packed = jnp.where(at_home, ABSENT, gaps * (ABSENT + 1) + label)
        moves = jnp.zeros(packed.shape, jnp.int32)
        bit = 0
        while 2**bit < count:
            marker = (ABSENT + 1) * 2**bit
            near = from_below(packed, 2**bit)
            taken = (near & marker) != 0
            left = (packed & marker) != 0
            packed = jnp.where(taken, near, jnp.where(left, ABSENT, packed))
            moves = jnp.where(taken, moves + 2**bit, moves)
            bit += 1
        most = count - jnp.min(jnp.sum(at_home_count, axis=0, keepdims=True)).astype(jnp.int32)
        return packed & ABSENT, moves, most

    inner_label, rim_label = split_rows(label_ref[...])
    inner_count = inner_label.shape[0]
    packed, moves, inner_most = compact(inner_label)
    packed_ref[0:inner_count, :] = packed
    moves_ref[0:inner_count, :] = moves
    packed, moves, rim_most = compact(rim_label)
    packed_ref[inner_count:, :] = packed
    moves_ref[inner_count:, :] = moves
    inner_steps = jnp.maximum((inner_most - INNER_ROWS + INNER_STEP - 1) // INNER_STEP, 0)
    rim_steps = jnp.maximum((rim_most - RIM_ROWS + RIM_STEP - 1) // RIM_STEP, 0)
    home_ref[2:3, :] = jnp.full((1, LANES), inner_steps.astype(jnp.float32))
    home_ref[3:4, :] = jnp.full((1, LANES), rim_steps.astype(jnp.float32))

    def look_up(first, rows):
        for start in range(0, rows, 4):
            places = [pl.ds(first + start + i, 1) for i in range(4)]
            group_label = jnp.concatenate([packed_ref[place, :] for place in places], axis=1)
            width = group_label.shape[1]
            group = one_hot(spread_rows((group_label >> 7).astype(jnp.float32)), 256)
            found = jnp.dot(
                turned_ref[...],
                jnp.concatenate([group, group], axis=0),
                preferred_element_type=jnp.float32,
            )
            hit = (group_label & 127) == lax.broadcasted_iota(jnp.int32, (LANES, width), 0)
            slot = jnp.sum(jnp.where(hit, found, 0.0), axis=0, keepdims=True)
            owner = jnp.floor(slot * (1.0 / LANES))
            lane = slot - owner * LANES
            for i, place in enumerate(places):
                device_ref[place, :] = owner[:, i * LANES : (i + 1) * LANES]
                lane_ref[place, :] = lane[:, i * LANES : (i + 1) * LANES]

    def more_inner(index, carry):
        look_up(INNER_ROWS + index * INNER_STEP, INNER_STEP)
        return carry

    def more_rim(index, carry):
        look_up(inner_count + RIM_ROWS + index * RIM_STEP, RIM_STEP)
        return carry

    look_up(0, INNER_ROWS)
    look_up(inner_count, RIM_ROWS)
    lax.fori_loop(0, inner_steps, more_inner, 0)
    lax.fori_loop(0, rim_steps, more_rim, 0)


def slots_of(owner_slot, label):
    count = label.size // LANES
    stack = jax.ShapeDtypeStruct((count, LANES), jnp.float32)
    return pl.pallas_call(
        slot_kernel,
        out_shape=(
            jax.ShapeDtypeStruct((count, LANES), jnp.int32),
            stack,
            stack,
            jax.ShapeDtypeStruct((8, LANES), jnp.float32),
        ),
        in_specs=[VMEM, VMEM],
        out_specs=(VMEM,) * 4,
        scratch_shapes=[
            pltpu.VMEM((256, LANES), jnp.float32),
            pltpu.VMEM((LANES, 512), jnp.bfloat16),
            pltpu.VMEM((count, LANES), jnp.int32),
        ],
        compiler_params=ROOMY,
        cost_estimate=pl.CostEstimate(
            flops=2 * 256 * 256 * label.size // 4, bytes_accessed=16 * label.size, transcendentals=0
        ),
        name="slot_lookup",
    )(owner_slot, label)


def below(x):
    return pltpu.roll(x, x.shape[0] - 1, 0)


def above(x):
    return pltpu.roll(x, 1, 0)


def rightward(x):
    return pltpu.roll(x, x.shape[1] - 1, 1)


def leftward(x):
    return pltpu.roll(x, 1, 1)


def window(depth, rough, adjoint):
    rows, columns = depth.shape
    conduct = jnp.where(rough > 0, rough_ref / jnp.where(rough > 0, rough, 1.0), 0.0)
    not_last = lax.broadcasted_iota(jnp.int32, (rows, columns), 1) < columns - 1
    under = below(conduct)
    beside = rightward(conduct)
    down_face = (conduct > 0) & (under > 0)
    side_face = (conduct > 0) & (beside > 0) & not_last
    down_weight = jnp.where(down_face, (0.5 * courant) * (conduct + under), 0.0)
    side_weight = jnp.where(side_face, (0.5 * courant) * (conduct + beside), 0.0)

    def steps(field):
        return below(field) - field, rightward(field) - field

    def advanced(field, down_step, side_step):
        down_flux = down_weight * down_step
        side_flux = side_weight * side_step
        return field + ((down_flux - above(down_flux)) + (side_flux - leftward(side_flux)))

    depth_steps = []
    for section in range(STEPS):
        depth_steps.append(steps(depth))
        if section < STEPS - 1:
            depth = advanced(depth, *depth_steps[-1])
    down_total = jnp.zeros((rows, columns), jnp.float32)
    side_total = jnp.zeros((rows, columns), jnp.float32)
    for section in reversed(range(STEPS)):
        down_step, side_step = steps(adjoint)
        down_total = down_total + depth_steps[section][0] * down_step
        side_total = side_total + depth_steps[section][1] * side_step
        adjoint = advanced(adjoint, down_step, side_step)
    down_total = jnp.where(down_face, down_total, 0.0)
    side_total = jnp.where(side_face, side_total, 0.0)
    total = (down_total + above(down_total)) + (side_total + leftward(side_total))
    return (0.5 * courant) * conduct * total, adjoint


def halves(x):
    upper = x.astype(jnp.bfloat16).astype(jnp.float32)
    return upper, x - upper


HOME_ROWS = 16


def zone_sums(rows):
    left = []
    right = []
    for device, lane, *values in rows:
        left.append(one_hot(spread_rows(device), 256))
        weights = [spread_rows(part) for part in values]
        right.append(jnp.concatenate(one_hot(spread_rows(lane), LANES, weights), axis=0))
    both = lax.dot_general(
        jnp.concatenate(left, axis=1),
        jnp.concatenate(right, axis=1),
        (((1,), (1,)), ((), ())),
        preferred_element_type=jnp.float32,
    )
    return jnp.concatenate(
        [
            both[:, 0:LANES] + both[:, LANES : 2 * LANES],
            both[:, 2 * LANES : 3 * LANES] + both[:, 3 * LANES :],
        ],
        axis=1,
    )


def pair_rows(upper, lower):
    width = upper.shape[1]
    pair = [jnp.broadcast_to(part, (8, width)) for part in (upper, lower)]
    return jnp.concatenate(pair, axis=0).astype(jnp.bfloat16)


def set_cells(cell_ref, offset, grad):
    cell_ref[0] = (offset >> 3).astype(jnp.float32)
    cell_ref[1] = (offset & 7).astype(jnp.float32)
    cell_ref[2], cell_ref[3] = halves(grad)
    cell_ref[4], cell_ref[5] = halves(grad * grad)


def home_products(cell_ref, first, count):
    zero = jnp.zeros((), jnp.bfloat16)
    width = cell_ref.shape[2]
    ids = lax.broadcasted_iota(jnp.int32, (16, width), 0)
    group_ids = ids.astype(jnp.float32).astype(jnp.bfloat16)
    within_ids = (ids & 7).astype(jnp.float32).astype(jnp.bfloat16)
    left = []
    right = []
    for step in range(count):
        row = slice(first + step, first + step + 1)
        group_hit = spread_rows(cell_ref[0, row, :]) == group_ids
        within_hit = spread_rows(cell_ref[1, row, :]) == within_ids
        left.append(jnp.where(group_hit, jnp.ones((), jnp.bfloat16), zero))
        weights = [
            pair_rows(cell_ref[2 + part, row, :], cell_ref[3 + part, row, :]) for part in (0, 2)
        ]
        right.append(jnp.concatenate([jnp.where(within_hit, w, zero) for w in weights], axis=0))
    return lax.dot_general(
        jnp.concatenate(left, axis=1),
        jnp.concatenate(right, axis=1),
        (((1,), (1,)), ((), ())),
        preferred_element_type=jnp.float32,
    )


def stray_rows(refs, first, start, count):
    device_ref, lane_ref, stray_ref = refs
    rows = []
    for step in range(count):
        slot = pl.ds(first + start + step, 1)
        value = pl.ds(start + step, 1)
        values = [stray_ref[part, value, :] for part in range(4)]
        rows.append((device_ref[slot, :], lane_ref[slot, :], *values))
    return rows


def inner_kernel(
    depth_ref,
    rough_ref_,
    seed_ref,
    label_ref,
    moves_ref,
    device_ref,
    lane_ref,
    home_ref,
    total_ref,
    adjoint_ref,
    products_ref,
    cell_ref,
    stray_ref,
):
    grad, adjoint = window(depth_ref[...], rough_ref_[...], seed_ref[...])
    adjoint_ref[...] = adjoint
    rows = grad.shape[0]
    inside = slice(RIM, rows - RIM)
    inner_grad, _ = split_rows(grad)
    set_strays(stray_ref, inner_grad, moves_ref[0 : inner_grad.shape[0], :])
    set_cells(cell_ref, (label_ref[...] - own_first_zone())[inside], grad[inside])
    home = home_products(cell_ref, 0, HOME_ROWS)
    for first in range(HOME_ROWS, rows - 2 * RIM, HOME_ROWS):
        home = home + home_products(cell_ref, first, HOME_ROWS)
    products_ref[...] = home
    refs = device_ref, lane_ref, stray_ref
    total_ref[...] = zone_sums(stray_rows(refs, 0, 0, INNER_ROWS))

    def more(index, carry):
        start = INNER_ROWS + index * INNER_STEP
        total_ref[...] += zone_sums(stray_rows(refs, 0, start, INNER_STEP))
        return carry

    lax.fori_loop(0, jnp.max(home_ref[2:3, :]).astype(jnp.int32), more, 0)


def inner_part(depth, rough, seed, label, *slots):
    inner_rows = depth.shape[0] - 2 * RIM
    return pl.pallas_call(
        inner_kernel,
        out_shape=(
            jax.ShapeDtypeStruct((256, 2 * LANES), jnp.float32),
            jax.ShapeDtypeStruct(depth.shape, jnp.float32),
            jax.ShapeDtypeStruct((16, 32), jnp.float32),
        ),
        in_specs=[VMEM] * (4 + len(slots)),
        out_specs=(VMEM,) * 3,
        scratch_shapes=[
            pltpu.VMEM((6, inner_rows, depth.shape[1]), jnp.float32),
            pltpu.VMEM((4, inner_rows * depth.shape[1] // LANES, LANES), jnp.float32),
        ],
        compiler_params=ROOMY,
        cost_estimate=pl.CostEstimate(
            flops=2 * 256 * 128 * depth.size, bytes_accessed=20 * depth.size, transcendentals=0
        ),
        name="inner_rows",
    )(depth, rough, seed, label, *slots)


def zone_kernel(
    depth_ref,
    rough_ref_,
    seed_ref,
    chip_ref,
    away_ref,
    inner_total_ref,
    inner_adjoint_ref,
    inner_home_ref,
    label_ref,
    moves_ref,
    device_ref,
    lane_ref,
    home_ref,
    own_ref,
    other_ref,
    adjoint_ref,
    total_ref,
    stray_ref,
    cell_ref,
):
    first_core = lax.axis_index("core") == 0
    chip_index, chips = lax.axis_index("chip"), lax.axis_size("chip")
    has_low = jnp.where(first_core & (chip_index == 0), 0.0, 1.0)
    has_high = jnp.where(first_core | (chip_index < chips - 1), 1.0, 0.0)
    rows = depth_ref.shape[0]
    near = RIM + HALO

    def rim(part, ref):
        halo = slice(part * HALO, (part + 1) * HALO)
        chip, away = chip_ref[halo, :], away_ref[halo, :]
        low = jnp.where(first_core, away, chip)
        high = jnp.where(first_core, chip, away)
        if part == 1:
            low, high = low * has_low, high * has_high
        return jnp.concatenate([low, ref[0:near, :], ref[rows - near : rows, :], high], axis=0)

    rim_grad, rim_adjoint = window(rim(0, depth_ref), rim(1, rough_ref_), rim(2, seed_ref))
    top = slice(HALO, HALO + RIM)
    bottom = slice(near + 2 * HALO, near + 2 * HALO + RIM)
    inside = slice(RIM, rows - RIM)
    adjoint_ref[...] = jnp.concatenate(
        [rim_adjoint[top], inner_adjoint_ref[inside, :], rim_adjoint[bottom]], axis=0
    )
    offset = label_ref[...] - own_first_zone()
    set_cells(
        cell_ref,
        jnp.concatenate([offset[:RIM], offset[rows - RIM :]], axis=0),
        jnp.concatenate([rim_grad[top], rim_grad[bottom]], axis=0),
    )
    first = moves_ref.shape[0] - stray_ref.shape[1]
    rim_grad = jnp.concatenate([rim_grad[top], rim_grad[bottom]], axis=0)
    set_strays(stray_ref, stacked(rim_grad), moves_ref[first:, :])
    home = inner_home_ref[...] + home_products(cell_ref, 0, 2 * RIM)
    part = lax.broadcasted_iota(jnp.int32, (32, 2 * LANES), 0)
    zone = lax.broadcasted_iota(jnp.int32, (32, 2 * LANES), 1)
    chosen = ((part & 7) == (zone & 7)) & ((part >= 16) == (zone >= LANES))
    home = jnp.dot(
        home,
        jnp.where(chosen, 1.0, 0.0),
        precision=lax.Precision.HIGHEST,
        preferred_element_type=jnp.float32,
    )
    group = lax.broadcasted_iota(jnp.int32, (16, 2 * LANES), 0)
    zone = lax.broadcasted_iota(jnp.int32, (16, 2 * LANES), 1)
    home = jnp.sum(jnp.where(((zone >> 3) & 15) == group, home, 0.0), axis=0, keepdims=True)
    home = halves(home[:, :LANES]) + halves(home[:, LANES:])

    refs = device_ref, lane_ref, stray_ref
    total_ref[...] = inner_total_ref[...] + zone_sums(
        stray_rows(refs, first, 0, RIM_ROWS) + [(home_ref[0:1, :], home_ref[1:2, :], *home)]
    )

    def more(index, carry):
        start = RIM_ROWS + index * RIM_STEP
        total_ref[...] += zone_sums(stray_rows(refs, first, start, RIM_STEP))
        return carry

    lax.fori_loop(0, jnp.max(home_ref[3:4, :]).astype(jnp.int32), more, 0)
    own_ref[...] = total_ref[0:LANES, :]
    other_ref[...] = total_ref[LANES:, :]


def zone_partials(depth, *others):
    half = jax.ShapeDtypeStruct((LANES, 2 * LANES), jnp.float32)
    return pl.pallas_call(
        zone_kernel,
        out_shape=(half, half, jax.ShapeDtypeStruct(depth.shape, jnp.float32)),
        in_specs=[VMEM] * (1 + len(others)),
        out_specs=(VMEM,) * 3,
        scratch_shapes=[
            pltpu.VMEM((256, 2 * LANES), jnp.float32),
            pltpu.VMEM((4, 2 * RIM * depth.shape[1] // LANES, LANES), jnp.float32),
            pltpu.VMEM((6, 2 * RIM, depth.shape[1]), jnp.float32),
        ],
        compiler_params=ROOMY,
        name="zone_partials",
    )(depth, *others)


def parcel_kernel(own_ref, other_ref, edge_ref, out_ref):
    chips = own_ref.shape[0]
    sums = own_ref[...] + other_ref[...]
    out_ref[pl.ds(0, chips, stride=4), :] = sums[:, :LANES]
    out_ref[pl.ds(1, chips, stride=4), :] = sums[:, LANES:]
    for part in range(2):
        edge = jnp.broadcast_to(edge_ref[part : part + 1, :], (chips, LANES))
        out_ref[pl.ds(2 + part, chips, stride=4), :] = edge


def parcels(own, other, edge):
    return pl.pallas_call(
        parcel_kernel,
        out_shape=jax.ShapeDtypeStruct((4 * own.shape[0], LANES), jnp.float32),
        in_specs=[VMEM] * 3,
        out_specs=VMEM,
        compiler_params=ROOMY,
        name="parcels",
    )(own, other, edge)


def result_kernel(arrived_ref, rate_ref, push_ref, grad_ref, curve_ref, reach_ref):
    rows = arrived_ref.shape[0]
    sums = arrived_ref[0:8, :]
    for start in range(8, rows, 8):
        sums = sums + arrived_ref[start : start + 8, :]
    grad_ref[...] = (sums[0:1, :] + sums[4:5, :])[:, :SPAN]
    curve_ref[...] = (sums[1:2, :] + sums[5:6, :])[:, :SPAN]
    basin, chip = lax.axis_index("basin"), lax.axis_index("chip")
    basins = lax.axis_size("basin")
    incoming = jnp.zeros((1, LANES), jnp.float32)
    for hop in reversed(range(1, basins)):
        there = jnp.where(basin + hop < basins, 1.0, 0.0)
        row = 4 * (chip * basins + jnp.minimum(basin + hop, basins - 1))
        rate = arrived_ref[pl.ds(row + 2, 1), :]
        push = arrived_ref[pl.ds(row + 3, 1), :]
        incoming = there * (rate * incoming + push)
    reach_ref[...] = rate_ref[...] * incoming + push_ref[...]


def results(arrived, rate, push):
    zone = jax.ShapeDtypeStruct((1, SPAN), jnp.float32)
    return pl.pallas_call(
        result_kernel,
        out_shape=(zone, zone, jax.ShapeDtypeStruct(rate.shape, jnp.float32)),
        in_specs=[VMEM] * 3,
        out_specs=(VMEM,) * 3,
        compiler_params=ROOMY,
        name="results",
    )(arrived, rate, push)


def reach_kernel(adjoint_ref, cell_ref, keep_ref, forcing_ref, rate_ref, push_ref, edge_ref):
    rows, columns = adjoint_ref.shape
    upper, lower = halves(adjoint_ref[...])
    table = jnp.concatenate([upper, lower], axis=0).astype(jnp.bfloat16)
    reaches = cell_ref.shape[0]
    width = cell_ref.shape[1]
    values = []
    for reach in range(0, reaches, 4):
        cells = jnp.concatenate([cell_ref[reach + i : reach + i + 1, :] for i in range(4)], axis=1)
        column = (cells & (columns - 1)).astype(jnp.float32)
        hot = jnp.concatenate(
            [one_hot(spread_rows(column - part * 256.0), 256) for part in range(columns // 256)],
            axis=0,
        )
        picked = jnp.dot(table, hot, preferred_element_type=jnp.float32)
        picked = picked[:rows] + picked[rows:]
        row_hit = (cells >> 9) == lax.broadcasted_iota(jnp.int32, (rows, 4 * width), 0)
        found = jnp.sum(jnp.where(row_hit, picked, 0.0), axis=0, keepdims=True)
        values += [found[:, i * width : (i + 1) * width] for i in range(4)]
    rate = jnp.ones((1, width), jnp.float32)
    push = jnp.zeros((1, width), jnp.float32)
    for reach in reversed(range(reaches)):
        keep = keep_ref[reach : reach + 1, :]
        push = keep * push + (forcing_ref[reach : reach + 1, :] + levee_gain * values[reach])
        rate = keep * rate
        rate_ref[reach : reach + 1, :] = rate
        push_ref[reach : reach + 1, :] = push
    edge_ref[0:1, :] = rate
    edge_ref[1:2, :] = push


def reach_maps(adjoint, cells, keep, forcing):
    shape = jax.ShapeDtypeStruct(cells.shape, jnp.float32)
    return pl.pallas_call(
        reach_kernel,
        out_shape=(shape, shape, jax.ShapeDtypeStruct((2, cells.shape[1]), jnp.float32)),
        in_specs=[VMEM] * 4,
        out_specs=(VMEM, VMEM, VMEM),
        compiler_params=ROOMY,
        name="reach_maps",
    )(adjoint, cells, keep, forcing)


def swapped(value):
    return lax.ppermute(value, "core", [(0, 1), (1, 0)])


def exchanged_away(value):
    tiles = lax.axis_size("chip") * lax.axis_size("core")
    pairs = [(i, (i + 1 if i % 2 else i - 1) % tiles) for i in range(tiles)]
    return lax.ppermute(value, ("chip", "core"), pairs)


def per_device(
    depth_start, roughness, depth_seed, zone_label, owner_slot, retention, forcing, levee_cell
):
    depth, rough, seed, label, owner_slot, to_chip, to_away = fetched(
        depth_start[0],
        roughness[0],
        depth_seed[0],
        zone_label[0],
        owner_slot.reshape(-1, LANES),
    )
    from_away = exchanged_away(to_away)
    moves, device, lane, home = slots_of(owner_slot, label)
    to_chip, home = lax.optimization_barrier((to_chip, home))
    from_chip = swapped(to_chip)
    inner = inner_part(depth, rough, seed, label, moves, device, lane, home)
    own, other, adjoint = zone_partials(
        depth, rough, seed, from_chip, from_away, *inner, label, moves, device, lane, home
    )
    other = swapped(other)
    rate, push, edge = reach_maps(adjoint, levee_cell, retention, forcing)
    sent = parcels(own, other, edge).reshape(-1, 4, LANES)
    arrived = lax.all_to_all(sent, ("chip", "basin"), 0, 0, tiled=True)
    grad, curve, reach_adjoint = results(arrived.reshape(-1, LANES), rate, push)
    return (grad.reshape(-1), curve.reshape(-1), reach_adjoint)


def solution(mesh):
    basins, tiles = mesh.devices.shape
    fine = jax.sharding.Mesh(
        mesh.devices.reshape(basins, tiles // 2, 2), ("basin", "chip", "core")
    )
    tile = ("chip", "core")
    cells = P("basin", tile, None)
    reaches = P("basin", tile)
    zones = P(("basin", "chip", "core"))
    return jax.shard_map(
        per_device,
        mesh=fine,
        in_specs=(cells, cells, cells, cells, P(), reaches, reaches, reaches),
        out_specs=(zones, zones, reaches),
        check_vma=False,
    )
```

```python
import functools

import jax
import jax.numpy as jnp
from jax import lax
from jax.experimental import pallas as pl
from jax.experimental.pallas import tpu as pltpu
from jax.sharding import PartitionSpec as P

STEPS = 4
HALO = STEPS
SPAN = 127
LANES = 128

courant = 0.24
rough_ref = 0.025
levee_gain = 0.1

VMEM = pl.BlockSpec(memory_space=pltpu.VMEM)
ROOMY = pltpu.CompilerParams(vmem_limit_bytes=48 * 2**20)


def iota_bf16(shape, offset=0):
    ids = lax.broadcasted_iota(jnp.int32, shape, len(shape) - 2)
    if len(shape) == 3:
        ids = ids + shape[1] * lax.broadcasted_iota(jnp.int32, shape, 0)
    return (ids + offset).astype(jnp.float32).astype(jnp.bfloat16)


def spread_rows(row):
    return jnp.broadcast_to(row, (16, row.shape[1])).astype(jnp.bfloat16)


def one_hot(spread, count, weights=None):
    width = spread.shape[1]
    ids = iota_bf16((count // 16, 16, width))
    hit = spread[None] == ids
    zero = jnp.zeros((), jnp.bfloat16)
    if weights is None:
        return jnp.where(hit, jnp.ones((), jnp.bfloat16), zero).reshape(count, width)
    return [jnp.where(hit, w[None], zero).reshape(count, width) for w in weights]


def stacked(x):
    return jnp.concatenate(
        [x[:, start : start + LANES] for start in range(0, x.shape[1], LANES)], axis=0
    )


def from_below(x, distance):
    return pltpu.roll(x, x.shape[0] - distance, 0)


HBM = pl.BlockSpec(memory_space=pltpu.HBM)


FETCH = pltpu.CompilerParams(vmem_limit_bytes=55800000)


def front_kernel(*refs):
    count = (len(refs) - 3) // 2
    sources, kept = refs[:count], refs[count : 2 * count]
    chip_ref, away_ref, arrived = refs[2 * count :]
    copies = [
        pltpu.make_async_copy(source, place, arrived.at[index])
        for index, (source, place) in enumerate(zip(sources, kept))
    ]
    for copy in copies:
        copy.start()
    first_core = lax.axis_index("core") == 0
    for part in range(3):
        copies[part].wait()
        ref = kept[part]
        rows = slice(part * HALO, (part + 1) * HALO)
        top = ref[0:HALO, :]
        bottom = ref[ref.shape[0] - HALO :, :]
        chip_ref[rows, :] = jnp.where(first_core, bottom, top)
        away_ref[rows, :] = jnp.where(first_core, top, bottom)
    for copy in copies[3:]:
        copy.wait()


def fetched(*arrays):
    edge = jax.ShapeDtypeStruct((3 * HALO, arrays[0].shape[1]), jnp.float32)
    kept = tuple(jax.ShapeDtypeStruct(x.shape, x.dtype) for x in arrays)
    return pl.pallas_call(
        front_kernel,
        out_shape=kept + (edge, edge),
        in_specs=[HBM] * len(arrays),
        out_specs=(VMEM,) * (len(arrays) + 2),
        scratch_shapes=[pltpu.SemaphoreType.DMA((len(arrays),))],
        compiler_params=FETCH,
        name="fetch_and_edges",
    )(*arrays)


ABSENT = 2**15 - 1


def split_rows(x):
    rows = x.shape[0]
    inner = stacked(x[RIM : rows - RIM])
    rim = stacked(jnp.concatenate([x[:RIM], x[rows - RIM :]], axis=0))
    return inner, rim


def compacted(x, moves):
    bit = 0
    while 2**bit < x.shape[0]:
        x = jnp.where((moves & 2**bit) != 0, from_below(x, 2**bit), x)
        bit += 1
    return x


def set_strays(stray_ref, grad, moves):
    grad = compacted(grad, moves)
    stray_ref[0], stray_ref[1] = halves(grad)
    stray_ref[2], stray_ref[3] = halves(grad * grad)


def chip_place():
    count = lax.axis_size("y") * lax.axis_size("z")
    return lax.axis_index("y") * lax.axis_size("z") + lax.axis_index("z"), count


def own_first_zone():
    index, count = chip_place()
    chip = lax.axis_index("basin") * count + index
    return (chip * lax.axis_size("core") + lax.axis_index("core")) * SPAN


INNER_ROWS = 40
RIM_ROWS = 20
INNER_STEP = 4
RIM_STEP = 4
RIM = 2 * HALO


def slot_kernel(
    owner_ref,
    label_ref,
    moves_ref,
    device_ref,
    lane_ref,
    home_ref,
    table_ref,
    turned_ref,
    packed_ref,
):
    first_zone = own_first_zone()
    core = lax.axis_index("core").astype(jnp.float32)
    table_ref[...] = jnp.full(table_ref.shape, 256.0 * SPAN, jnp.float32)
    table_ref[0 : owner_ref.shape[0], :] = owner_ref[...].astype(jnp.float32)

    def placed(slots):
        owners = jnp.floor((slots + 0.5) * (1.0 / SPAN))
        lanes = slots - owners * SPAN
        chips = jnp.floor(owners * 0.5)
        swapped = jnp.abs((owners - 2.0 * chips) - core)
        basins, height, depth = (lax.axis_size(axis) for axis in ("basin", "y", "z"))
        line = jnp.floor(chips * (1.0 / depth))
        basin = jnp.floor(chips * (1.0 / (height * depth)))
        place = ((chips - depth * line) * height + (line - height * basin)) * basins + basin
        return jnp.where(owners < 256.0, place + 128.0 * swapped, 256.0), lanes

    owners, lanes = placed(jnp.transpose(table_ref[...]))
    turned_ref[:, 0:256] = (owners * LANES).astype(jnp.bfloat16)
    turned_ref[:, 256:512] = lanes.astype(jnp.bfloat16)

    home_row = first_zone // LANES
    shift = first_zone % LANES
    back = jnp.where(shift == 0, 0, LANES - shift)
    pair = table_ref[pl.ds(home_row, 1), :], table_ref[pl.ds(home_row + 1, 1), :]
    pair = [pltpu.roll(jnp.broadcast_to(row, (8, LANES)), back, 1) for row in pair]
    spot = lax.broadcasted_iota(jnp.int32, (8, LANES), 1)
    home = jnp.where(spot + shift < LANES, pair[0], pair[1])
    home_device, home_lane = placed(jnp.where(spot < SPAN, home, 256.0 * SPAN))
    home_ref[0:1, :] = home_device[0:1]
    home_ref[1:2, :] = home_lane[0:1]

    def compact(label):
        count = label.shape[0]
        offset = label - first_zone
        at_home = (offset >= 0) & (offset < SPAN)
        at_home_count = jnp.where(at_home, 1.0, 0.0)
        row_ids = lax.broadcasted_iota(jnp.int32, (count, count), 0)
        column_ids = lax.broadcasted_iota(jnp.int32, (count, count), 1)
        earlier = jnp.where(column_ids < row_ids, 1.0, 0.0).astype(jnp.bfloat16)
        gaps = jnp.dot(
            earlier, at_home_count.astype(jnp.bfloat16), preferred_element_type=jnp.float32
        ).astype(jnp.int32)
        packed = jnp.where(at_home, ABSENT, gaps * (ABSENT + 1) + label)
        moves = jnp.zeros(packed.shape, jnp.int32)
        bit = 0
        while 2**bit < count:
            marker = (ABSENT + 1) * 2**bit
            near = from_below(packed, 2**bit)
            taken = (near & marker) != 0
            left = (packed & marker) != 0
            packed = jnp.where(taken, near, jnp.where(left, ABSENT, packed))
            moves = jnp.where(taken, moves + 2**bit, moves)
            bit += 1
        most = count - jnp.min(jnp.sum(at_home_count, axis=0, keepdims=True)).astype(jnp.int32)
        return packed & ABSENT, moves, most

    inner_label, rim_label = split_rows(label_ref[...])
    inner_count = inner_label.shape[0]
    packed, moves, inner_most = compact(inner_label)
    packed_ref[0:inner_count, :] = packed
    moves_ref[0:inner_count, :] = moves
    packed, moves, rim_most = compact(rim_label)
    packed_ref[inner_count:, :] = packed
    moves_ref[inner_count:, :] = moves
    inner_steps = jnp.maximum((inner_most - INNER_ROWS + INNER_STEP - 1) // INNER_STEP, 0)
    rim_steps = jnp.maximum((rim_most - RIM_ROWS + RIM_STEP - 1) // RIM_STEP, 0)
    home_ref[2:3, :] = jnp.full((1, LANES), inner_steps.astype(jnp.float32))
    home_ref[3:4, :] = jnp.full((1, LANES), rim_steps.astype(jnp.float32))

    def look_up(first, rows):
        for start in range(0, rows, 4):
            places = [pl.ds(first + start + i, 1) for i in range(4)]
            group_label = jnp.concatenate([packed_ref[place, :] for place in places], axis=1)
            width = group_label.shape[1]
            group = one_hot(spread_rows((group_label >> 7).astype(jnp.float32)), 256)
            found = jnp.dot(
                turned_ref[...],
                jnp.concatenate([group, group], axis=0),
                preferred_element_type=jnp.float32,
            )
            hit = (group_label & 127) == lax.broadcasted_iota(jnp.int32, (LANES, width), 0)
            slot = jnp.sum(jnp.where(hit, found, 0.0), axis=0, keepdims=True)
            owner = jnp.floor(slot * (1.0 / LANES))
            lane = slot - owner * LANES
            for i, place in enumerate(places):
                device_ref[place, :] = owner[:, i * LANES : (i + 1) * LANES]
                lane_ref[place, :] = lane[:, i * LANES : (i + 1) * LANES]

    def more_inner(index, carry):
        look_up(INNER_ROWS + index * INNER_STEP, INNER_STEP)
        return carry

    def more_rim(index, carry):
        look_up(inner_count + RIM_ROWS + index * RIM_STEP, RIM_STEP)
        return carry

    look_up(0, INNER_ROWS)
    look_up(inner_count, RIM_ROWS)
    lax.fori_loop(0, inner_steps, more_inner, 0)
    lax.fori_loop(0, rim_steps, more_rim, 0)


def slots_of(owner_slot, label):
    count = label.size // LANES
    stack = jax.ShapeDtypeStruct((count, LANES), jnp.float32)
    return pl.pallas_call(
        slot_kernel,
        out_shape=(
            jax.ShapeDtypeStruct((count, LANES), jnp.int32),
            stack,
            stack,
            jax.ShapeDtypeStruct((8, LANES), jnp.float32),
        ),
        in_specs=[VMEM, VMEM],
        out_specs=(VMEM,) * 4,
        scratch_shapes=[
            pltpu.VMEM((256, LANES), jnp.float32),
            pltpu.VMEM((LANES, 512), jnp.bfloat16),
            pltpu.VMEM((count, LANES), jnp.int32),
        ],
        compiler_params=ROOMY,
        cost_estimate=pl.CostEstimate(
            flops=2 * 256 * 256 * label.size // 4, bytes_accessed=16 * label.size, transcendentals=0
        ),
        name="slot_lookup",
    )(owner_slot, label)


def below(x):
    return pltpu.roll(x, x.shape[0] - 1, 0)


def above(x):
    return pltpu.roll(x, 1, 0)


def rightward(x):
    return pltpu.roll(x, x.shape[1] - 1, 1)


def leftward(x):
    return pltpu.roll(x, 1, 1)


def window(depth, rough, adjoint):
    rows, columns = depth.shape
    conduct = jnp.where(rough > 0, rough_ref / jnp.where(rough > 0, rough, 1.0), 0.0)
    not_last = lax.broadcasted_iota(jnp.int32, (rows, columns), 1) < columns - 1
    under = below(conduct)
    beside = rightward(conduct)
    down_face = (conduct > 0) & (under > 0)
    side_face = (conduct > 0) & (beside > 0) & not_last
    down_weight = jnp.where(down_face, (0.5 * courant) * (conduct + under), 0.0)
    side_weight = jnp.where(side_face, (0.5 * courant) * (conduct + beside), 0.0)

    def steps(field):
        return below(field) - field, rightward(field) - field

    def advanced(field, down_step, side_step):
        down_flux = down_weight * down_step
        side_flux = side_weight * side_step
        return field + ((down_flux - above(down_flux)) + (side_flux - leftward(side_flux)))

    depth_steps = []
    for section in range(STEPS):
        depth_steps.append(steps(depth))
        if section < STEPS - 1:
            depth = advanced(depth, *depth_steps[-1])
    down_total = jnp.zeros((rows, columns), jnp.float32)
    side_total = jnp.zeros((rows, columns), jnp.float32)
    for section in reversed(range(STEPS)):
        down_step, side_step = steps(adjoint)
        down_total = down_total + depth_steps[section][0] * down_step
        side_total = side_total + depth_steps[section][1] * side_step
        adjoint = advanced(adjoint, down_step, side_step)
    down_total = jnp.where(down_face, down_total, 0.0)
    side_total = jnp.where(side_face, side_total, 0.0)
    total = (down_total + above(down_total)) + (side_total + leftward(side_total))
    return (0.5 * courant) * conduct * total, adjoint


def halves(x):
    upper = x.astype(jnp.bfloat16).astype(jnp.float32)
    return upper, x - upper


HOME_ROWS = 16


def zone_sums(rows):
    left = []
    right = []
    for device, lane, *values in rows:
        left.append(one_hot(spread_rows(device), 256))
        weights = [spread_rows(part) for part in values]
        right.append(jnp.concatenate(one_hot(spread_rows(lane), LANES, weights), axis=0))
    both = lax.dot_general(
        jnp.concatenate(left, axis=1),
        jnp.concatenate(right, axis=1),
        (((1,), (1,)), ((), ())),
        preferred_element_type=jnp.float32,
    )
    return jnp.concatenate(
        [
            both[:, 0:LANES] + both[:, LANES : 2 * LANES],
            both[:, 2 * LANES : 3 * LANES] + both[:, 3 * LANES :],
        ],
        axis=1,
    )


def pair_rows(upper, lower):
    width = upper.shape[1]
    pair = [jnp.broadcast_to(part, (8, width)) for part in (upper, lower)]
    return jnp.concatenate(pair, axis=0).astype(jnp.bfloat16)


def set_cells(cell_ref, offset, grad):
    cell_ref[0] = (offset >> 3).astype(jnp.float32)
    cell_ref[1] = (offset & 7).astype(jnp.float32)
    cell_ref[2], cell_ref[3] = halves(grad)
    cell_ref[4], cell_ref[5] = halves(grad * grad)


def home_products(cell_ref, first, count):
    zero = jnp.zeros((), jnp.bfloat16)
    width = cell_ref.shape[2]
    ids = lax.broadcasted_iota(jnp.int32, (16, width), 0)
    group_ids = ids.astype(jnp.float32).astype(jnp.bfloat16)
    within_ids = (ids & 7).astype(jnp.float32).astype(jnp.bfloat16)
    left = []
    right = []
    for step in range(count):
        row = slice(first + step, first + step + 1)
        group_hit = spread_rows(cell_ref[0, row, :]) == group_ids
        within_hit = spread_rows(cell_ref[1, row, :]) == within_ids
        left.append(jnp.where(group_hit, jnp.ones((), jnp.bfloat16), zero))
        weights = [
            pair_rows(cell_ref[2 + part, row, :], cell_ref[3 + part, row, :]) for part in (0, 2)
        ]
        right.append(jnp.concatenate([jnp.where(within_hit, w, zero) for w in weights], axis=0))
    return lax.dot_general(
        jnp.concatenate(left, axis=1),
        jnp.concatenate(right, axis=1),
        (((1,), (1,)), ((), ())),
        preferred_element_type=jnp.float32,
    )


def stray_rows(refs, first, start, count):
    device_ref, lane_ref, stray_ref = refs
    rows = []
    for step in range(count):
        slot = pl.ds(first + start + step, 1)
        value = pl.ds(start + step, 1)
        values = [stray_ref[part, value, :] for part in range(4)]
        rows.append((device_ref[slot, :], lane_ref[slot, :], *values))
    return rows


def inner_kernel(
    depth_ref,
    rough_ref_,
    seed_ref,
    label_ref,
    moves_ref,
    device_ref,
    lane_ref,
    home_ref,
    total_ref,
    adjoint_ref,
    products_ref,
    cell_ref,
    stray_ref,
):
    grad, adjoint = window(depth_ref[...], rough_ref_[...], seed_ref[...])
    adjoint_ref[...] = adjoint
    rows = grad.shape[0]
    inside = slice(RIM, rows - RIM)
    inner_grad, _ = split_rows(grad)
    set_strays(stray_ref, inner_grad, moves_ref[0 : inner_grad.shape[0], :])
    set_cells(cell_ref, (label_ref[...] - own_first_zone())[inside], grad[inside])
    home = home_products(cell_ref, 0, HOME_ROWS)
    for first in range(HOME_ROWS, rows - 2 * RIM, HOME_ROWS):
        home = home + home_products(cell_ref, first, HOME_ROWS)
    products_ref[...] = home
    refs = device_ref, lane_ref, stray_ref
    total_ref[...] = zone_sums(stray_rows(refs, 0, 0, INNER_ROWS))

    def more(index, carry):
        start = INNER_ROWS + index * INNER_STEP
        total_ref[...] += zone_sums(stray_rows(refs, 0, start, INNER_STEP))
        return carry

    lax.fori_loop(0, jnp.max(home_ref[2:3, :]).astype(jnp.int32), more, 0)


def inner_part(depth, rough, seed, label, *slots):
    inner_rows = depth.shape[0] - 2 * RIM
    return pl.pallas_call(
        inner_kernel,
        out_shape=(
            jax.ShapeDtypeStruct((256, 2 * LANES), jnp.float32),
            jax.ShapeDtypeStruct(depth.shape, jnp.float32),
            jax.ShapeDtypeStruct((16, 32), jnp.float32),
        ),
        in_specs=[VMEM] * (4 + len(slots)),
        out_specs=(VMEM,) * 3,
        scratch_shapes=[
            pltpu.VMEM((6, inner_rows, depth.shape[1]), jnp.float32),
            pltpu.VMEM((4, inner_rows * depth.shape[1] // LANES, LANES), jnp.float32),
        ],
        compiler_params=ROOMY,
        cost_estimate=pl.CostEstimate(
            flops=2 * 256 * 128 * depth.size, bytes_accessed=20 * depth.size, transcendentals=0
        ),
        name="inner_rows",
    )(depth, rough, seed, label, *slots)


def zone_kernel(
    depth_ref,
    rough_ref_,
    seed_ref,
    chip_ref,
    away_ref,
    inner_total_ref,
    inner_adjoint_ref,
    inner_home_ref,
    label_ref,
    moves_ref,
    device_ref,
    lane_ref,
    home_ref,
    own_ref,
    other_ref,
    adjoint_ref,
    total_ref,
    stray_ref,
    cell_ref,
):
    first_core = lax.axis_index("core") == 0
    chip_index, chips = chip_place()
    has_low = jnp.where(first_core & (chip_index == 0), 0.0, 1.0)
    has_high = jnp.where(first_core | (chip_index < chips - 1), 1.0, 0.0)
    rows = depth_ref.shape[0]
    near = RIM + HALO

    def rim(part, ref):
        halo = slice(part * HALO, (part + 1) * HALO)
        chip, away = chip_ref[halo, :], away_ref[halo, :]
        low = jnp.where(first_core, away, chip)
        high = jnp.where(first_core, chip, away)
        if part == 1:
            low, high = low * has_low, high * has_high
        return jnp.concatenate([low, ref[0:near, :], ref[rows - near : rows, :], high], axis=0)

    rim_grad, rim_adjoint = window(rim(0, depth_ref), rim(1, rough_ref_), rim(2, seed_ref))
    top = slice(HALO, HALO + RIM)
    bottom = slice(near + 2 * HALO, near + 2 * HALO + RIM)
    inside = slice(RIM, rows - RIM)
    adjoint_ref[...] = jnp.concatenate(
        [rim_adjoint[top], inner_adjoint_ref[inside, :], rim_adjoint[bottom]], axis=0
    )
    offset = label_ref[...] - own_first_zone()
    set_cells(
        cell_ref,
        jnp.concatenate([offset[:RIM], offset[rows - RIM :]], axis=0),
        jnp.concatenate([rim_grad[top], rim_grad[bottom]], axis=0),
    )
    first = moves_ref.shape[0] - stray_ref.shape[1]
    rim_grad = jnp.concatenate([rim_grad[top], rim_grad[bottom]], axis=0)
    set_strays(stray_ref, stacked(rim_grad), moves_ref[first:, :])
    home = inner_home_ref[...] + home_products(cell_ref, 0, 2 * RIM)
    part = lax.broadcasted_iota(jnp.int32, (32, 2 * LANES), 0)
    zone = lax.broadcasted_iota(jnp.int32, (32, 2 * LANES), 1)
    chosen = ((part & 7) == (zone & 7)) & ((part >= 16) == (zone >= LANES))
    home = jnp.dot(
        home,
        jnp.where(chosen, 1.0, 0.0),
        precision=lax.Precision.HIGHEST,
        preferred_element_type=jnp.float32,
    )
    group = lax.broadcasted_iota(jnp.int32, (16, 2 * LANES), 0)
    zone = lax.broadcasted_iota(jnp.int32, (16, 2 * LANES), 1)
    home = jnp.sum(jnp.where(((zone >> 3) & 15) == group, home, 0.0), axis=0, keepdims=True)
    home = halves(home[:, :LANES]) + halves(home[:, LANES:])

    refs = device_ref, lane_ref, stray_ref
    total_ref[...] = inner_total_ref[...] + zone_sums(
        stray_rows(refs, first, 0, RIM_ROWS) + [(home_ref[0:1, :], home_ref[1:2, :], *home)]
    )

    def more(index, carry):
        start = RIM_ROWS + index * RIM_STEP
        total_ref[...] += zone_sums(stray_rows(refs, first, start, RIM_STEP))
        return carry

    lax.fori_loop(0, jnp.max(home_ref[3:4, :]).astype(jnp.int32), more, 0)
    own_ref[...] = total_ref[0:LANES, :]
    other_ref[...] = total_ref[LANES:, :]


def zone_partials(depth, *others):
    half = jax.ShapeDtypeStruct((LANES, 2 * LANES), jnp.float32)
    return pl.pallas_call(
        zone_kernel,
        out_shape=(half, half, jax.ShapeDtypeStruct(depth.shape, jnp.float32)),
        in_specs=[VMEM] * (1 + len(others)),
        out_specs=(VMEM,) * 3,
        scratch_shapes=[
            pltpu.VMEM((256, 2 * LANES), jnp.float32),
            pltpu.VMEM((4, 2 * RIM * depth.shape[1] // LANES, LANES), jnp.float32),
            pltpu.VMEM((6, 2 * RIM, depth.shape[1]), jnp.float32),
        ],
        compiler_params=ROOMY,
        name="zone_partials",
    )(depth, *others)


def parcel_kernel(own_ref, other_ref, edge_ref, out_ref):
    chips = own_ref.shape[0]
    sums = own_ref[...] + other_ref[...]
    out_ref[pl.ds(0, chips, stride=4), :] = sums[:, :LANES]
    out_ref[pl.ds(1, chips, stride=4), :] = sums[:, LANES:]
    for part in range(2):
        edge = jnp.broadcast_to(edge_ref[part : part + 1, :], (chips, LANES))
        out_ref[pl.ds(2 + part, chips, stride=4), :] = edge


def parcels(own, other, edge):
    return pl.pallas_call(
        parcel_kernel,
        out_shape=jax.ShapeDtypeStruct((4 * own.shape[0], LANES), jnp.float32),
        in_specs=[VMEM] * 3,
        out_specs=VMEM,
        compiler_params=ROOMY,
        name="parcels",
    )(own, other, edge)


def result_kernel(arrived_ref, rate_ref, push_ref, grad_ref, curve_ref, reach_ref):
    rows = arrived_ref.shape[0]
    sums = arrived_ref[0:8, :]
    for start in range(8, rows, 8):
        sums = sums + arrived_ref[start : start + 8, :]
    grad_ref[...] = (sums[0:1, :] + sums[4:5, :])[:, :SPAN]
    curve_ref[...] = (sums[1:2, :] + sums[5:6, :])[:, :SPAN]
    basin = lax.axis_index("basin")
    chip = lax.axis_index("z") * lax.axis_size("y") + lax.axis_index("y")
    basins = lax.axis_size("basin")
    incoming = jnp.zeros((1, LANES), jnp.float32)
    for hop in reversed(range(1, basins)):
        there = jnp.where(basin + hop < basins, 1.0, 0.0)
        row = 4 * (chip * basins + jnp.minimum(basin + hop, basins - 1))
        rate = arrived_ref[pl.ds(row + 2, 1), :]
        push = arrived_ref[pl.ds(row + 3, 1), :]
        incoming = there * (rate * incoming + push)
    reach_ref[...] = rate_ref[...] * incoming + push_ref[...]


def results(arrived, rate, push):
    zone = jax.ShapeDtypeStruct((1, SPAN), jnp.float32)
    return pl.pallas_call(
        result_kernel,
        out_shape=(zone, zone, jax.ShapeDtypeStruct(rate.shape, jnp.float32)),
        in_specs=[VMEM] * 3,
        out_specs=(VMEM,) * 3,
        compiler_params=ROOMY,
        name="results",
    )(arrived, rate, push)


def reach_kernel(adjoint_ref, cell_ref, keep_ref, forcing_ref, rate_ref, push_ref, edge_ref):
    rows, columns = adjoint_ref.shape
    upper, lower = halves(adjoint_ref[...])
    table = jnp.concatenate([upper, lower], axis=0).astype(jnp.bfloat16)
    reaches = cell_ref.shape[0]
    width = cell_ref.shape[1]
    values = []
    for reach in range(0, reaches, 4):
        cells = jnp.concatenate([cell_ref[reach + i : reach + i + 1, :] for i in range(4)], axis=1)
        column = (cells & (columns - 1)).astype(jnp.float32)
        hot = jnp.concatenate(
            [one_hot(spread_rows(column - part * 256.0), 256) for part in range(columns // 256)],
            axis=0,
        )
        picked = jnp.dot(table, hot, preferred_element_type=jnp.float32)
        picked = picked[:rows] + picked[rows:]
        row_hit = (cells >> 9) == lax.broadcasted_iota(jnp.int32, (rows, 4 * width), 0)
        found = jnp.sum(jnp.where(row_hit, picked, 0.0), axis=0, keepdims=True)
        values += [found[:, i * width : (i + 1) * width] for i in range(4)]
    rate = jnp.ones((1, width), jnp.float32)
    push = jnp.zeros((1, width), jnp.float32)
    for reach in reversed(range(reaches)):
        keep = keep_ref[reach : reach + 1, :]
        push = keep * push + (forcing_ref[reach : reach + 1, :] + levee_gain * values[reach])
        rate = keep * rate
        rate_ref[reach : reach + 1, :] = rate
        push_ref[reach : reach + 1, :] = push
    edge_ref[0:1, :] = rate
    edge_ref[1:2, :] = push


def reach_maps(adjoint, cells, keep, forcing):
    shape = jax.ShapeDtypeStruct(cells.shape, jnp.float32)
    return pl.pallas_call(
        reach_kernel,
        out_shape=(shape, shape, jax.ShapeDtypeStruct((2, cells.shape[1]), jnp.float32)),
        in_specs=[VMEM] * 4,
        out_specs=(VMEM, VMEM, VMEM),
        compiler_params=ROOMY,
        name="reach_maps",
    )(adjoint, cells, keep, forcing)


def swapped(value):
    return lax.ppermute(value, "core", [(0, 1), (1, 0)])


def exchanged_away(value):
    tiles = chip_place()[1] * lax.axis_size("core")
    pairs = [(i, (i + 1 if i % 2 else i - 1) % tiles) for i in range(tiles)]
    return lax.ppermute(value, ("y", "z", "core"), pairs)


def per_device(
    depth_start, roughness, depth_seed, zone_label, owner_slot, retention, forcing, levee_cell
):
    depth, rough, seed, label, owner_slot, to_chip, to_away = fetched(
        depth_start[0],
        roughness[0],
        depth_seed[0],
        zone_label[0],
        owner_slot.reshape(-1, LANES),
    )
    from_away = exchanged_away(to_away)
    moves, device, lane, home = slots_of(owner_slot, label)
    to_chip, home = lax.optimization_barrier((to_chip, home))
    from_chip = swapped(to_chip)
    inner = inner_part(depth, rough, seed, label, moves, device, lane, home)
    own, other, adjoint = zone_partials(
        depth, rough, seed, from_chip, from_away, *inner, label, moves, device, lane, home
    )
    other = swapped(other)
    rate, push, edge = reach_maps(adjoint, levee_cell, retention, forcing)
    sent = parcels(own, other, edge).reshape(-1, 4, LANES)
    arrived = lax.all_to_all(sent, ("z", "y", "basin"), 0, 0, tiled=True)
    grad, curve, reach_adjoint = results(arrived.reshape(-1, LANES), rate, push)
    return (grad.reshape(-1), curve.reshape(-1), reach_adjoint)


def solution(mesh):
    basins, tiles = mesh.devices.shape
    fine = jax.sharding.Mesh(
        mesh.devices.reshape(basins, tiles // 16, 8, 2), ("basin", "y", "z", "core")
    )
    tile = ("y", "z", "core")
    cells = P("basin", tile, None)
    reaches = P("basin", tile)
    zones = P(("basin", "y", "z", "core"))
    return jax.shard_map(
        per_device,
        mesh=fine,
        in_specs=(cells, cells, cells, cells, P(), reaches, reaches, reaches),
        out_specs=(zones, zones, reaches),
        check_vma=False,
    )
```

```python
import functools

import jax
import jax.numpy as jnp
from jax import lax
from jax.experimental import pallas as pl
from jax.experimental.pallas import tpu as pltpu
from jax.sharding import PartitionSpec as P

STEPS = 4
HALO = STEPS
SPAN = 127
LANES = 128

courant = 0.24
rough_ref = 0.025
levee_gain = 0.1

VMEM = pl.BlockSpec(memory_space=pltpu.VMEM)
ROOMY = pltpu.CompilerParams(vmem_limit_bytes=48 * 2**20)


def iota_bf16(shape, offset=0):
    ids = lax.broadcasted_iota(jnp.int32, shape, len(shape) - 2)
    if len(shape) == 3:
        ids = ids + shape[1] * lax.broadcasted_iota(jnp.int32, shape, 0)
    return (ids + offset).astype(jnp.float32).astype(jnp.bfloat16)


def spread_rows(row):
    return jnp.broadcast_to(row, (16, row.shape[1])).astype(jnp.bfloat16)


def one_hot(spread, count, weights=None):
    width = spread.shape[1]
    ids = iota_bf16((count // 16, 16, width))
    hit = spread[None] == ids
    zero = jnp.zeros((), jnp.bfloat16)
    if weights is None:
        return jnp.where(hit, jnp.ones((), jnp.bfloat16), zero).reshape(count, width)
    return [jnp.where(hit, w[None], zero).reshape(count, width) for w in weights]


def stacked(x):
    return jnp.concatenate(
        [x[:, start : start + LANES] for start in range(0, x.shape[1], LANES)], axis=0
    )


def from_below(x, distance):
    return pltpu.roll(x, x.shape[0] - distance, 0)


HBM = pl.BlockSpec(memory_space=pltpu.HBM)


FETCH = pltpu.CompilerParams(vmem_limit_bytes=55800000)


def front_kernel(*refs):
    count = (len(refs) - 3) // 2
    sources, kept = refs[:count], refs[count : 2 * count]
    chip_ref, away_ref, arrived = refs[2 * count :]
    copies = [
        pltpu.make_async_copy(source, place, arrived.at[index])
        for index, (source, place) in enumerate(zip(sources, kept))
    ]
    for copy in copies:
        copy.start()
    first_core = lax.axis_index("core") == 0
    for part in range(3):
        copies[part].wait()
        ref = kept[part]
        rows = slice(part * HALO, (part + 1) * HALO)
        top = ref[0:HALO, :]
        bottom = ref[ref.shape[0] - HALO :, :]
        chip_ref[rows, :] = jnp.where(first_core, bottom, top)
        away_ref[rows, :] = jnp.where(first_core, top, bottom)
    for copy in copies[3:]:
        copy.wait()


def fetched(*arrays):
    edge = jax.ShapeDtypeStruct((3 * HALO, arrays[0].shape[1]), jnp.float32)
    kept = tuple(jax.ShapeDtypeStruct(x.shape, x.dtype) for x in arrays)
    return pl.pallas_call(
        front_kernel,
        out_shape=kept + (edge, edge),
        in_specs=[HBM] * len(arrays),
        out_specs=(VMEM,) * (len(arrays) + 2),
        scratch_shapes=[pltpu.SemaphoreType.DMA((len(arrays),))],
        compiler_params=FETCH,
        name="fetch_and_edges",
    )(*arrays)


ABSENT = 2**15 - 1


def split_rows(x):
    rows = x.shape[0]
    inner = stacked(x[RIM : rows - RIM])
    rim = stacked(jnp.concatenate([x[:RIM], x[rows - RIM :]], axis=0))
    return inner, rim


def compacted(x, moves):
    bit = 0
    while 2**bit < x.shape[0]:
        x = jnp.where((moves & 2**bit) != 0, from_below(x, 2**bit), x)
        bit += 1
    return x


def set_strays(stray_ref, grad, moves):
    grad = compacted(grad, moves)
    stray_ref[0], stray_ref[1] = halves(grad)
    stray_ref[2], stray_ref[3] = halves(grad * grad)


def own_first_zone():
    chip = lax.axis_index("basin") * lax.axis_size("chip") + lax.axis_index("chip")
    return (chip * lax.axis_size("core") + lax.axis_index("core")) * SPAN


INNER_ROWS = 40
RIM_ROWS = 20
INNER_STEP = 4
RIM_STEP = 4
RIM = 2 * HALO


def slot_kernel(
    owner_ref,
    label_ref,
    moves_ref,
    device_ref,
    lane_ref,
    home_ref,
    table_ref,
    turned_ref,
    packed_ref,
):
    first_zone = own_first_zone()
    core = lax.axis_index("core").astype(jnp.float32)
    table_ref[...] = jnp.full(table_ref.shape, 256.0 * SPAN, jnp.float32)
    table_ref[0 : owner_ref.shape[0], :] = owner_ref[...].astype(jnp.float32)

    def placed(slots):
        owners = jnp.floor((slots + 0.5) * (1.0 / SPAN))
        lanes = slots - owners * SPAN
        chips = jnp.floor(owners * 0.5)
        swapped = jnp.abs((owners - 2.0 * chips) - core)
        basins, per_basin = lax.axis_size("basin"), lax.axis_size("chip")
        basin = jnp.floor(chips * (1.0 / per_basin))
        place = (chips - per_basin * basin) * basins + basin
        return jnp.where(owners < 256.0, place + 128.0 * swapped, 256.0), lanes

    owners, lanes = placed(jnp.transpose(table_ref[...]))
    turned_ref[:, 0:256] = (owners * LANES).astype(jnp.bfloat16)
    turned_ref[:, 256:512] = lanes.astype(jnp.bfloat16)

    home_row = first_zone // LANES
    shift = first_zone % LANES
    back = jnp.where(shift == 0, 0, LANES - shift)
    pair = table_ref[pl.ds(home_row, 1), :], table_ref[pl.ds(home_row + 1, 1), :]
    pair = [pltpu.roll(jnp.broadcast_to(row, (8, LANES)), back, 1) for row in pair]
    spot = lax.broadcasted_iota(jnp.int32, (8, LANES), 1)
    home = jnp.where(spot + shift < LANES, pair[0], pair[1])
    home_device, home_lane = placed(jnp.where(spot < SPAN, home, 256.0 * SPAN))
    home_ref[0:1, :] = home_device[0:1]
    home_ref[1:2, :] = home_lane[0:1]

    def compact(label):
        count = label.shape[0]
        offset = label - first_zone
        at_home = (offset >= 0) & (offset < SPAN)
        at_home_count = jnp.where(at_home, 1.0, 0.0)
        row_ids = lax.broadcasted_iota(jnp.int32, (count, count), 0)
        column_ids = lax.broadcasted_iota(jnp.int32, (count, count), 1)
        earlier = jnp.where(column_ids < row_ids, 1.0, 0.0).astype(jnp.bfloat16)
        gaps = jnp.dot(
            earlier, at_home_count.astype(jnp.bfloat16), preferred_element_type=jnp.float32
        ).astype(jnp.int32)
        packed = jnp.where(at_home, ABSENT, gaps * (ABSENT + 1) + label)
        moves = jnp.zeros(packed.shape, jnp.int32)
        bit = 0
        while 2**bit < count:
            marker = (ABSENT + 1) * 2**bit
            near = from_below(packed, 2**bit)
            taken = (near & marker) != 0
            left = (packed & marker) != 0
            packed = jnp.where(taken, near, jnp.where(left, ABSENT, packed))
            moves = jnp.where(taken, moves + 2**bit, moves)
            bit += 1
        most = count - jnp.min(jnp.sum(at_home_count, axis=0, keepdims=True)).astype(jnp.int32)
        return packed & ABSENT, moves, most

    inner_label, rim_label = split_rows(label_ref[...])
    inner_count = inner_label.shape[0]
    packed, moves, inner_most = compact(inner_label)
    packed_ref[0:inner_count, :] = packed
    moves_ref[0:inner_count, :] = moves
    packed, moves, rim_most = compact(rim_label)
    packed_ref[inner_count:, :] = packed
    moves_ref[inner_count:, :] = moves
    inner_steps = jnp.maximum((inner_most - INNER_ROWS + INNER_STEP - 1) // INNER_STEP, 0)
    rim_steps = jnp.maximum((rim_most - RIM_ROWS + RIM_STEP - 1) // RIM_STEP, 0)
    home_ref[2:3, :] = jnp.full((1, LANES), inner_steps.astype(jnp.float32))
    home_ref[3:4, :] = jnp.full((1, LANES), rim_steps.astype(jnp.float32))

    def look_up(first, rows):
        for start in range(0, rows, 4):
            places = [pl.ds(first + start + i, 1) for i in range(4)]
            group_label = jnp.concatenate([packed_ref[place, :] for place in places], axis=1)
            width = group_label.shape[1]
            group = one_hot(spread_rows((group_label >> 7).astype(jnp.float32)), 256)
            found = jnp.dot(
                turned_ref[...],
                jnp.concatenate([group, group], axis=0),
                preferred_element_type=jnp.float32,
            )
            hit = (group_label & 127) == lax.broadcasted_iota(jnp.int32, (LANES, width), 0)
            slot = jnp.sum(jnp.where(hit, found, 0.0), axis=0, keepdims=True)
            owner = jnp.floor(slot * (1.0 / LANES))
            lane = slot - owner * LANES
            for i, place in enumerate(places):
                device_ref[place, :] = owner[:, i * LANES : (i + 1) * LANES]
                lane_ref[place, :] = lane[:, i * LANES : (i + 1) * LANES]

    def more_inner(index, carry):
        look_up(INNER_ROWS + index * INNER_STEP, INNER_STEP)
        return carry

    def more_rim(index, carry):
        look_up(inner_count + RIM_ROWS + index * RIM_STEP, RIM_STEP)
        return carry

    look_up(0, INNER_ROWS)
    look_up(inner_count, RIM_ROWS)
    lax.fori_loop(0, inner_steps, more_inner, 0)
    lax.fori_loop(0, rim_steps, more_rim, 0)


def slots_of(owner_slot, label):
    count = label.size // LANES
    stack = jax.ShapeDtypeStruct((count, LANES), jnp.float32)
    return pl.pallas_call(
        slot_kernel,
        out_shape=(
            jax.ShapeDtypeStruct((count, LANES), jnp.int32),
            stack,
            stack,
            jax.ShapeDtypeStruct((8, LANES), jnp.float32),
        ),
        in_specs=[VMEM, VMEM],
        out_specs=(VMEM,) * 4,
        scratch_shapes=[
            pltpu.VMEM((256, LANES), jnp.float32),
            pltpu.VMEM((LANES, 512), jnp.bfloat16),
            pltpu.VMEM((count, LANES), jnp.int32),
        ],
        compiler_params=ROOMY,
        cost_estimate=pl.CostEstimate(
            flops=2 * 256 * 256 * label.size // 4, bytes_accessed=16 * label.size, transcendentals=0
        ),
        name="slot_lookup",
    )(owner_slot, label)


def below(x):
    return pltpu.roll(x, x.shape[0] - 1, 0)


def above(x):
    return pltpu.roll(x, 1, 0)


def rightward(x):
    return pltpu.roll(x, x.shape[1] - 1, 1)


def leftward(x):
    return pltpu.roll(x, 1, 1)


def window(depth, rough, adjoint):
    rows, columns = depth.shape
    conduct = jnp.where(rough > 0, rough_ref / jnp.where(rough > 0, rough, 1.0), 0.0)
    not_last = lax.broadcasted_iota(jnp.int32, (rows, columns), 1) < columns - 1
    under = below(conduct)
    beside = rightward(conduct)
    down_face = (conduct > 0) & (under > 0)
    side_face = (conduct > 0) & (beside > 0) & not_last
    down_weight = jnp.where(down_face, (0.5 * courant) * (conduct + under), 0.0)
    side_weight = jnp.where(side_face, (0.5 * courant) * (conduct + beside), 0.0)

    def steps(field):
        return below(field) - field, rightward(field) - field

    def advanced(field, down_step, side_step):
        down_flux = down_weight * down_step
        side_flux = side_weight * side_step
        return field + ((down_flux - above(down_flux)) + (side_flux - leftward(side_flux)))

    depth_steps = []
    for section in range(STEPS):
        depth_steps.append(steps(depth))
        if section < STEPS - 1:
            depth = advanced(depth, *depth_steps[-1])
    down_total = jnp.zeros((rows, columns), jnp.float32)
    side_total = jnp.zeros((rows, columns), jnp.float32)
    for section in reversed(range(STEPS)):
        down_step, side_step = steps(adjoint)
        down_total = down_total + depth_steps[section][0] * down_step
        side_total = side_total + depth_steps[section][1] * side_step
        adjoint = advanced(adjoint, down_step, side_step)
    down_total = jnp.where(down_face, down_total, 0.0)
    side_total = jnp.where(side_face, side_total, 0.0)
    total = (down_total + above(down_total)) + (side_total + leftward(side_total))
    return (0.5 * courant) * conduct * total, adjoint


def halves(x):
    upper = x.astype(jnp.bfloat16).astype(jnp.float32)
    return upper, x - upper


HOME_ROWS = 16


def zone_sums(rows):
    left = []
    right = []
    for device, lane, *values in rows:
        left.append(one_hot(spread_rows(device), 256))
        weights = [spread_rows(part) for part in values]
        right.append(jnp.concatenate(one_hot(spread_rows(lane), LANES, weights), axis=0))
    both = lax.dot_general(
        jnp.concatenate(left, axis=1),
        jnp.concatenate(right, axis=1),
        (((1,), (1,)), ((), ())),
        preferred_element_type=jnp.float32,
    )
    return jnp.concatenate(
        [
            both[:, 0:LANES] + both[:, LANES : 2 * LANES],
            both[:, 2 * LANES : 3 * LANES] + both[:, 3 * LANES :],
        ],
        axis=1,
    )


def pair_rows(upper, lower):
    width = upper.shape[1]
    pair = [jnp.broadcast_to(part, (8, width)) for part in (upper, lower)]
    return jnp.concatenate(pair, axis=0).astype(jnp.bfloat16)


def set_cells(cell_ref, offset, grad):
    cell_ref[0] = (offset >> 3).astype(jnp.float32)
    cell_ref[1] = (offset & 7).astype(jnp.float32)
    cell_ref[2], cell_ref[3] = halves(grad)
    cell_ref[4], cell_ref[5] = halves(grad * grad)


def home_products(cell_ref, first, count):
    zero = jnp.zeros((), jnp.bfloat16)
    width = cell_ref.shape[2]
    ids = lax.broadcasted_iota(jnp.int32, (16, width), 0)
    group_ids = ids.astype(jnp.float32).astype(jnp.bfloat16)
    within_ids = (ids & 7).astype(jnp.float32).astype(jnp.bfloat16)
    left = []
    right = []
    for step in range(count):
        row = slice(first + step, first + step + 1)
        group_hit = spread_rows(cell_ref[0, row, :]) == group_ids
        within_hit = spread_rows(cell_ref[1, row, :]) == within_ids
        left.append(jnp.where(group_hit, jnp.ones((), jnp.bfloat16), zero))
        weights = [
            pair_rows(cell_ref[2 + part, row, :], cell_ref[3 + part, row, :]) for part in (0, 2)
        ]
        right.append(jnp.concatenate([jnp.where(within_hit, w, zero) for w in weights], axis=0))
    return lax.dot_general(
        jnp.concatenate(left, axis=1),
        jnp.concatenate(right, axis=1),
        (((1,), (1,)), ((), ())),
        preferred_element_type=jnp.float32,
    )


def stray_rows(refs, first, start, count):
    device_ref, lane_ref, stray_ref = refs
    rows = []
    for step in range(count):
        slot = pl.ds(first + start + step, 1)
        value = pl.ds(start + step, 1)
        values = [stray_ref[part, value, :] for part in range(4)]
        rows.append((device_ref[slot, :], lane_ref[slot, :], *values))
    return rows


def inner_kernel(
    depth_ref,
    rough_ref_,
    seed_ref,
    label_ref,
    moves_ref,
    device_ref,
    lane_ref,
    home_ref,
    total_ref,
    adjoint_ref,
    products_ref,
    cell_ref,
    stray_ref,
):
    grad, adjoint = window(depth_ref[...], rough_ref_[...], seed_ref[...])
    adjoint_ref[...] = adjoint
    rows = grad.shape[0]
    inside = slice(RIM, rows - RIM)
    inner_grad, _ = split_rows(grad)
    set_strays(stray_ref, inner_grad, moves_ref[0 : inner_grad.shape[0], :])
    set_cells(cell_ref, (label_ref[...] - own_first_zone())[inside], grad[inside])
    home = home_products(cell_ref, 0, HOME_ROWS)
    for first in range(HOME_ROWS, rows - 2 * RIM, HOME_ROWS):
        home = home + home_products(cell_ref, first, HOME_ROWS)
    products_ref[...] = home
    refs = device_ref, lane_ref, stray_ref
    total_ref[...] = zone_sums(stray_rows(refs, 0, 0, INNER_ROWS))

    def more(index, carry):
        start = INNER_ROWS + index * INNER_STEP
        total_ref[...] += zone_sums(stray_rows(refs, 0, start, INNER_STEP))
        return carry

    lax.fori_loop(0, jnp.max(home_ref[2:3, :]).astype(jnp.int32), more, 0)


def inner_part(depth, rough, seed, label, *slots):
    inner_rows = depth.shape[0] - 2 * RIM
    return pl.pallas_call(
        inner_kernel,
        out_shape=(
            jax.ShapeDtypeStruct((256, 2 * LANES), jnp.float32),
            jax.ShapeDtypeStruct(depth.shape, jnp.float32),
            jax.ShapeDtypeStruct((16, 32), jnp.float32),
        ),
        in_specs=[VMEM] * (4 + len(slots)),
        out_specs=(VMEM,) * 3,
        scratch_shapes=[
            pltpu.VMEM((6, inner_rows, depth.shape[1]), jnp.float32),
            pltpu.VMEM((4, inner_rows * depth.shape[1] // LANES, LANES), jnp.float32),
        ],
        compiler_params=ROOMY,
        cost_estimate=pl.CostEstimate(
            flops=2 * 256 * 128 * depth.size, bytes_accessed=20 * depth.size, transcendentals=0
        ),
        name="inner_rows",
    )(depth, rough, seed, label, *slots)


def zone_kernel(
    depth_ref,
    rough_ref_,
    seed_ref,
    chip_ref,
    away_ref,
    inner_total_ref,
    inner_adjoint_ref,
    inner_home_ref,
    label_ref,
    moves_ref,
    device_ref,
    lane_ref,
    home_ref,
    own_ref,
    other_ref,
    adjoint_ref,
    total_ref,
    stray_ref,
    cell_ref,
):
    first_core = lax.axis_index("core") == 0
    chip_index, chips = lax.axis_index("chip"), lax.axis_size("chip")
    has_low = jnp.where(first_core & (chip_index == 0), 0.0, 1.0)
    has_high = jnp.where(first_core | (chip_index < chips - 1), 1.0, 0.0)
    rows = depth_ref.shape[0]
    near = RIM + HALO

    def rim(part, ref):
        halo = slice(part * HALO, (part + 1) * HALO)
        chip, away = chip_ref[halo, :], away_ref[halo, :]
        low = jnp.where(first_core, away, chip)
        high = jnp.where(first_core, chip, away)
        if part == 1:
            low, high = low * has_low, high * has_high
        return jnp.concatenate([low, ref[0:near, :], ref[rows - near : rows, :], high], axis=0)

    rim_grad, rim_adjoint = window(rim(0, depth_ref), rim(1, rough_ref_), rim(2, seed_ref))
    top = slice(HALO, HALO + RIM)
    bottom = slice(near + 2 * HALO, near + 2 * HALO + RIM)
    inside = slice(RIM, rows - RIM)
    adjoint_ref[...] = jnp.concatenate(
        [rim_adjoint[top], inner_adjoint_ref[inside, :], rim_adjoint[bottom]], axis=0
    )
    offset = label_ref[...] - own_first_zone()
    set_cells(
        cell_ref,
        jnp.concatenate([offset[:RIM], offset[rows - RIM :]], axis=0),
        jnp.concatenate([rim_grad[top], rim_grad[bottom]], axis=0),
    )
    first = moves_ref.shape[0] - stray_ref.shape[1]
    rim_grad = jnp.concatenate([rim_grad[top], rim_grad[bottom]], axis=0)
    set_strays(stray_ref, stacked(rim_grad), moves_ref[first:, :])
    home = inner_home_ref[...] + home_products(cell_ref, 0, 2 * RIM)
    part = lax.broadcasted_iota(jnp.int32, (32, 2 * LANES), 0)
    zone = lax.broadcasted_iota(jnp.int32, (32, 2 * LANES), 1)
    chosen = ((part & 7) == (zone & 7)) & ((part >= 16) == (zone >= LANES))
    home = jnp.dot(
        home,
        jnp.where(chosen, 1.0, 0.0),
        precision=lax.Precision.HIGHEST,
        preferred_element_type=jnp.float32,
    )
    group = lax.broadcasted_iota(jnp.int32, (16, 2 * LANES), 0)
    zone = lax.broadcasted_iota(jnp.int32, (16, 2 * LANES), 1)
    home = jnp.sum(jnp.where(((zone >> 3) & 15) == group, home, 0.0), axis=0, keepdims=True)
    home = halves(home[:, :LANES]) + halves(home[:, LANES:])

    refs = device_ref, lane_ref, stray_ref
    total_ref[...] = inner_total_ref[...] + zone_sums(
        stray_rows(refs, first, 0, RIM_ROWS) + [(home_ref[0:1, :], home_ref[1:2, :], *home)]
    )

    def more(index, carry):
        start = RIM_ROWS + index * RIM_STEP
        total_ref[...] += zone_sums(stray_rows(refs, first, start, RIM_STEP))
        return carry

    lax.fori_loop(0, jnp.max(home_ref[3:4, :]).astype(jnp.int32), more, 0)
    own_ref[...] = total_ref[0:LANES, :]
    other_ref[...] = total_ref[LANES:, :]


def zone_partials(depth, *others):
    half = jax.ShapeDtypeStruct((LANES, 2 * LANES), jnp.float32)
    return pl.pallas_call(
        zone_kernel,
        out_shape=(half, half, jax.ShapeDtypeStruct(depth.shape, jnp.float32)),
        in_specs=[VMEM] * (1 + len(others)),
        out_specs=(VMEM,) * 3,
        scratch_shapes=[
            pltpu.VMEM((256, 2 * LANES), jnp.float32),
            pltpu.VMEM((4, 2 * RIM * depth.shape[1] // LANES, LANES), jnp.float32),
            pltpu.VMEM((6, 2 * RIM, depth.shape[1]), jnp.float32),
        ],
        compiler_params=ROOMY,
        name="zone_partials",
    )(depth, *others)


def parcel_kernel(own_ref, other_ref, edge_ref, out_ref):
    chips = own_ref.shape[0]
    sums = own_ref[...] + other_ref[...]
    out_ref[pl.ds(0, chips, stride=4), :] = sums[:, :LANES]
    out_ref[pl.ds(1, chips, stride=4), :] = sums[:, LANES:]
    for part in range(2):
        edge = jnp.broadcast_to(edge_ref[part : part + 1, :], (chips, LANES))
        out_ref[pl.ds(2 + part, chips, stride=4), :] = edge


def parcels(own, other, edge):
    return pl.pallas_call(
        parcel_kernel,
        out_shape=jax.ShapeDtypeStruct((4 * own.shape[0], LANES), jnp.float32),
        in_specs=[VMEM] * 3,
        out_specs=VMEM,
        compiler_params=ROOMY,
        name="parcels",
    )(own, other, edge)


def result_kernel(arrived_ref, rate_ref, push_ref, grad_ref, curve_ref, reach_ref):
    rows = arrived_ref.shape[0]
    sums = arrived_ref[0:8, :]
    for start in range(8, rows, 8):
        sums = sums + arrived_ref[start : start + 8, :]
    grad_ref[...] = (sums[0:1, :] + sums[4:5, :])[:, :SPAN]
    curve_ref[...] = (sums[1:2, :] + sums[5:6, :])[:, :SPAN]
    basin, chip = lax.axis_index("basin"), lax.axis_index("chip")
    basins = lax.axis_size("basin")
    incoming = jnp.zeros((1, LANES), jnp.float32)
    for hop in reversed(range(1, basins)):
        there = jnp.where(basin + hop < basins, 1.0, 0.0)
        row = 4 * (chip * basins + jnp.minimum(basin + hop, basins - 1))
        rate = arrived_ref[pl.ds(row + 2, 1), :]
        push = arrived_ref[pl.ds(row + 3, 1), :]
        incoming = there * (rate * incoming + push)
    reach_ref[...] = rate_ref[...] * incoming + push_ref[...]


def results(arrived, rate, push):
    zone = jax.ShapeDtypeStruct((1, SPAN), jnp.float32)
    return pl.pallas_call(
        result_kernel,
        out_shape=(zone, zone, jax.ShapeDtypeStruct(rate.shape, jnp.float32)),
        in_specs=[VMEM] * 3,
        out_specs=(VMEM,) * 3,
        compiler_params=ROOMY,
        name="results",
    )(arrived, rate, push)


def reach_kernel(adjoint_ref, cell_ref, keep_ref, forcing_ref, rate_ref, push_ref, edge_ref):
    rows, columns = adjoint_ref.shape
    upper, lower = halves(adjoint_ref[...])
    table = jnp.concatenate([upper, lower], axis=0).astype(jnp.bfloat16)
    reaches = cell_ref.shape[0]
    width = cell_ref.shape[1]
    values = []
    for reach in range(0, reaches, 4):
        cells = jnp.concatenate([cell_ref[reach + i : reach + i + 1, :] for i in range(4)], axis=1)
        column = (cells & (columns - 1)).astype(jnp.float32)
        hot = jnp.concatenate(
            [one_hot(spread_rows(column - part * 256.0), 256) for part in range(columns // 256)],
            axis=0,
        )
        picked = jnp.dot(table, hot, preferred_element_type=jnp.float32)
        picked = picked[:rows] + picked[rows:]
        row_hit = (cells >> 9) == lax.broadcasted_iota(jnp.int32, (rows, 4 * width), 0)
        found = jnp.sum(jnp.where(row_hit, picked, 0.0), axis=0, keepdims=True)
        values += [found[:, i * width : (i + 1) * width] for i in range(4)]
    rate = jnp.ones((1, width), jnp.float32)
    push = jnp.zeros((1, width), jnp.float32)
    for reach in reversed(range(reaches)):
        keep = keep_ref[reach : reach + 1, :]
        push = keep * push + (forcing_ref[reach : reach + 1, :] + levee_gain * values[reach])
        rate = keep * rate
        rate_ref[reach : reach + 1, :] = rate
        push_ref[reach : reach + 1, :] = push
    edge_ref[0:1, :] = rate
    edge_ref[1:2, :] = push


def reach_maps(adjoint, cells, keep, forcing):
    shape = jax.ShapeDtypeStruct(cells.shape, jnp.float32)
    return pl.pallas_call(
        reach_kernel,
        out_shape=(shape, shape, jax.ShapeDtypeStruct((2, cells.shape[1]), jnp.float32)),
        in_specs=[VMEM] * 4,
        out_specs=(VMEM, VMEM, VMEM),
        compiler_params=ROOMY,
        name="reach_maps",
    )(adjoint, cells, keep, forcing)


def swapped(value):
    return lax.ppermute(value, "core", [(0, 1), (1, 0)])


def exchanged_away(value):
    tiles = lax.axis_size("chip") * lax.axis_size("core")
    pairs = [(i, (i + 1 if i % 2 else i - 1) % tiles) for i in range(tiles)]
    return lax.ppermute(value, ("chip", "core"), pairs)


def per_device(
    depth_start, roughness, depth_seed, zone_label, owner_slot, retention, forcing, levee_cell
):
    depth, rough, seed, label, owner_slot, to_chip, to_away = fetched(
        depth_start[0],
        roughness[0],
        depth_seed[0],
        zone_label[0],
        owner_slot.reshape(-1, LANES),
    )
    from_away = exchanged_away(to_away)
    from_chip = swapped(to_chip)
    moves, device, lane, home = slots_of(owner_slot, label)
    inner = inner_part(depth, rough, seed, label, moves, device, lane, home)
    own, other, adjoint = zone_partials(
        depth, rough, seed, from_chip, from_away, *inner, label, moves, device, lane, home
    )
    other = swapped(other)
    rate, push, edge = reach_maps(adjoint, levee_cell, retention, forcing)
    sent = parcels(own, other, edge).reshape(-1, 4, LANES)
    arrived = lax.all_to_all(sent, ("chip", "basin"), 0, 0, tiled=True)
    grad, curve, reach_adjoint = results(arrived.reshape(-1, LANES), rate, push)
    return (grad.reshape(-1), curve.reshape(-1), reach_adjoint)


def solution(mesh):
    basins, tiles = mesh.devices.shape
    fine = jax.sharding.Mesh(
        mesh.devices.reshape(basins, tiles // 2, 2), ("basin", "chip", "core")
    )
    tile = ("chip", "core")
    cells = P("basin", tile, None)
    reaches = P("basin", tile)
    zones = P(("basin", "chip", "core"))
    return jax.shard_map(
        per_device,
        mesh=fine,
        in_specs=(cells, cells, cells, cells, P(), reaches, reaches, reaches),
        out_specs=(zones, zones, reaches),
        check_vma=False,
    )
```

```python
import functools

import jax
import jax.numpy as jnp
from jax import lax
from jax.experimental import pallas as pl
from jax.experimental.pallas import tpu as pltpu
from jax.sharding import PartitionSpec as P

STEPS = 4
HALO = STEPS
SPAN = 127
LANES = 128

courant = 0.24
rough_ref = 0.025
levee_gain = 0.1

VMEM = pl.BlockSpec(memory_space=pltpu.VMEM)
ROOMY = pltpu.CompilerParams(vmem_limit_bytes=48 * 2**20)


def iota_bf16(shape, offset=0):
    ids = lax.broadcasted_iota(jnp.int32, shape, len(shape) - 2)
    if len(shape) == 3:
        ids = ids + shape[1] * lax.broadcasted_iota(jnp.int32, shape, 0)
    return (ids + offset).astype(jnp.float32).astype(jnp.bfloat16)


def spread_rows(row):
    return jnp.broadcast_to(row, (16, row.shape[1])).astype(jnp.bfloat16)


def one_hot(spread, count, weights=None):
    width = spread.shape[1]
    ids = iota_bf16((count // 16, 16, width))
    hit = spread[None] == ids
    zero = jnp.zeros((), jnp.bfloat16)
    if weights is None:
        return jnp.where(hit, jnp.ones((), jnp.bfloat16), zero).reshape(count, width)
    return [jnp.where(hit, w[None], zero).reshape(count, width) for w in weights]


def stacked(x):
    return jnp.concatenate(
        [x[:, start : start + LANES] for start in range(0, x.shape[1], LANES)], axis=0
    )


def from_below(x, distance):
    return pltpu.roll(x, x.shape[0] - distance, 0)


HBM = pl.BlockSpec(memory_space=pltpu.HBM)


FETCH = pltpu.CompilerParams(vmem_limit_bytes=55800000)


def front_kernel(*refs):
    count = (len(refs) - 3) // 2
    sources, kept = refs[:count], refs[count : 2 * count]
    chip_ref, away_ref, arrived = refs[2 * count :]
    copies = [
        pltpu.make_async_copy(source, place, arrived.at[index])
        for index, (source, place) in enumerate(zip(sources, kept))
    ]
    for copy in copies:
        copy.start()
    first_core = lax.axis_index("core") == 0
    for part in range(3):
        copies[part].wait()
        ref = kept[part]
        rows = slice(part * HALO, (part + 1) * HALO)
        top = ref[0:HALO, :]
        bottom = ref[ref.shape[0] - HALO :, :]
        chip_ref[rows, :] = jnp.where(first_core, bottom, top)
        away_ref[rows, :] = jnp.where(first_core, top, bottom)
    for copy in copies[3:]:
        copy.wait()


def fetched(*arrays):
    edge = jax.ShapeDtypeStruct((3 * HALO, arrays[0].shape[1]), jnp.float32)
    kept = tuple(jax.ShapeDtypeStruct(x.shape, x.dtype) for x in arrays)
    return pl.pallas_call(
        front_kernel,
        out_shape=kept + (edge, edge),
        in_specs=[HBM] * len(arrays),
        out_specs=(VMEM,) * (len(arrays) + 2),
        scratch_shapes=[pltpu.SemaphoreType.DMA((len(arrays),))],
        compiler_params=FETCH,
        name="fetch_and_edges",
    )(*arrays)


ABSENT = 2**15 - 1


def split_rows(x):
    rows = x.shape[0]
    inner = stacked(x[RIM : rows - RIM])
    rim = stacked(jnp.concatenate([x[:RIM], x[rows - RIM :]], axis=0))
    return inner, rim


def compacted(x, moves):
    bit = 0
    while 2**bit < x.shape[0]:
        x = jnp.where((moves & 2**bit) != 0, from_below(x, 2**bit), x)
        bit += 1
    return x


def set_strays(stray_ref, grad, moves):
    grad = compacted(grad, moves)
    stray_ref[0], stray_ref[1] = halves(grad)
    stray_ref[2], stray_ref[3] = halves(grad * grad)


def chip_place():
    count = lax.axis_size("y") * lax.axis_size("z")
    return lax.axis_index("y") * lax.axis_size("z") + lax.axis_index("z"), count


def own_first_zone():
    index, count = chip_place()
    chip = lax.axis_index("basin") * count + index
    return (chip * lax.axis_size("core") + lax.axis_index("core")) * SPAN


INNER_ROWS = 40
RIM_ROWS = 20
INNER_STEP = 4
RIM_STEP = 4
RIM = 2 * HALO


def slot_kernel(
    owner_ref,
    label_ref,
    moves_ref,
    device_ref,
    lane_ref,
    home_ref,
    table_ref,
    turned_ref,
    packed_ref,
):
    first_zone = own_first_zone()
    core = lax.axis_index("core").astype(jnp.float32)
    table_ref[...] = jnp.full(table_ref.shape, 256.0 * SPAN, jnp.float32)
    table_ref[0 : owner_ref.shape[0], :] = owner_ref[...].astype(jnp.float32)

    def placed(slots):
        owners = jnp.floor((slots + 0.5) * (1.0 / SPAN))
        lanes = slots - owners * SPAN
        chips = jnp.floor(owners * 0.5)
        swapped = jnp.abs((owners - 2.0 * chips) - core)
        basins, height, depth = (lax.axis_size(axis) for axis in ("basin", "y", "z"))
        line = jnp.floor(chips * (1.0 / depth))
        basin = jnp.floor(chips * (1.0 / (height * depth)))
        place = ((line - height * basin) * basins + basin) * depth + (chips - depth * line)
        return jnp.where(owners < 256.0, place + 128.0 * swapped, 256.0), lanes

    owners, lanes = placed(jnp.transpose(table_ref[...]))
    turned_ref[:, 0:256] = (owners * LANES).astype(jnp.bfloat16)
    turned_ref[:, 256:512] = lanes.astype(jnp.bfloat16)

    home_row = first_zone // LANES
    shift = first_zone % LANES
    back = jnp.where(shift == 0, 0, LANES - shift)
    pair = table_ref[pl.ds(home_row, 1), :], table_ref[pl.ds(home_row + 1, 1), :]
    pair = [pltpu.roll(jnp.broadcast_to(row, (8, LANES)), back, 1) for row in pair]
    spot = lax.broadcasted_iota(jnp.int32, (8, LANES), 1)
    home = jnp.where(spot + shift < LANES, pair[0], pair[1])
    home_device, home_lane = placed(jnp.where(spot < SPAN, home, 256.0 * SPAN))
    home_ref[0:1, :] = home_device[0:1]
    home_ref[1:2, :] = home_lane[0:1]

    def compact(label):
        count = label.shape[0]
        offset = label - first_zone
        at_home = (offset >= 0) & (offset < SPAN)
        at_home_count = jnp.where(at_home, 1.0, 0.0)
        row_ids = lax.broadcasted_iota(jnp.int32, (count, count), 0)
        column_ids = lax.broadcasted_iota(jnp.int32, (count, count), 1)
        earlier = jnp.where(column_ids < row_ids, 1.0, 0.0).astype(jnp.bfloat16)
        gaps = jnp.dot(
            earlier, at_home_count.astype(jnp.bfloat16), preferred_element_type=jnp.float32
        ).astype(jnp.int32)
        packed = jnp.where(at_home, ABSENT, gaps * (ABSENT + 1) + label)
        moves = jnp.zeros(packed.shape, jnp.int32)
        bit = 0
        while 2**bit < count:
            marker = (ABSENT + 1) * 2**bit
            near = from_below(packed, 2**bit)
            taken = (near & marker) != 0
            left = (packed & marker) != 0
            packed = jnp.where(taken, near, jnp.where(left, ABSENT, packed))
            moves = jnp.where(taken, moves + 2**bit, moves)
            bit += 1
        most = count - jnp.min(jnp.sum(at_home_count, axis=0, keepdims=True)).astype(jnp.int32)
        return packed & ABSENT, moves, most

    inner_label, rim_label = split_rows(label_ref[...])
    inner_count = inner_label.shape[0]
    packed, moves, inner_most = compact(inner_label)
    packed_ref[0:inner_count, :] = packed
    moves_ref[0:inner_count, :] = moves
    packed, moves, rim_most = compact(rim_label)
    packed_ref[inner_count:, :] = packed
    moves_ref[inner_count:, :] = moves
    inner_steps = jnp.maximum((inner_most - INNER_ROWS + INNER_STEP - 1) // INNER_STEP, 0)
    rim_steps = jnp.maximum((rim_most - RIM_ROWS + RIM_STEP - 1) // RIM_STEP, 0)
    home_ref[2:3, :] = jnp.full((1, LANES), inner_steps.astype(jnp.float32))
    home_ref[3:4, :] = jnp.full((1, LANES), rim_steps.astype(jnp.float32))

    def look_up(first, rows):
        for start in range(0, rows, 4):
            places = [pl.ds(first + start + i, 1) for i in range(4)]
            group_label = jnp.concatenate([packed_ref[place, :] for place in places], axis=1)
            width = group_label.shape[1]
            group = one_hot(spread_rows((group_label >> 7).astype(jnp.float32)), 256)
            found = jnp.dot(
                turned_ref[...],
                jnp.concatenate([group, group], axis=0),
                preferred_element_type=jnp.float32,
            )
            hit = (group_label & 127) == lax.broadcasted_iota(jnp.int32, (LANES, width), 0)
            slot = jnp.sum(jnp.where(hit, found, 0.0), axis=0, keepdims=True)
            owner = jnp.floor(slot * (1.0 / LANES))
            lane = slot - owner * LANES
            for i, place in enumerate(places):
                device_ref[place, :] = owner[:, i * LANES : (i + 1) * LANES]
                lane_ref[place, :] = lane[:, i * LANES : (i + 1) * LANES]

    def more_inner(index, carry):
        look_up(INNER_ROWS + index * INNER_STEP, INNER_STEP)
        return carry

    def more_rim(index, carry):
        look_up(inner_count + RIM_ROWS + index * RIM_STEP, RIM_STEP)
        return carry

    look_up(0, INNER_ROWS)
    look_up(inner_count, RIM_ROWS)
    lax.fori_loop(0, inner_steps, more_inner, 0)
    lax.fori_loop(0, rim_steps, more_rim, 0)


def slots_of(owner_slot, label):
    count = label.size // LANES
    stack = jax.ShapeDtypeStruct((count, LANES), jnp.float32)
    return pl.pallas_call(
        slot_kernel,
        out_shape=(
            jax.ShapeDtypeStruct((count, LANES), jnp.int32),
            stack,
            stack,
            jax.ShapeDtypeStruct((8, LANES), jnp.float32),
        ),
        in_specs=[VMEM, VMEM],
        out_specs=(VMEM,) * 4,
        scratch_shapes=[
            pltpu.VMEM((256, LANES), jnp.float32),
            pltpu.VMEM((LANES, 512), jnp.bfloat16),
            pltpu.VMEM((count, LANES), jnp.int32),
        ],
        compiler_params=ROOMY,
        cost_estimate=pl.CostEstimate(
            flops=2 * 256 * 256 * label.size // 4, bytes_accessed=16 * label.size, transcendentals=0
        ),
        name="slot_lookup",
    )(owner_slot, label)


def below(x):
    return pltpu.roll(x, x.shape[0] - 1, 0)


def above(x):
    return pltpu.roll(x, 1, 0)


def rightward(x):
    return pltpu.roll(x, x.shape[1] - 1, 1)


def leftward(x):
    return pltpu.roll(x, 1, 1)


def window(depth, rough, adjoint):
    rows, columns = depth.shape
    conduct = jnp.where(rough > 0, rough_ref / jnp.where(rough > 0, rough, 1.0), 0.0)
    not_last = lax.broadcasted_iota(jnp.int32, (rows, columns), 1) < columns - 1
    under = below(conduct)
    beside = rightward(conduct)
    down_face = (conduct > 0) & (under > 0)
    side_face = (conduct > 0) & (beside > 0) & not_last
    down_weight = jnp.where(down_face, (0.5 * courant) * (conduct + under), 0.0)
    side_weight = jnp.where(side_face, (0.5 * courant) * (conduct + beside), 0.0)

    def steps(field):
        return below(field) - field, rightward(field) - field

    def advanced(field, down_step, side_step):
        down_flux = down_weight * down_step
        side_flux = side_weight * side_step
        return field + ((down_flux - above(down_flux)) + (side_flux - leftward(side_flux)))

    depth_steps = []
    for section in range(STEPS):
        depth_steps.append(steps(depth))
        if section < STEPS - 1:
            depth = advanced(depth, *depth_steps[-1])
    down_total = jnp.zeros((rows, columns), jnp.float32)
    side_total = jnp.zeros((rows, columns), jnp.float32)
    for section in reversed(range(STEPS)):
        down_step, side_step = steps(adjoint)
        down_total = down_total + depth_steps[section][0] * down_step
        side_total = side_total + depth_steps[section][1] * side_step
        adjoint = advanced(adjoint, down_step, side_step)
    down_total = jnp.where(down_face, down_total, 0.0)
    side_total = jnp.where(side_face, side_total, 0.0)
    total = (down_total + above(down_total)) + (side_total + leftward(side_total))
    return (0.5 * courant) * conduct * total, adjoint


def halves(x):
    upper = x.astype(jnp.bfloat16).astype(jnp.float32)
    return upper, x - upper


HOME_ROWS = 16


def zone_sums(rows):
    left = []
    right = []
    for device, lane, *values in rows:
        left.append(one_hot(spread_rows(device), 256))
        weights = [spread_rows(part) for part in values]
        right.append(jnp.concatenate(one_hot(spread_rows(lane), LANES, weights), axis=0))
    both = lax.dot_general(
        jnp.concatenate(left, axis=1),
        jnp.concatenate(right, axis=1),
        (((1,), (1,)), ((), ())),
        preferred_element_type=jnp.float32,
    )
    return jnp.concatenate(
        [
            both[:, 0:LANES] + both[:, LANES : 2 * LANES],
            both[:, 2 * LANES : 3 * LANES] + both[:, 3 * LANES :],
        ],
        axis=1,
    )


def pair_rows(upper, lower):
    width = upper.shape[1]
    pair = [jnp.broadcast_to(part, (8, width)) for part in (upper, lower)]
    return jnp.concatenate(pair, axis=0).astype(jnp.bfloat16)


def set_cells(cell_ref, offset, grad):
    cell_ref[0] = (offset >> 3).astype(jnp.float32)
    cell_ref[1] = (offset & 7).astype(jnp.float32)
    cell_ref[2], cell_ref[3] = halves(grad)
    cell_ref[4], cell_ref[5] = halves(grad * grad)


def home_products(cell_ref, first, count):
    zero = jnp.zeros((), jnp.bfloat16)
    width = cell_ref.shape[2]
    ids = lax.broadcasted_iota(jnp.int32, (16, width), 0)
    group_ids = ids.astype(jnp.float32).astype(jnp.bfloat16)
    within_ids = (ids & 7).astype(jnp.float32).astype(jnp.bfloat16)
    left = []
    right = []
    for step in range(count):
        row = slice(first + step, first + step + 1)
        group_hit = spread_rows(cell_ref[0, row, :]) == group_ids
        within_hit = spread_rows(cell_ref[1, row, :]) == within_ids
        left.append(jnp.where(group_hit, jnp.ones((), jnp.bfloat16), zero))
        weights = [
            pair_rows(cell_ref[2 + part, row, :], cell_ref[3 + part, row, :]) for part in (0, 2)
        ]
        right.append(jnp.concatenate([jnp.where(within_hit, w, zero) for w in weights], axis=0))
    return lax.dot_general(
        jnp.concatenate(left, axis=1),
        jnp.concatenate(right, axis=1),
        (((1,), (1,)), ((), ())),
        preferred_element_type=jnp.float32,
    )


def stray_rows(refs, first, start, count):
    device_ref, lane_ref, stray_ref = refs
    rows = []
    for step in range(count):
        slot = pl.ds(first + start + step, 1)
        value = pl.ds(start + step, 1)
        values = [stray_ref[part, value, :] for part in range(4)]
        rows.append((device_ref[slot, :], lane_ref[slot, :], *values))
    return rows


def inner_kernel(
    depth_ref,
    rough_ref_,
    seed_ref,
    label_ref,
    moves_ref,
    device_ref,
    lane_ref,
    home_ref,
    total_ref,
    adjoint_ref,
    products_ref,
    cell_ref,
    stray_ref,
):
    grad, adjoint = window(depth_ref[...], rough_ref_[...], seed_ref[...])
    adjoint_ref[...] = adjoint
    rows = grad.shape[0]
    inside = slice(RIM, rows - RIM)
    inner_grad, _ = split_rows(grad)
    set_strays(stray_ref, inner_grad, moves_ref[0 : inner_grad.shape[0], :])
    set_cells(cell_ref, (label_ref[...] - own_first_zone())[inside], grad[inside])
    home = home_products(cell_ref, 0, HOME_ROWS)
    for first in range(HOME_ROWS, rows - 2 * RIM, HOME_ROWS):
        home = home + home_products(cell_ref, first, HOME_ROWS)
    products_ref[...] = home
    refs = device_ref, lane_ref, stray_ref
    total_ref[...] = zone_sums(stray_rows(refs, 0, 0, INNER_ROWS))

    def more(index, carry):
        start = INNER_ROWS + index * INNER_STEP
        total_ref[...] += zone_sums(stray_rows(refs, 0, start, INNER_STEP))
        return carry

    lax.fori_loop(0, jnp.max(home_ref[2:3, :]).astype(jnp.int32), more, 0)


def inner_part(depth, rough, seed, label, *slots):
    inner_rows = depth.shape[0] - 2 * RIM
    return pl.pallas_call(
        inner_kernel,
        out_shape=(
            jax.ShapeDtypeStruct((256, 2 * LANES), jnp.float32),
            jax.ShapeDtypeStruct(depth.shape, jnp.float32),
            jax.ShapeDtypeStruct((16, 32), jnp.float32),
        ),
        in_specs=[VMEM] * (4 + len(slots)),
        out_specs=(VMEM,) * 3,
        scratch_shapes=[
            pltpu.VMEM((6, inner_rows, depth.shape[1]), jnp.float32),
            pltpu.VMEM((4, inner_rows * depth.shape[1] // LANES, LANES), jnp.float32),
        ],
        compiler_params=ROOMY,
        cost_estimate=pl.CostEstimate(
            flops=2 * 256 * 128 * depth.size, bytes_accessed=20 * depth.size, transcendentals=0
        ),
        name="inner_rows",
    )(depth, rough, seed, label, *slots)


def zone_kernel(
    depth_ref,
    rough_ref_,
    seed_ref,
    chip_ref,
    away_ref,
    inner_total_ref,
    inner_adjoint_ref,
    inner_home_ref,
    label_ref,
    moves_ref,
    device_ref,
    lane_ref,
    home_ref,
    own_ref,
    other_ref,
    adjoint_ref,
    total_ref,
    stray_ref,
    cell_ref,
):
    first_core = lax.axis_index("core") == 0
    chip_index, chips = chip_place()
    has_low = jnp.where(first_core & (chip_index == 0), 0.0, 1.0)
    has_high = jnp.where(first_core | (chip_index < chips - 1), 1.0, 0.0)
    rows = depth_ref.shape[0]
    near = RIM + HALO

    def rim(part, ref):
        halo = slice(part * HALO, (part + 1) * HALO)
        chip, away = chip_ref[halo, :], away_ref[halo, :]
        low = jnp.where(first_core, away, chip)
        high = jnp.where(first_core, chip, away)
        if part == 1:
            low, high = low * has_low, high * has_high
        return jnp.concatenate([low, ref[0:near, :], ref[rows - near : rows, :], high], axis=0)

    rim_grad, rim_adjoint = window(rim(0, depth_ref), rim(1, rough_ref_), rim(2, seed_ref))
    top = slice(HALO, HALO + RIM)
    bottom = slice(near + 2 * HALO, near + 2 * HALO + RIM)
    inside = slice(RIM, rows - RIM)
    adjoint_ref[...] = jnp.concatenate(
        [rim_adjoint[top], inner_adjoint_ref[inside, :], rim_adjoint[bottom]], axis=0
    )
    offset = label_ref[...] - own_first_zone()
    set_cells(
        cell_ref,
        jnp.concatenate([offset[:RIM], offset[rows - RIM :]], axis=0),
        jnp.concatenate([rim_grad[top], rim_grad[bottom]], axis=0),
    )
    first = moves_ref.shape[0] - stray_ref.shape[1]
    rim_grad = jnp.concatenate([rim_grad[top], rim_grad[bottom]], axis=0)
    set_strays(stray_ref, stacked(rim_grad), moves_ref[first:, :])
    home = inner_home_ref[...] + home_products(cell_ref, 0, 2 * RIM)
    part = lax.broadcasted_iota(jnp.int32, (32, 2 * LANES), 0)
    zone = lax.broadcasted_iota(jnp.int32, (32, 2 * LANES), 1)
    chosen = ((part & 7) == (zone & 7)) & ((part >= 16) == (zone >= LANES))
    home = jnp.dot(
        home,
        jnp.where(chosen, 1.0, 0.0),
        precision=lax.Precision.HIGHEST,
        preferred_element_type=jnp.float32,
    )
    group = lax.broadcasted_iota(jnp.int32, (16, 2 * LANES), 0)
    zone = lax.broadcasted_iota(jnp.int32, (16, 2 * LANES), 1)
    home = jnp.sum(jnp.where(((zone >> 3) & 15) == group, home, 0.0), axis=0, keepdims=True)
    home = halves(home[:, :LANES]) + halves(home[:, LANES:])

    refs = device_ref, lane_ref, stray_ref
    total_ref[...] = inner_total_ref[...] + zone_sums(
        stray_rows(refs, first, 0, RIM_ROWS) + [(home_ref[0:1, :], home_ref[1:2, :], *home)]
    )

    def more(index, carry):
        start = RIM_ROWS + index * RIM_STEP
        total_ref[...] += zone_sums(stray_rows(refs, first, start, RIM_STEP))
        return carry

    lax.fori_loop(0, jnp.max(home_ref[3:4, :]).astype(jnp.int32), more, 0)
    own_ref[...] = total_ref[0:LANES, :]
    other_ref[...] = total_ref[LANES:, :]


def zone_partials(depth, *others):
    half = jax.ShapeDtypeStruct((LANES, 2 * LANES), jnp.float32)
    return pl.pallas_call(
        zone_kernel,
        out_shape=(half, half, jax.ShapeDtypeStruct(depth.shape, jnp.float32)),
        in_specs=[VMEM] * (1 + len(others)),
        out_specs=(VMEM,) * 3,
        scratch_shapes=[
            pltpu.VMEM((256, 2 * LANES), jnp.float32),
            pltpu.VMEM((4, 2 * RIM * depth.shape[1] // LANES, LANES), jnp.float32),
            pltpu.VMEM((6, 2 * RIM, depth.shape[1]), jnp.float32),
        ],
        compiler_params=ROOMY,
        name="zone_partials",
    )(depth, *others)


def parcel_kernel(own_ref, other_ref, edge_ref, out_ref):
    chips = own_ref.shape[0]
    sums = own_ref[...] + other_ref[...]
    out_ref[pl.ds(0, chips, stride=4), :] = sums[:, :LANES]
    out_ref[pl.ds(1, chips, stride=4), :] = sums[:, LANES:]
    for part in range(2):
        edge = jnp.broadcast_to(edge_ref[part : part + 1, :], (chips, LANES))
        out_ref[pl.ds(2 + part, chips, stride=4), :] = edge


def parcels(own, other, edge):
    return pl.pallas_call(
        parcel_kernel,
        out_shape=jax.ShapeDtypeStruct((4 * own.shape[0], LANES), jnp.float32),
        in_specs=[VMEM] * 3,
        out_specs=VMEM,
        compiler_params=ROOMY,
        name="parcels",
    )(own, other, edge)


def result_kernel(arrived_ref, rate_ref, push_ref, grad_ref, curve_ref, reach_ref):
    rows = arrived_ref.shape[0]
    sums = arrived_ref[0:8, :]
    for start in range(8, rows, 8):
        sums = sums + arrived_ref[start : start + 8, :]
    grad_ref[...] = (sums[0:1, :] + sums[4:5, :])[:, :SPAN]
    curve_ref[...] = (sums[1:2, :] + sums[5:6, :])[:, :SPAN]
    basin = lax.axis_index("basin")
    height, level, depth = lax.axis_index("y"), lax.axis_index("z"), lax.axis_size("z")
    basins = lax.axis_size("basin")
    incoming = jnp.zeros((1, LANES), jnp.float32)
    for hop in reversed(range(1, basins)):
        there = jnp.where(basin + hop < basins, 1.0, 0.0)
        below_here = height * basins + jnp.minimum(basin + hop, basins - 1)
        row = 4 * (below_here * depth + level)
        rate = arrived_ref[pl.ds(row + 2, 1), :]
        push = arrived_ref[pl.ds(row + 3, 1), :]
        incoming = there * (rate * incoming + push)
    reach_ref[...] = rate_ref[...] * incoming + push_ref[...]


def results(arrived, rate, push):
    zone = jax.ShapeDtypeStruct((1, SPAN), jnp.float32)
    return pl.pallas_call(
        result_kernel,
        out_shape=(zone, zone, jax.ShapeDtypeStruct(rate.shape, jnp.float32)),
        in_specs=[VMEM] * 3,
        out_specs=(VMEM,) * 3,
        compiler_params=ROOMY,
        name="results",
    )(arrived, rate, push)


def reach_kernel(adjoint_ref, cell_ref, keep_ref, forcing_ref, rate_ref, push_ref, edge_ref):
    rows, columns = adjoint_ref.shape
    upper, lower = halves(adjoint_ref[...])
    table = jnp.concatenate([upper, lower], axis=0).astype(jnp.bfloat16)
    reaches = cell_ref.shape[0]
    width = cell_ref.shape[1]
    values = []
    for reach in range(0, reaches, 4):
        cells = jnp.concatenate([cell_ref[reach + i : reach + i + 1, :] for i in range(4)], axis=1)
        column = (cells & (columns - 1)).astype(jnp.float32)
        hot = jnp.concatenate(
            [one_hot(spread_rows(column - part * 256.0), 256) for part in range(columns // 256)],
            axis=0,
        )
        picked = jnp.dot(table, hot, preferred_element_type=jnp.float32)
        picked = picked[:rows] + picked[rows:]
        row_hit = (cells >> 9) == lax.broadcasted_iota(jnp.int32, (rows, 4 * width), 0)
        found = jnp.sum(jnp.where(row_hit, picked, 0.0), axis=0, keepdims=True)
        values += [found[:, i * width : (i + 1) * width] for i in range(4)]
    rate = jnp.ones((1, width), jnp.float32)
    push = jnp.zeros((1, width), jnp.float32)
    for reach in reversed(range(reaches)):
        keep = keep_ref[reach : reach + 1, :]
        push = keep * push + (forcing_ref[reach : reach + 1, :] + levee_gain * values[reach])
        rate = keep * rate
        rate_ref[reach : reach + 1, :] = rate
        push_ref[reach : reach + 1, :] = push
    edge_ref[0:1, :] = rate
    edge_ref[1:2, :] = push


def reach_maps(adjoint, cells, keep, forcing):
    shape = jax.ShapeDtypeStruct(cells.shape, jnp.float32)
    return pl.pallas_call(
        reach_kernel,
        out_shape=(shape, shape, jax.ShapeDtypeStruct((2, cells.shape[1]), jnp.float32)),
        in_specs=[VMEM] * 4,
        out_specs=(VMEM, VMEM, VMEM),
        compiler_params=ROOMY,
        name="reach_maps",
    )(adjoint, cells, keep, forcing)


def swapped(value):
    return lax.ppermute(value, "core", [(0, 1), (1, 0)])


def exchanged_away(value):
    tiles = chip_place()[1] * lax.axis_size("core")
    pairs = [(i, (i + 1 if i % 2 else i - 1) % tiles) for i in range(tiles)]
    return lax.ppermute(value, ("y", "z", "core"), pairs)


def per_device(
    depth_start, roughness, depth_seed, zone_label, owner_slot, retention, forcing, levee_cell
):
    depth, rough, seed, label, owner_slot, to_chip, to_away = fetched(
        depth_start[0],
        roughness[0],
        depth_seed[0],
        zone_label[0],
        owner_slot.reshape(-1, LANES),
    )
    from_away = exchanged_away(to_away)
    moves, device, lane, home = slots_of(owner_slot, label)
    to_chip, home = lax.optimization_barrier((to_chip, home))
    from_chip = swapped(to_chip)
    inner = inner_part(depth, rough, seed, label, moves, device, lane, home)
    own, other, adjoint = zone_partials(
        depth, rough, seed, from_chip, from_away, *inner, label, moves, device, lane, home
    )
    other = swapped(other)
    rate, push, edge = reach_maps(adjoint, levee_cell, retention, forcing)
    sent = parcels(own, other, edge).reshape(-1, 4, LANES)
    arrived = lax.all_to_all(sent, ("y", "basin", "z"), 0, 0, tiled=True)
    grad, curve, reach_adjoint = results(arrived.reshape(-1, LANES), rate, push)
    return (grad.reshape(-1), curve.reshape(-1), reach_adjoint)


def solution(mesh):
    basins, tiles = mesh.devices.shape
    fine = jax.sharding.Mesh(
        mesh.devices.reshape(basins, tiles // 16, 8, 2), ("basin", "y", "z", "core")
    )
    tile = ("y", "z", "core")
    cells = P("basin", tile, None)
    reaches = P("basin", tile)
    zones = P(("basin", "y", "z", "core"))
    return jax.shard_map(
        per_device,
        mesh=fine,
        in_specs=(cells, cells, cells, cells, P(), reaches, reaches, reaches),
        out_specs=(zones, zones, reaches),
        check_vma=False,
    )
```
